32 devices in a mesh: rows: 8 (over z, y), cols: 4 (over x, core).
Axes of the slice: x: 2, y: 2, z: 4, core: 2. Of those that a mesh axis runs over, the one named last changes fastest.
Arguments:
- features: bfloat16 [2, 8, 128, 512], P(None, 'rows', 'cols'), may hold values from -6 to 6
- skip_feat: bfloat16 [2, 16, 256, 512], P(None, 'rows', 'cols'), may hold values from -6 to 6
- labels: int32 [2, 16, 256], P(None, 'rows', 'cols'), may hold values from 0 to 1
- pixel_weight: int32 [2, 16, 256], P(None, 'rows', 'cols'), may hold values from 1 to 10
- valid_mask: int32 [2, 16, 256], P(None, 'rows', 'cols'), may hold values from 0 to 1, as said below
- conv_first: float32 [4718592], P(('rows', 'cols')), may hold values from -0.09375 to 0.09375
- conv_first_mom: float32 [4718592], P(('rows', 'cols')), may hold values from -3.8146973e-06 to 3.8146973e-06
- conv_first_sec: float32 [4718592], P(('rows', 'cols')), may hold values from 5.2981907e-15 to 2.1192763e-14
- conv_second: float32 [9437184], P(('rows', 'cols')), may hold values from -0.0625 to 0.0625
- conv_second_mom: float32 [9437184], P(('rows', 'cols')), may hold values from -3.8146973e-06 to 3.8146973e-06
- conv_second_sec: float32 [9437184], P(('rows', 'cols')), may hold values from 5.9339736e-15 to 2.3841858e-14
- up_conv: float32 [2097152], P(('rows', 'cols')), may hold values from -0.1875 to 0.1875
- up_conv_mom: float32 [2097152], P(('rows', 'cols')), may hold values from -1.1444092e-05 to 1.1444092e-05
- up_conv_sec: float32 [2097152], P(('rows', 'cols')), may hold values from 4.7683716e-14 to 1.9073487e-13
- conv_merge: float32 [4718592], P(('rows', 'cols')), may hold values from -0.0625 to 0.0625
- conv_merge_mom: float32 [4718592], P(('rows', 'cols')), may hold values from -2.670288e-05 to 2.670288e-05
- conv_merge_sec: float32 [4718592], P(('rows', 'cols')), may hold values from 2.5431314e-13 to 1.0384454e-12
- head_weight: float32 [512, 2], replicated, may hold values from -0.25 to 0.25
- head_mom: float32 [512, 2], replicated, may hold values from -0.0007324219 to 0.0007324219
- head_sec: float32 [512, 2], replicated, may hold values from 2.1972656e-10 to 8.789062e-10
- biases: float32 [3074], replicated, may hold values from -0.75 to 0.75
- biases_mom: float32 [3074], replicated, may hold values from -0.00015258789 to 0.00015258789
- biases_sec: float32 [3074], replicated, may hold values from 8.132726e-12 to 3.2530905e-11
Outputs:
- first_mom_out: float32 [4718592], P(('rows', 'cols'))
- first_sec_out: float32 [4718592], P(('rows', 'cols'))
- first_new: float32 [4718592], P(('rows', 'cols'))
- second_mom_out: float32 [9437184], P(('rows', 'cols'))
- second_sec_out: float32 [9437184], P(('rows', 'cols'))
- second_new: float32 [9437184], P(('rows', 'cols'))
- up_mom_out: float32 [2097152], P(('rows', 'cols'))
- up_sec_out: float32 [2097152], P(('rows', 'cols'))
- up_new: float32 [2097152], P(('rows', 'cols'))
- merge_mom_out: float32 [4718592], P(('rows', 'cols'))
- merge_sec_out: float32 [4718592], P(('rows', 'cols'))
- merge_new: float32 [4718592], P(('rows', 'cols'))
- head_mom_out: float32 [512, 2], replicated
- head_sec_out: float32 [512, 2], replicated
- head_new: float32 [512, 2], replicated
- biases_mom_out: float32 [3074], replicated
- biases_sec_out: float32 [3074], replicated
- biases_new: float32 [3074], replicated
- loss_sum: float32 [], replicated
- valid_count: float32 [], replicated
- grad_norm: float32 [], replicated
The draws below stay inside these ranges and needn't reach their ends.
Inputs may be any that keep to these rules, and one draw needn't show every extreme that they name: `valid_mask`: 1 at the last pixel of every image.
All inputs are finite; a program needn't handle non-finite values.
Results may differ from the reference program's by a relative error of at most 0.011.
Values may be sent and summed in bfloat16 or wider, within the bound.
No kernel may reach another device: no remote copies, remote signals or barrier semaphores. Data moves between devices by JAX's collectives and lax.ppermute only.
A program may use at most 384 MiB of HBM per device.

```python
import math
import jax
import jax.numpy as jnp
from jax import lax

C0 = 512
C1 = 1024
CLASSES = 2
IMAGES = 2
STEP = 10
H = 8
W = 128
K_FIRST = 4718592
K_SECOND = 9437184
K_UP = 2097152
K_MERGE = 4718592
BIAS_ALL = 3074


def draw_valid_mask(key, part):
    key = jax.random.fold_in(key, 7)
    row_pos = jnp.arange(2 * H, dtype=jnp.int32)[:, None]
    col_pos = jnp.arange(2 * W, dtype=jnp.int32)[None, :]
    limit = 2 + 48 * row_pos // (2 * H) + 48 * col_pos // (2 * W)
    picks = jax.random.randint(key, (IMAGES, 2 * H, 2 * W), 0, 100)
    marked = (picks < limit[None]).astype(jnp.int32)
    return marked.at[:, 2 * H - 1, 2 * W - 1].set(1)


def with_ends(values, own_key, smallest, largest):
    extent = values.shape
    index_at = [jax.random.randint(jax.random.fold_in(own_key, axis), (), 0, extent[axis]) for axis in range(len(extent))]
    values = values.at[tuple(index_at)].set(smallest)
    longest = extent.index(max(extent))
    index_at[longest] = (index_at[longest] + 1) % extent[longest]
    return values.at[tuple(index_at)].set(largest)


def steps_of(stream_key, shape, split, least, largest):
    def one(position, blocks):
        draws = jax.random.uniform(jax.random.fold_in(jax.random.fold_in(stream_key, 6), position), (blocks,), jnp.float32, least / len(split), largest / len(split))
        return jnp.repeat(jnp.exp(draws), shape[position] // blocks).reshape((-1,) + (1,) * (len(shape) - position - 1))

    gain = one(*split[0])
    for cut in split[1:]:
        gain = gain * one(*cut)
    return gain


def scatter_about(own_key, shape, width, most, shards=(), kind=jnp.bfloat16):
    entries = width * jax.random.normal(own_key, shape, jnp.float32)
    if shards:
        entries = entries * steps_of(own_key, shape, shards, -0.22, 0.18)
    return jnp.clip(entries, -most, most).astype(kind)


def setup_inputs(seed: int = 0) -> dict:
    arg_keys = jax.random.split(jax.random.key(seed), 24)
    features = scatter_about(arg_keys[0], (IMAGES, H, W, C0), 1.0, 6.0, ((1, 8), (2, 4)))
    skip_feat = scatter_about(arg_keys[1], (IMAGES, 2 * H, 2 * W, C0), 1.0, 6.0, ((1, 8), (2, 4)))
    labels = with_ends(jax.random.randint(arg_keys[2], (IMAGES, 2 * H, 2 * W), 0, CLASSES), jax.random.fold_in(arg_keys[2], 1), 0, CLASSES - 1).astype(jnp.int32)
    pixel_weight = with_ends(jax.random.randint(arg_keys[3], (IMAGES, 2 * H, 2 * W), 1, 11), jax.random.fold_in(arg_keys[3], 1), 1, 10).astype(jnp.int32)
    valid_mask = draw_valid_mask(jax.random.fold_in(arg_keys[23], 71), 0)
    conv_first = scatter_about(arg_keys[5], (K_FIRST,), (9 * C0) ** -0.5, 0.09375, ((0, 32),), jnp.float32)
    conv_first_mom = scatter_about(arg_keys[6], (K_FIRST,), (0.00055 / K_FIRST ** 0.5), 3.814697265625e-06, ((0, 32),), jnp.float32)
    conv_first_sec = jnp.clip(jnp.exp(math.log(2.11927626462367e-14) - 1.3862944 * jax.random.uniform(arg_keys[7], (K_FIRST,), jnp.float32) ** steps_of(arg_keys[7], (K_FIRST,), ((0, 32),), -0.2, 0.2)), 5.298190661559175e-15, 2.11927626462367e-14)
    conv_second = scatter_about(arg_keys[8], (K_SECOND,), (9 * C1) ** -0.5, 0.0625, ((0, 32),), jnp.float32)
    conv_second_mom = scatter_about(arg_keys[9], (K_SECOND,), (0.000825 / K_SECOND ** 0.5), 3.814697265625e-06, ((0, 32),), jnp.float32)
    conv_second_sec = jnp.clip(jnp.exp(math.log(2.3841858188774524e-14) - 1.3907487 * jax.random.uniform(arg_keys[10], (K_SECOND,), jnp.float32) ** steps_of(arg_keys[10], (K_SECOND,), ((0, 32),), -0.2, 0.2)), 5.933973591768253e-15, 2.3841858188774524e-14)
    up_conv = scatter_about(arg_keys[11], (K_UP,), C1 ** -0.5, 0.1875, ((0, 32),), jnp.float32)
    up_conv_mom = scatter_about(arg_keys[12], (K_UP,), (0.0011 / K_UP ** 0.5), 1.1444091796875e-05, ((0, 32),), jnp.float32)
    up_conv_sec = jnp.clip(jnp.exp(math.log(1.907348655101962e-13) - 1.3862944 * jax.random.uniform(arg_keys[13], (K_UP,), jnp.float32) ** steps_of(arg_keys[13], (K_UP,), ((0, 32),), -0.2, 0.2)), 4.768371637754905e-14, 1.907348655101962e-13)
    conv_merge = scatter_about(arg_keys[14], (K_MERGE,), (18 * C0) ** -0.5, 0.0625, ((0, 32),), jnp.float32)
    conv_merge_mom = scatter_about(arg_keys[15], (K_MERGE,), (0.00385 / K_MERGE ** 0.5), 2.6702880859375e-05, ((0, 32),), jnp.float32)
    conv_merge_sec = jnp.clip(jnp.exp(math.log(1.0384453713596642e-12) - 1.40691368 * jax.random.uniform(arg_keys[16], (K_MERGE,), jnp.float32) ** steps_of(arg_keys[16], (K_MERGE,), ((0, 32),), -0.2, 0.2)), 2.543131449785768e-13, 1.0384453713596642e-12)
    head_weight = scatter_about(arg_keys[17], (C0, CLASSES), C0 ** -0.5, 0.25, (), jnp.float32)
    head_mom = scatter_about(arg_keys[18], (C0, CLASSES), (0.00165 / (C0 * CLASSES) ** 0.5), 0.0007324219, (), jnp.float32)
    head_sec = jnp.clip(jnp.exp(jax.random.uniform(arg_keys[19], (C0, CLASSES), jnp.float32, math.log(2.1972655639412864e-10), math.log(8.789062255765145e-10))), 2.1972655639412864e-10, 8.789062255765145e-10)
    biases = scatter_about(arg_keys[20], (BIAS_ALL,), 0.05, 0.75, (), jnp.float32)
    biases_mom = scatter_about(arg_keys[21], (BIAS_ALL,), (0.00055 / BIAS_ALL ** 0.5), 0.00015258789, (), jnp.float32)
    biases_sec = jnp.clip(jnp.exp(jax.random.uniform(arg_keys[22], (BIAS_ALL,), jnp.float32, math.log(8.132726263265777e-12), math.log(3.253090505306311e-11))), 8.132726263265777e-12, 3.253090505306311e-11)
    return {"features": features, "skip_feat": skip_feat, "labels": labels, "pixel_weight": pixel_weight, "valid_mask": valid_mask, "conv_first": conv_first, "conv_first_mom": conv_first_mom, "conv_first_sec": conv_first_sec, "conv_second": conv_second, "conv_second_mom": conv_second_mom, "conv_second_sec": conv_second_sec, "up_conv": up_conv, "up_conv_mom": up_conv_mom, "up_conv_sec": up_conv_sec, "conv_merge": conv_merge, "conv_merge_mom": conv_merge_mom, "conv_merge_sec": conv_merge_sec, "head_weight": head_weight, "head_mom": head_mom, "head_sec": head_sec, "biases": biases, "biases_mom": biases_mom, "biases_sec": biases_sec}


@jax.custom_vjp
def low(v):
    return lax.optimization_barrier(v.astype(jnp.bfloat16)).astype(jnp.float32)

@jax.custom_vjp
def low_back(v):
    return v

def low_keep(v):
    return (low(v), None)

def low_pass(kept, grad):
    return (grad,)

def back_keep(v):
    return (v, None)

def back_low(kept, grad):
    return (low(grad),)
low.defvjp(low_keep, low_pass)
low_back.defvjp(back_keep, back_low)
clip_norm = 0.05
learn_rate = 0.02
beta_first = 0.9
beta_second = 0.999
epsilon = 1e-08
weight_decay = 0.1

def convolve(values, kernel):
    return lax.conv_general_dilated(values, kernel, (1, 1), ((1, 1), (1, 1)), dimension_numbers=('NHWC', 'HWIO', 'NHWC'), precision=lax.Precision.HIGHEST)

def upsample(values, kernel):
    images, rows_in, cols_in = (values.shape[0], values.shape[1], values.shape[2])
    expanded = jnp.einsum('nhwc,abco->nhawbo', values, kernel, precision=lax.Precision.HIGHEST)
    return expanded.reshape(images, 2 * rows_in, 2 * cols_in, kernel.shape[3])

def network(first, second, upward, merge, head, biases, features, skip_feat, onehot, scaled, count_all):
    kernel_one = low(first).reshape(3, 3, C0, C1)
    kernel_two = low(second).reshape(3, 3, C1, C1)
    kernel_up = low(upward).reshape(2, 2, C1, C0)
    kernel_merge = low(merge).reshape(3, 3, 2 * C0, C0)
    head_low = low(head)
    pre_one = low_back(convolve(features, kernel_one) + biases[:C1])
    act_one = low(jax.nn.gelu(pre_one))
    pre_two = low_back(convolve(act_one, kernel_two) + biases[C1:2 * C1])
    act_two = low(jax.nn.gelu(pre_two))
    upsampled = low(low_back(upsample(act_two, kernel_up) + biases[2 * C1:2 * C1 + C0]))
    joined = jnp.concatenate([upsampled, skip_feat], axis=3)
    pre_three = low_back(convolve(joined, kernel_merge) + biases[2 * C1 + C0:2 * C1 + 2 * C0])
    act_three = low(jax.nn.gelu(pre_three))
    logits = low_back(jnp.einsum('nhwc,ck->nhwk', act_three, head_low, precision=lax.Precision.HIGHEST) + biases[2 * C1 + 2 * C0:])
    log_probs = jax.nn.log_softmax(logits, axis=-1)
    loss_total = -jnp.sum(scaled * lax.optimization_barrier(jnp.sum(onehot * log_probs, axis=-1)))
    return (loss_total / count_all, loss_total)

def adamw(weight, moment, second, grad, decay):
    new_mom = beta_first * moment + (1.0 - beta_first) * grad
    new_sec = beta_second * second + (1.0 - beta_second) * grad * grad
    corrected = new_mom / (1.0 - beta_first ** STEP)
    spread = jnp.sqrt(new_sec / (1.0 - beta_second ** STEP))
    return (new_mom, new_sec, weight - learn_rate * (corrected / (spread + epsilon) + decay * weight))

def reference(features, skip_feat, labels, pixel_weight, valid_mask, conv_first, conv_first_mom, conv_first_sec, conv_second, conv_second_mom, conv_second_sec, up_conv, up_conv_mom, up_conv_sec, conv_merge, conv_merge_mom, conv_merge_sec, head_weight, head_mom, head_sec, biases, biases_mom, biases_sec):
    count_all = jnp.sum(valid_mask.astype(jnp.float32))
    scaled = (valid_mask * pixel_weight).astype(jnp.float32)
    onehot = (labels[..., None] == jnp.arange(CLASSES, dtype=jnp.int32)).astype(jnp.float32)
    feat_wide = features.astype(jnp.float32)
    skip_wide = skip_feat.astype(jnp.float32)

    def loss_of(first, second, upward, merge, head, bias_all):
        return network(first, second, upward, merge, head, bias_all, feat_wide, skip_wide, onehot, scaled, count_all)
    loss_value, pullback, loss_total = jax.vjp(loss_of, conv_first, conv_second, up_conv, conv_merge, head_weight, biases, has_aux=True)
    grad_one, grad_two, grad_up, grad_merge, grad_head, grad_bias = pullback(jnp.ones((), jnp.float32))
    squares = jnp.sum(grad_one * grad_one) + jnp.sum(grad_two * grad_two) + jnp.sum(grad_up * grad_up) + jnp.sum(grad_merge * grad_merge) + jnp.sum(grad_head * grad_head) + jnp.sum(grad_bias * grad_bias)
    grad_norm = jnp.sqrt(squares)
    factor = clip_norm / jnp.maximum(grad_norm, clip_norm)
    one_m, one_v, one_w = adamw(conv_first, conv_first_mom, conv_first_sec, grad_one * factor, weight_decay)
    two_m, two_v, two_w = adamw(conv_second, conv_second_mom, conv_second_sec, grad_two * factor, weight_decay)
    up_m, up_v, up_w = adamw(up_conv, up_conv_mom, up_conv_sec, grad_up * factor, weight_decay)
    mer_m, mer_v, mer_w = adamw(conv_merge, conv_merge_mom, conv_merge_sec, grad_merge * factor, weight_decay)
    head_m, head_v, head_w = adamw(head_weight, head_mom, head_sec, grad_head * factor, weight_decay)
    bias_m, bias_v, bias_w = adamw(biases, biases_mom, biases_sec, grad_bias * factor, 0.0)
    return (one_m, one_v, one_w, two_m, two_v, two_w, up_m, up_v, up_w, mer_m, mer_v, mer_w, head_m, head_v, head_w, bias_m, bias_v, bias_w, loss_total, count_all, grad_norm)
```

```python
import jax
import jax.numpy as jnp
from jax import lax
from jax.sharding import Mesh
from jax.sharding import PartitionSpec as P

C0 = 512
C1 = 1024
CLASSES = 2
STEP = 10

clip_norm = 0.05
learn_rate = 0.02
beta_first = 0.9
beta_second = 0.999
epsilon = 1e-08
weight_decay = 0.1

AXES = ("zh", "zl", "y", "x", "core")
MEMBERS = ("zl", "y", "core")
CHIPS = ("zh", "zl", "y", "x")
ROWS = ("zh", "zl", "y")
bf16 = jnp.bfloat16
f32 = jnp.float32


def size_of(axis):
    return lax.axis_size(axis)


def shifted(values, axis, step):
    count = size_of(axis)
    return lax.ppermute(
        values, axis, [(i, i + step) for i in range(count) if 0 <= i + step < count]
    )


def swapped(values, axis):
    return lax.ppermute(values, axis, [(0, 1), (1, 0)])


def padded(cells, axis, dim, width):
    head = lax.slice_in_dim(cells, 0, width, axis=dim)
    tail = lax.slice_in_dim(cells, cells.shape[dim] - width, cells.shape[dim], axis=dim)
    return jnp.concatenate(
        [shifted(tail, axis, 1), cells, shifted(head, axis, -1)], axis=dim
    )


def in_order(own, other, axis, dim):
    first = lax.axis_index(axis) == 0
    return jnp.concatenate(
        [jnp.where(first, own, other), jnp.where(first, other, own)], axis=dim
    )


def pair_gather(own, axis, dim):
    return in_order(own, swapped(own, axis), axis, dim)


def pair_half(values, axis, dim, index):
    width = values.shape[dim] // 2
    return lax.dynamic_slice_in_dim(values, index * width, width, axis=dim)


def pair_scatter(values, axis, dim, kind):
    me = lax.axis_index(axis)
    away = pair_half(values, axis, dim, 1 - me).astype(kind)
    return pair_half(values, axis, dim, me).astype(f32) + swapped(away, axis).astype(f32)


def total(values):
    for axis in ("core", "x", "y", "zl"):
        values = values + swapped(values, axis)
    if size_of("zh") == 2:
        return values + swapped(values, "zh")
    return lax.psum(values, "zh")


def convolve(values, kernel, pad=0):
    return lax.conv_general_dilated(
        values,
        kernel,
        (1, 1),
        ((pad, pad), (pad, pad)),
        dimension_numbers=("NHWC", "HWIO", "NHWC"),
        preferred_element_type=f32,
    )


def kernel_grad(cells, grad):
    rows_in, cols_in = (grad.shape[1], grad.shape[2])
    terms = [
        jnp.einsum(
            "nhwc,nhwo->co",
            cells[:, shift_h : shift_h + rows_in, shift_w : shift_w + cols_in],
            grad,
            preferred_element_type=f32,
        )
        for shift_h in range(3)
        for shift_w in range(3)
    ]
    return jnp.concatenate(terms, axis=0)


def turned(kernel):
    return jnp.swapaxes(kernel[::-1, ::-1], 2, 3)


def gelu_back(pre_act, upstream):
    return jax.vjp(jax.nn.gelu, pre_act)[1](upstream)[0]


def column_sum(values):
    return jnp.sum(values, axis=(0, 1, 2), dtype=f32)


def group_gather(block):
    n, _, w, c = block.shape
    sent = jnp.broadcast_to(block[None], (8,) + block.shape)
    got = lax.all_to_all(sent, MEMBERS, 0, 0, tiled=True)
    got = got.reshape(4, 2, n, w, c)
    return got.transpose(2, 0, 1, 3, 4).reshape(n, 4, 2 * w, c)


def group_scatter(partial):
    n, _, w2, c = partial.shape
    sent = partial.astype(bf16).reshape(n, 4, 2, w2 // 2, c).transpose(1, 2, 0, 3, 4)
    got = lax.all_to_all(sent.reshape(8, n, w2 // 2, c), MEMBERS, 0, 0, tiled=True)
    return jnp.sum(got.astype(f32), axis=0)[:, None]


def far_gather(part):
    got = (
        pair_gather(part[None], "zh", 0)
        if size_of("zh") == 2
        else lax.all_gather(part, "zh", axis=0)
    )
    got = pair_gather(got[:, None], "x", 1)
    zh, _, _, r, o = got.shape
    got = got.reshape(zh, 2, 2, 2, 2, r, o).transpose(0, 2, 3, 1, 4, 5, 6)
    return got.reshape(zh * 16 * r, o)


def far_scatter(grad, kind=bf16):
    zh = size_of("zh")
    o = grad.shape[1]
    r = grad.shape[0] // (16 * zh)
    split = grad.reshape(zh, 2, 2, 2, 2, r, o).transpose(3, 0, 1, 2, 4, 5, 6)
    split = pair_scatter(split, "x", 0, kind)[0]
    if zh == 2:
        split = pair_scatter(split, "zh", 0, kind)[0]
    else:
        split = lax.psum_scatter(split, "zh", scatter_dimension=0)
    return split.reshape(8, r, o)


def adamw(weight, moment, second, grad, decay):
    new_mom = beta_first * moment + (1.0 - beta_first) * grad
    new_sec = beta_second * second + (1.0 - beta_second) * grad * grad
    corrected = new_mom / (1.0 - beta_first**STEP)
    spread = jnp.sqrt(new_sec / (1.0 - beta_second**STEP))
    return (
        new_mom,
        new_sec,
        weight - learn_rate * (corrected / (spread + epsilon) + decay * weight),
    )


def shards(
    features,
    skip_feat,
    labels,
    pixel_weight,
    valid_mask,
    conv_first,
    conv_first_mom,
    conv_first_sec,
    conv_second,
    conv_second_mom,
    conv_second_sec,
    up_conv,
    up_conv_mom,
    up_conv_sec,
    conv_merge,
    conv_merge_mom,
    conv_merge_sec,
    head_weight,
    head_mom,
    head_sec,
    biases,
    biases_mom,
    biases_sec,
):
    core = lax.axis_index("core")
    member = (lax.axis_index("zl") * 2 + lax.axis_index("y")) * 2 + core
    zh, x = lax.axis_index("zh"), lax.axis_index("x")

    r1 = conv_first.shape[0] // C1
    low_one = conv_first.astype(bf16).reshape(r1, C1 // 8, 8).transpose(2, 0, 1)
    low_one = lax.all_to_all(low_one, MEMBERS, 0, 0, tiled=True)
    kernel_one = far_gather(low_one).reshape(3, 3, C0, C1 // 8)
    r2 = conv_second.shape[0] // C1
    low_two = conv_second.astype(bf16).reshape(r2, C1)
    if r2 % 8 == 0:
        low_two = low_two.reshape(r2 // 8, 8, C1).transpose(1, 0, 2)
        low_two = lax.all_to_all(low_two, MEMBERS, 0, 0, tiled=True)
        kernel_two = far_gather(low_two)
    else:
        low_two = lax.all_gather(low_two, AXES, axis=0, tiled=True).reshape(-1, 8, C1)
        kernel_two = lax.dynamic_index_in_dim(low_two, member, axis=1, keepdims=False)
    kernel_two = kernel_two.reshape(3, 3, C1 // 8, C1)

    def chip_kernel(flat):
        rows_in = flat.shape[0] // C0
        cut = flat.astype(bf16).reshape(rows_in, 2, C0 // 2).transpose(1, 0, 2)
        cut = pair_swap(cut).reshape(2 * rows_in, C0 // 2)
        return lax.all_gather(cut, CHIPS, axis=0, tiled=True)

    def pair_swap(cut):
        own = lax.dynamic_slice_in_dim(cut, core, 1, axis=0)
        away = lax.dynamic_slice_in_dim(cut, 1 - core, 1, axis=0)
        return in_order(own, swapped(away, "core"), "core", 0)

    kernel_up = chip_kernel(up_conv).reshape(2, 2, C1, C0 // 2)
    kernel_merge = chip_kernel(conv_merge).reshape(3, 3, 2 * C0, C0 // 2)

    bias_one = lax.dynamic_index_in_dim(
        biases[:C1].reshape(C1 // 8, 8), member, axis=1, keepdims=False
    )
    bias_two = biases[C1 : 2 * C1]
    bias_up = lax.dynamic_slice_in_dim(biases[2 * C1 : 2 * C1 + C0], core * (C0 // 2), C0 // 2)
    bias_three = lax.dynamic_slice_in_dim(
        biases[2 * C1 + C0 : 2 * C1 + 2 * C0], core * (C0 // 2), C0 // 2
    )
    bias_head = biases[2 * C1 + 2 * C0 :]
    head_low = lax.dynamic_slice_in_dim(
        head_weight.astype(bf16), core * (C0 // 2), C0 // 2, axis=0
    )

    count_all = total(jnp.sum(valid_mask.astype(f32)))

    feat = group_gather(features)
    feat = padded(feat, "zh", 1, 2)
    feat = padded(feat, "x", 2, 2)
    pre_one = convolve(feat, kernel_one) + bias_one
    high, wide = pre_one.shape[1], pre_one.shape[2]
    row_at = jnp.arange(high)
    col_at = jnp.arange(wide)
    row_in = ((row_at > 0) | (zh > 0)) & ((row_at < high - 1) | (zh < size_of("zh") - 1))
    col_in = ((col_at > 0) | (x > 0)) & ((col_at < wide - 1) | (x < size_of("x") - 1))
    inside = (row_in[:, None] & col_in[None, :])[None, :, :, None]
    act_one = jnp.where(inside, jax.nn.gelu(pre_one), 0.0).astype(bf16)
    pre_two = group_scatter(convolve(act_one, kernel_two)) + bias_two
    act_two = jax.nn.gelu(pre_two).astype(bf16)

    skip = padded(pair_gather(skip_feat, "core", 2), ROWS, 1, 1)
    skip = padded(skip, "x", 2, 1)
    act_chip = pair_gather(act_two, "core", 2)
    images, rows_in, cols_in = act_chip.shape[:3]
    ups = jnp.einsum("nhwc,abco->nhawbo", act_chip, kernel_up, preferred_element_type=f32)
    ups = ups.reshape(images, 2 * rows_in, 2 * cols_in, C0 // 2) + bias_up
    ups = padded(ups.astype(bf16), ROWS, 1, 1)
    ups = padded(ups, "x", 2, 1)
    joined = jnp.concatenate([pair_gather(ups, "core", 3), skip], axis=3)
    pre_three = convolve(joined, kernel_merge) + bias_three
    act_three = jax.nn.gelu(pre_three).astype(bf16)
    logits = jnp.einsum("nhwc,ck->nhwk", act_three, head_low, preferred_element_type=f32)
    logits = logits + swapped(logits, "core") + bias_head

    marks = jnp.stack([labels, valid_mask * pixel_weight])
    marks = pair_gather(marks, "core", 3)
    scaled = marks[1].astype(f32)
    onehot = (marks[0][..., None] == jnp.arange(CLASSES, dtype=jnp.int32)).astype(f32)
    log_probs = jax.nn.log_softmax(logits, axis=-1)
    loss_part = -0.5 * jnp.sum(scaled * jnp.sum(onehot * log_probs, axis=-1))
    grad_logits = ((jnp.exp(log_probs) - onehot) * (scaled / count_all)[..., None]).astype(bf16)

    head_part = jnp.einsum("nhwc,nhwk->ck", act_three, grad_logits, preferred_element_type=f32)
    grad_act_three = jnp.einsum("nhwk,ck->nhwc", grad_logits, head_low, preferred_element_type=f32)
    grad_pre_three = gelu_back(pre_three, grad_act_three).astype(bf16)
    merge_grad = kernel_grad(joined, grad_pre_three)
    border = padded(grad_pre_three, ROWS, 1, 1)
    border = padded(border, "x", 2, 1)
    grad_ups = convolve(border, turned(kernel_merge[:, :, :C0]))
    grad_upper = pair_scatter(grad_ups, "core", 3, bf16).astype(bf16)
    grad_blocks = grad_upper.reshape(images, rows_in, 2, cols_in, 2, C0 // 2)
    up_grad = jnp.einsum(
        "nhwc,nhawbo->abco", act_chip, grad_blocks, preferred_element_type=f32
    ).reshape(-1, C0 // 2)
    grad_act_two = jnp.einsum(
        "nhawbo,abco->nhwc", grad_blocks, kernel_up, preferred_element_type=f32
    )
    grad_act_two = pair_scatter(grad_act_two, "core", 2, f32)
    grad_pre_two = gelu_back(pre_two, grad_act_two).astype(bf16)

    grad_two = group_gather(grad_pre_two)
    second_grad = kernel_grad(act_one, grad_two)
    spill = convolve(grad_two, turned(kernel_two), 2)
    inner = spill[:, 1:-1]
    inner = inner.at[:, :1].add(shifted(spill[:, -1:], "zh", 1))
    inner = inner.at[:, -1:].add(shifted(spill[:, :1], "zh", -1))
    core_part = inner[:, :, 1:-1]
    core_part = core_part.at[:, :, :1].add(shifted(inner[:, :, -1:], "x", 1))
    core_part = core_part.at[:, :, -1:].add(shifted(inner[:, :, :1], "x", -1))
    grad_pre_one = gelu_back(pre_one[:, 1:-1, 1:-1], core_part).astype(bf16)
    first_grad = kernel_grad(feat[:, 1:-1, 1:-1], grad_pre_one)

    def chip_grad(grad):
        mine = lax.psum_scatter(grad.astype(bf16), CHIPS, scatter_dimension=0, tiled=True)
        rows_out = mine.shape[0] // 2
        cut = pair_swap(mine.reshape(2, rows_out, C0 // 2))
        return cut.transpose(1, 0, 2).reshape(-1).astype(f32)

    share_merge = chip_grad(merge_grad)
    share_up = chip_grad(up_grad)
    if r2 % 8 == 0:
        part_two = far_scatter(second_grad).astype(bf16)
        part_two = lax.all_to_all(part_two, MEMBERS, 0, 0, tiled=True)
        share_two = part_two.transpose(1, 0, 2).reshape(-1).astype(f32)
    else:
        mine = jnp.arange(8)[None, :, None] == member
        part_two = jnp.where(mine, second_grad.astype(bf16)[:, None], 0)
        share_two = lax.psum_scatter(
            part_two.reshape(-1, C1), AXES, scatter_dimension=0, tiled=True
        ).reshape(-1).astype(f32)
    part_one = far_scatter(first_grad).astype(bf16)
    part_one = lax.all_to_all(part_one, MEMBERS, 0, 0, tiled=True)
    share_one = part_one.transpose(1, 2, 0).reshape(-1).astype(f32)

    share_sq = (
        jnp.sum(share_one * share_one)
        + jnp.sum(share_two * share_two)
        + jnp.sum(share_up * share_up)
        + jnp.sum(share_merge * share_merge)
    )
    spread_one = (
        jnp.where(jnp.arange(8)[None, :] == member, column_sum(grad_pre_one)[:, None], 0.0)
    ).reshape(-1)

    def half_of(values):
        shape = (2 * values.shape[0],) + values.shape[1:]
        return lax.dynamic_update_slice_in_dim(
            jnp.zeros(shape, f32), values, core * values.shape[0], axis=0
        )

    packed = jnp.concatenate(
        [
            spread_one,
            column_sum(grad_pre_two),
            half_of(column_sum(grad_upper)),
            half_of(column_sum(grad_pre_three)),
            0.5 * column_sum(grad_logits),
            half_of(head_part).reshape(-1),
            share_sq[None],
            loss_part[None],
        ]
    )
    packed = total(packed)
    bias_total = packed[: biases.shape[0]]
    head_total = packed[biases.shape[0] : -2].reshape(head_weight.shape)
    sq_total, loss_total = packed[-2], packed[-1]
    grad_norm = jnp.sqrt(
        sq_total + jnp.sum(bias_total * bias_total) + jnp.sum(head_total * head_total)
    )
    factor = clip_norm / jnp.maximum(grad_norm, clip_norm)
    outs = ()
    for weight, moment, second, grad, decay in (
        (conv_first, conv_first_mom, conv_first_sec, share_one, weight_decay),
        (conv_second, conv_second_mom, conv_second_sec, share_two, weight_decay),
        (up_conv, up_conv_mom, up_conv_sec, share_up, weight_decay),
        (conv_merge, conv_merge_mom, conv_merge_sec, share_merge, weight_decay),
        (head_weight, head_mom, head_sec, head_total, weight_decay),
        (biases, biases_mom, biases_sec, bias_total, 0.0),
    ):
        outs += adamw(weight, moment, second, grad * factor, decay)
    return outs + (loss_total, count_all, grad_norm)


def solution(mesh):
    rows, cols = mesh.shape["rows"], mesh.shape["cols"]
    split = Mesh(mesh.devices.reshape(rows // 4, 2, 2, cols // 2, 2), AXES)
    image = P(None, ROWS, ("x", "core"))
    flat = P(AXES)
    return jax.shard_map(
        shards,
        mesh=split,
        in_specs=(image,) * 5 + (flat,) * 12 + (P(),) * 6,
        out_specs=(flat,) * 12 + (P(),) * 9,
        check_vma=False,
    )
```

```python
import jax
import jax.numpy as jnp
from jax import lax
from jax.experimental import pallas as pl
from jax.experimental.pallas import tpu as pltpu
from jax.sharding import Mesh
from jax.sharding import PartitionSpec as P

C0 = 512
C1 = 1024
CLASSES = 2
STEP = 10

clip_norm = 0.05
learn_rate = 0.02
beta_first = 0.9
beta_second = 0.999
epsilon = 1e-08
weight_decay = 0.1

AXES = ("zh", "zl", "y", "x", "core")
MEMBERS = ("zl", "y", "core")
CHIPS = ("zh", "zl", "y", "x")
ROWS = ("zh", "zl", "y")
bf16 = jnp.bfloat16
f32 = jnp.float32


def size_of(axis):
    return lax.axis_size(axis)


def shifted(values, axis, step):
    count = size_of(axis)
    return lax.ppermute(
        values, axis, [(i, i + step) for i in range(count) if 0 <= i + step < count]
    )


def swapped(values, axis):
    return lax.ppermute(values, axis, [(0, 1), (1, 0)])


def padded(cells, axis, dim, width):
    head = lax.slice_in_dim(cells, 0, width, axis=dim)
    tail = lax.slice_in_dim(cells, cells.shape[dim] - width, cells.shape[dim], axis=dim)
    return jnp.concatenate(
        [shifted(tail, axis, 1), cells, shifted(head, axis, -1)], axis=dim
    )


def in_order(own, other, axis, dim):
    first = lax.axis_index(axis) == 0
    return jnp.concatenate(
        [jnp.where(first, own, other), jnp.where(first, other, own)], axis=dim
    )


def pair_gather(own, axis, dim):
    return in_order(own, swapped(own, axis), axis, dim)


def pair_half(values, axis, dim, index):
    width = values.shape[dim] // 2
    return lax.dynamic_slice_in_dim(values, index * width, width, axis=dim)


def pair_scatter(values, axis, dim, kind):
    me = lax.axis_index(axis)
    away = pair_half(values, axis, dim, 1 - me).astype(kind)
    return pair_half(values, axis, dim, me).astype(f32) + swapped(away, axis).astype(f32)


def total(values, axes=("core", "x", "y", "zl", "zh")):
    for axis in axes:
        if size_of(axis) == 2:
            values = values + swapped(values, axis)
        else:
            values = lax.psum(values, axis)
    return values


def convolve(values, kernel, pad=0):
    return lax.conv_general_dilated(
        values,
        kernel,
        (1, 1),
        ((pad, pad), (pad, pad)),
        dimension_numbers=("NHWC", "HWIO", "NHWC"),
        preferred_element_type=f32,
    )


def kernel_grad(cells, grad):
    rows_in, cols_in = (grad.shape[1], grad.shape[2])
    terms = [
        jnp.einsum(
            "nhwc,nhwo->co",
            cells[:, shift_h : shift_h + rows_in, shift_w : shift_w + cols_in],
            grad,
            preferred_element_type=f32,
        )
        for shift_h in range(3)
        for shift_w in range(3)
    ]
    return jnp.concatenate(terms, axis=0)


def turned(kernel):
    return jnp.swapaxes(kernel[::-1, ::-1], 2, 3)


def gelu_back(pre_act, upstream):
    return jax.vjp(jax.nn.gelu, pre_act)[1](upstream)[0]


def column_sum(values):
    return jnp.sum(values, axis=tuple(range(values.ndim - 1)), dtype=f32)


def group_gather(block):
    n, _, w, c = block.shape
    sent = jnp.broadcast_to(block[None], (8,) + block.shape)
    got = lax.all_to_all(sent, MEMBERS, 0, 0, tiled=True)
    got = got.reshape(4, 2, n, w, c)
    return got.transpose(2, 0, 1, 3, 4).reshape(n, 4, 2 * w, c)


def group_scatter(partial):
    n, _, w2, c = partial.shape
    sent = partial.astype(bf16).reshape(n, 4, 2, w2 // 2, c).transpose(1, 2, 0, 3, 4)
    got = lax.all_to_all(sent.reshape(8, n, w2 // 2, c), MEMBERS, 0, 0, tiled=True)
    return jnp.sum(got.astype(f32), axis=0)[:, None]


def over_zh(part):
    if size_of("zh") == 2:
        return pair_gather(part[None], "zh", 0)
    return lax.all_gather(part, "zh", axis=0)


def over_x(part):
    part = pair_gather(part[:, None], "x", 1)
    zh, _, _, r, o = part.shape
    return part.reshape(zh, 2, 2, 2, 2, r, o).transpose(0, 2, 3, 1, 4, 5, 6)


def far_scatter(grad, kind=bf16):
    zh = size_of("zh")
    o = grad.shape[1]
    r = grad.shape[0] // (16 * zh)
    split = grad.reshape(zh, 2, 2, 2, 2, r, o).transpose(3, 0, 1, 2, 4, 5, 6)
    split = pair_scatter(split, "x", 0, kind)[0]
    if zh == 2:
        split = pair_scatter(split, "zh", 0, kind)[0]
    else:
        split = lax.psum_scatter(split, "zh", scatter_dimension=0)
    return split.reshape(8, r, o)


VMEM_LIMIT = 60 * 1024 * 1024
HALF = C0 // 2


def joined_on(values, axis):
    return jnp.concatenate([values, swapped(values, axis)], axis=0)


def kept_on(own, away, axis):
    got = swapped(away, axis)
    half = own.shape[0] // 2
    sums = [
        v.astype(f32) + w.astype(f32)
        for v, w in ((own[:half], got[:half]), (own[half:], got[half:]))
    ]
    return sums[0].astype(bf16), sums[1].astype(bf16)


def place(chunk, me, first):
    bits = [me[i] if not (chunk >> (4 - i)) & 1 else 1 - me[i] for i in range(5)]
    zh, zl, y, x, core = bits
    high, low = (zl, y) if first == "y" else (y, zl)
    return high * 16 + low * 8 + x * 4 + zh * 2 + core


def pieces_of(rows, cut, zhs):
    if zhs != 2:
        return [(0, None, 0, rows, 0)]
    return cut


def chunk_list(r3, ru, zhs):
    cut = (r3 + ru) // 2
    merge, up = [], []
    for chunk in range(32):
        merge.append((0, (chunk, "y"), 0, cut, r3 * chunk))
        merge.append((1, (chunk, "zl"), 0, r3 - cut, r3 * chunk + cut))
        up.append((0, (chunk, "zl"), r3 - cut, ru, ru * chunk))
    return pieces_of(32 * r3, merge, zhs), pieces_of(32 * ru, up, zhs)


def copies(pieces, me, sources, target, sems):
    made = []
    for i, (which, spot, start, count, to) in enumerate(pieces):
        at = 0 if spot is None else place(spot[0], me, spot[1])
        there = sources[which].at[at, pl.ds(start, count), :]
        here = target.at[pl.ds(to, count), :]
        made.append(pltpu.make_async_copy(there, here, sems.at[i]))
    return made


def send_out(pieces, me, targets, source, sems):
    made = []
    for i, (which, spot, _, count, to) in enumerate(pieces):
        at = 0 if spot is None else place(spot[0], me, spot[1])
        here = source.at[pl.ds(to, count), :]
        if spot is None:
            pltpu.make_async_copy(here, targets[which].at[0], sems.at[i]).start()
        else:
            for side in range(2):
                inside = at - 16 * side

                @pl.when((inside >= 0) & (inside < 16))
                def _(here=here, there=targets[which + side], inside=inside, i=i):
                    pltpu.make_async_copy(here, there.at[inside], sems.at[i]).start()

        made.append(pltpu.make_async_copy(here, targets[which].at[0], sems.at[i]))
    for copy in made:
        copy.wait()


def on_chip(body, ins, outs, scratch, spaces, flops):
    kinds = {"v": pltpu.VMEM, "s": pltpu.SMEM, "a": pl.ANY}
    moved = sum(v.size * v.dtype.itemsize for v in list(ins) + list(outs))
    return pl.pallas_call(
        body,
        out_shape=outs,
        in_specs=[pl.BlockSpec(memory_space=kinds[k]) for k in spaces[0]],
        out_specs=[pl.BlockSpec(memory_space=kinds[k]) for k in spaces[1]],
        scratch_shapes=scratch,
        compiler_params=pltpu.CompilerParams(vmem_limit_bytes=VMEM_LIMIT),
        cost_estimate=pl.CostEstimate(flops=flops, bytes_accessed=moved, transcendentals=0),
    )(*ins)


def up_on_chip(me, own, other, source, bias, pieces):
    def body(me_ref, own_ref, other_ref, source_ref, bias_ref, ups_ref, kernel_ref, act_ref, sems):
        made = copies(pieces, me_ref, (source_ref,), kernel_ref, sems)
        for copy in made:
            copy.start()
        core = me_ref[4]
        mine = pl.ds(pl.multiple_of(core * 32, 32), 32)
        yours = pl.ds(pl.multiple_of((1 - core) * 32, 32), 32)
        for image in range(2):
            act_ref[image, mine, :] = own_ref[image]
            act_ref[image, yours, :] = other_ref[image]
        for copy in made:
            copy.wait()
        values = act_ref[...].reshape(128, C1)
        for tap in range(4):
            got = jnp.dot(
                values, kernel_ref[tap * C1 : (tap + 1) * C1, :], preferred_element_type=f32
            )
            got = (got + bias_ref[...]).astype(bf16).reshape(2, 64, HALF)
            for image in range(2):
                ups_ref[image, tap // 2, tap % 2] = got[image]

    return on_chip(
        body,
        (me, own, other, source, bias),
        (
            jax.ShapeDtypeStruct((2, 2, 2, 64, HALF), bf16),
            jax.ShapeDtypeStruct((4 * C1, HALF), bf16),
            jax.ShapeDtypeStruct((2, 64, C1), bf16),
        ),
        [pltpu.SemaphoreType.DMA((len(pieces),))],
        ("svvav", "vvv"),
        2 * 128 * C1 * 4 * HALF,
    )


def planes_in(target, lanes, rows_ref, sides_ref):
    line = lax.broadcasted_iota(jnp.int32, (64, 1), 0)
    for image in range(2):
        for row in range(4):
            even = rows_ref[image, row, 0]
            odd = rows_ref[image, row, 1]
            target[image, row, 1, :, lanes] = even
            target[image, row, 2, :, lanes] = odd
            left = sides_ref[0, image, row : row + 1, :].astype(f32)
            right = sides_ref[1, image, row : row + 1, :].astype(f32)
            moved = pltpu.roll(odd.astype(f32), 1, 0)
            target[image, row, 0, :, lanes] = jnp.where(line == 0, left, moved).astype(bf16)
            moved = pltpu.roll(even.astype(f32), 63, 0)
            target[image, row, 3, :, lanes] = jnp.where(line == 63, right, moved).astype(bf16)


def tapped(planes, image, tap, lanes):
    high, wide = tap // 3, tap % 3
    cells = planes[image, high : high + 2, wide : wide + 2, :, lanes]
    return cells.reshape(256, cells.shape[-1])


def merge_on_chip(me, own, other, own_sides, other_sides, skip, sources, bias, head, pieces):
    count = len(sources)

    def body(me_ref, own_ref, other_ref, own_sides_ref, other_sides_ref, skip_ref, bias_ref, head_ref, *rest):
        source_refs = rest[:count]
        pre_ref, logits_ref, planes_ref, kernel, sems = rest[count:]
        made = copies(pieces, me_ref, source_refs, kernel, sems)
        for copy in made:
            copy.start()
        core = me_ref[4]
        planes_in(planes_ref, slice(0, HALF), own_ref, own_sides_ref)
        planes_in(planes_ref, slice(HALF, C0), other_ref, other_sides_ref)
        planes_ref[:, :, :, :, C0:] = skip_ref[...]
        for copy in made:
            copy.wait()
        for image in range(2):
            total = jnp.broadcast_to(bias_ref[...], (256, HALF))
            for tap in range(9):
                base = tap * 2 * C0
                for lanes, start, size in (
                    (slice(0, HALF), pl.multiple_of(base + core * HALF, HALF), HALF),
                    (slice(HALF, C0), pl.multiple_of(base + (1 - core) * HALF, HALF), HALF),
                    (slice(C0, 2 * C0), base + C0, C0),
                ):
                    total = total + jnp.dot(
                        tapped(planes_ref, image, tap, lanes),
                        kernel[pl.ds(start, size), :],
                        preferred_element_type=f32,
                    )
            rows = slice(image * 256, (image + 1) * 256)
            pre_ref[rows, :] = total
            act = jax.nn.gelu(total).astype(bf16)
            logits_ref[rows, :] = jnp.dot(act, head_ref[...], preferred_element_type=f32)

    return on_chip(
        body,
        (me, own, other, own_sides, other_sides, skip, bias, head, *sources),
        (
            jax.ShapeDtypeStruct((512, HALF), f32),
            jax.ShapeDtypeStruct((512, 128), f32),
            jax.ShapeDtypeStruct((2, 4, 4, 64, 2 * C0), bf16),
        ),
        [pltpu.VMEM((18 * C0, HALF), bf16), pltpu.SemaphoreType.DMA((len(pieces),))],
        ("svvvvvvv" + "a" * count, "vvv"),
        2 * 512 * 18 * C0 * HALF,
    )


def ups_grad_on_chip(me, rows, sides, sources, pieces):
    count = len(sources)

    def body(me_ref, rows_ref, sides_ref, *rest):
        source_refs = rest[:count]
        own_ref, away_ref, planes, kernel, sems = rest[count:]
        made = copies(pieces, me_ref, source_refs, kernel, sems)
        for copy in made:
            copy.start()
        core = me_ref[4]
        planes_in(planes, slice(0, HALF), rows_ref, sides_ref)
        for copy in made:
            copy.wait()
        for image in range(2):
            lines = slice(image * 256, (image + 1) * 256)
            for target, half in ((own_ref, core), (away_ref, 1 - core)):
                total = jnp.zeros((256, HALF), f32)
                for tap in range(9):
                    start = pl.multiple_of((8 - tap) * 2 * C0 + half * HALF, HALF)
                    total = total + lax.dot_general(
                        tapped(planes, image, tap, slice(0, HALF)),
                        kernel[pl.ds(start, HALF), :],
                        (((1,), (1,)), ((), ())),
                        preferred_element_type=f32,
                    )
                target[lines, :] = total.astype(target.dtype)

    return on_chip(
        body,
        (me, rows, sides, *sources),
        (jax.ShapeDtypeStruct((512, HALF), f32), jax.ShapeDtypeStruct((512, HALF), bf16)),
        [
            pltpu.VMEM((2, 4, 4, 64, HALF), bf16),
            pltpu.VMEM((18 * C0, HALF), bf16),
            pltpu.SemaphoreType.DMA((len(pieces),)),
        ],
        ("svv" + "a" * count, "vv"),
        2 * 512 * 9 * C0 * HALF,
    )


def merge_grad_on_chip(me, planes, grad, pieces, shapes):
    def body(me_ref, planes_ref, grad_ref, *rest):
        out_refs = rest[: len(shapes)]
        whole, sems = rest[len(shapes) :]
        core = me_ref[4]
        for tap in range(9):
            base = tap * 2 * C0
            for lanes, start, size in (
                (slice(0, HALF), pl.multiple_of(base + core * HALF, HALF), HALF),
                (slice(HALF, C0), pl.multiple_of(base + (1 - core) * HALF, HALF), HALF),
                (slice(C0, 2 * C0), base + C0, C0),
            ):
                total = jnp.zeros((size, HALF), f32)
                for image in range(2):
                    total = total + lax.dot_general(
                        tapped(planes_ref, image, tap, lanes),
                        grad_ref[image * 256 : (image + 1) * 256, :],
                        (((0,), (0,)), ((), ())),
                        preferred_element_type=f32,
                    )
                whole[pl.ds(start, size), :] = total.astype(bf16)
        send_out(pieces, me_ref, out_refs, whole, sems)

    return on_chip(
        body,
        (me, planes, grad),
        tuple(jax.ShapeDtypeStruct(shape, bf16) for shape in shapes),
        [pltpu.VMEM((18 * C0, HALF), bf16), pltpu.SemaphoreType.DMA((len(pieces),))],
        ("svv", "a" * len(shapes)),
        2 * 512 * 18 * C0 * HALF,
    )


def up_grad_on_chip(me, act, grad, pieces, shapes):
    def body(me_ref, act_ref, grad_ref, *rest):
        out_refs = rest[: len(shapes)]
        whole, sems = rest[len(shapes) :]
        values = act_ref[...].reshape(128, C1)
        for tap in range(4):
            cells = grad_ref[:, tap // 2, tap % 2].reshape(128, HALF)
            total = lax.dot_general(
                values, cells, (((0,), (0,)), ((), ())), preferred_element_type=f32
            )
            whole[tap * C1 : (tap + 1) * C1, :] = total.astype(bf16)
        send_out(pieces, me_ref, out_refs, whole, sems)

    return on_chip(
        body,
        (me, act, grad),
        tuple(jax.ShapeDtypeStruct(shape, bf16) for shape in shapes),
        [pltpu.VMEM((4 * C1, HALF), bf16), pltpu.SemaphoreType.DMA((len(pieces),))],
        ("svv", "a" * len(shapes)),
        2 * 128 * C1 * 4 * HALF,
    )


def split_list(rows, zhs):
    if zhs != 2:
        return [(0, None, 0, 32 * rows, 0)], [(1, 32 * rows, HALF)]
    half = rows // 2
    pieces = []
    for chunk in range(32):
        pieces.append((0, (chunk, "y"), 0, half, rows * chunk))
        pieces.append((2, (chunk, "zl"), 0, half, rows * chunk + half))
    return pieces, [(16, half, HALF)] * 4


def first_sum(parts):
    if len(parts) == 1:
        return parts
    return kept_on(*parts[:2], "zl") + kept_on(*parts[2:], "y")


def second_sum(parts):
    if len(parts) == 1:
        return parts
    first, second = kept_on(*parts[:2], "y"), kept_on(*parts[2:], "zl")
    return tuple(jnp.concatenate(pair, axis=1) for pair in zip(first, second))


def cross_sum(parts):
    return kept_on(*parts, "x") if len(parts) == 2 else parts


def last_sum(parts):
    if len(parts) == 2:
        return parts[0].astype(f32) + swapped(parts[1], "zh").astype(f32)
    whole = parts[0].reshape(8 * size_of("zh"), 2, -1, HALF)
    whole = lax.psum_scatter(whole, CHIPS, scatter_dimension=0)
    return in_order_back(whole).astype(f32)


def in_order_back(pair):
    own = lax.dynamic_index_in_dim(pair, lax.axis_index("core"), axis=0)
    away = lax.dynamic_index_in_dim(pair, 1 - lax.axis_index("core"), axis=0)
    return jnp.concatenate([own, away], axis=0)


def crossed(values, step):
    count = size_of("zh") * 4
    moves = [
        (2 * i + side, 2 * (i + step) + 1 - side)
        for i in range(count)
        for side in range(2)
        if 0 <= i + step < count
    ]
    return lax.ppermute(values, ROWS + ("x",), moves)


def halo(cells):
    left_chip = lax.axis_index("x") == 0
    edge = jnp.where(left_chip, cells[:, :, 1, 63], cells[:, :, 0, 0])
    above = shifted(cells[:, 1:], ROWS, 1)
    below = shifted(cells[:, :1], ROWS, -1)
    beside = jnp.concatenate(
        [crossed(edge[:, 1:], 1), swapped(edge, "x"), crossed(edge[:, :1], -1)], axis=1
    )
    rows = jnp.concatenate([above, cells, below], axis=1)
    none = jnp.zeros_like(beside)
    sides = jnp.stack([jnp.where(left_chip, none, beside), jnp.where(left_chip, beside, none)])
    return rows, sides


def adamw(weight, moment, second, grad, decay):
    new_mom = beta_first * moment + (1.0 - beta_first) * grad
    new_sec = beta_second * second + (1.0 - beta_second) * grad * grad
    corrected = new_mom / (1.0 - beta_first**STEP)
    spread = jnp.sqrt(new_sec / (1.0 - beta_second**STEP))
    return (
        new_mom,
        new_sec,
        weight - learn_rate * (corrected / (spread + epsilon) + decay * weight),
    )


def shards(
    features,
    skip_feat,
    labels,
    pixel_weight,
    valid_mask,
    conv_first,
    conv_first_mom,
    conv_first_sec,
    conv_second,
    conv_second_mom,
    conv_second_sec,
    up_conv,
    up_conv_mom,
    up_conv_sec,
    conv_merge,
    conv_merge_mom,
    conv_merge_sec,
    head_weight,
    head_mom,
    head_sec,
    biases,
    biases_mom,
    biases_sec,
):
    core = lax.axis_index("core")
    member = (lax.axis_index("zl") * 2 + lax.axis_index("y")) * 2 + core
    zh, x = lax.axis_index("zh"), lax.axis_index("x")

    channel = jnp.arange(8)[:, None] + 8 * jnp.arange(C1 // 8)[None, :]
    sorting = (jnp.arange(C1)[:, None, None] == channel[None]).astype(bf16)
    r1 = conv_first.shape[0] // C1
    r2 = conv_second.shape[0] // C1
    even = r2 % 8 == 0
    count_own = jnp.sum(valid_mask).astype(bf16)
    low_one = jnp.einsum("rc,cqm->qrm", conv_first.astype(bf16).reshape(r1, C1), sorting)
    low_two = conv_second.astype(bf16)
    block = features.reshape(1, -1, 128)
    lead = [jnp.full((8, 16, 128), count_own, bf16), low_one]
    early = 0
    if even:
        low_two = low_two.reshape(r2 // 8, 8, C1 // 128, 128).transpose(1, 0, 2, 3)
        low_two = low_two.reshape(8, r2, 128)
        early = (r2 - r1 - 16) // 2 // 16 * 16
        lead.append(low_two[:, :early])
    lead_rows = 16 + r1 + early
    lead = jnp.concatenate(lead + [jnp.broadcast_to(block, (8,) + block.shape[1:])], axis=1)
    lead, low_two, conv_merge, up_conv, skip_feat, labels, pixel_weight = lax.optimization_barrier(
        (lead, low_two, conv_merge, up_conv, skip_feat, labels, pixel_weight)
    )

    lead = lax.all_to_all(lead, MEMBERS, 0, 0, tiled=True)
    tail = lax.all_to_all(low_two[:, early:], MEMBERS, 0, 0, tiled=True) if even else low_two
    r3 = conv_merge.shape[0] // C0
    ru = up_conv.shape[0] // C0
    zhs = size_of("zh")
    me = jnp.stack([lax.axis_index(axis) for axis in AXES]).astype(jnp.int32)
    low_chip = jnp.concatenate(
        [conv_merge.astype(bf16).reshape(r3, C0), up_conv.astype(bf16).reshape(ru, C0)], axis=0
    )
    low_chip = in_order_back(low_chip.reshape(r3 + ru, 2, HALF).transpose(1, 0, 2))
    low_chip = jnp.concatenate([low_chip[:1], swapped(low_chip[1:], "core")], axis=0)
    merge_pieces, up_pieces = chunk_list(r3 * zhs // 2, ru * zhs // 2, zhs)
    if zhs == 2:
        low_chip = joined_on(low_chip, "zh")
    skip = padded(pair_gather(skip_feat, "core", 2), ROWS, 1, 1)
    marks = pair_gather(jnp.stack([labels, valid_mask * pixel_weight]), "core", 3)
    lead, low_chip, skip, marks = lax.optimization_barrier((lead, low_chip, skip, marks))

    feat = lead[:, lead_rows:].reshape((4, 2) + features.shape[:1] + features.shape[2:])
    feat = feat.transpose(2, 0, 1, 3, 4)
    feat = feat.reshape(feat.shape[0], 4, 2 * feat.shape[3], C0)
    lead = lead[:, :lead_rows].reshape(-1, 128)
    if zhs == 2:
        edge = jnp.where(zh == 0, feat[:, -2:], feat[:, :2])
        got = swapped(jnp.concatenate([lead, edge.reshape(-1, 128)], axis=0), "zh")
        edge = got[8 * lead_rows :].reshape(edge.shape)
        none = jnp.zeros_like(edge)
        feat = jnp.concatenate(
            [jnp.where(zh == 0, none, edge), feat, jnp.where(zh == 0, edge, none)], axis=1
        )
        lead = in_order(lead, got[: 8 * lead_rows], "zh", 0)
    else:
        feat = padded(feat, "zh", 1, 2)
        lead = lax.all_gather(lead, "zh", axis=0, tiled=True)
    skip = padded(skip, "x", 2, 1)
    skip = jnp.stack(
        [skip[:, :, 0:128:2], skip[:, :, 1:129:2], skip[:, :, 2:130:2], skip[:, :, 3:130:2]], axis=2
    )
    marks = marks.reshape(2, 2, 2, 64, 2).swapaxes(3, 4)
    first = second = jnp.zeros((), bf16)
    if zhs == 2:
        low_chip = joined_on(low_chip, "x")
        cut = (r3 + ru) // 2
        first, second = low_chip[:, :cut], low_chip[:, cut:]
    feat, skip, lead, tail, first, second, marks = lax.optimization_barrier(
        (feat, skip, lead, tail, first, second, marks)
    )

    edge = jnp.where(x == 0, feat[:, :, -2:], feat[:, :, :2])
    got = swapped(jnp.concatenate([lead, edge.reshape(-1, 128)], axis=0), "x")
    edge = got[lead.shape[0] :].reshape(edge.shape)
    none = jnp.zeros_like(edge)
    feat = jnp.concatenate(
        [jnp.where(x == 0, none, edge), feat, jnp.where(x == 0, edge, none)], axis=2
    )

    def ordered(own, other):
        both = jnp.stack([own, other]).reshape(2, zhs, 2, 2, 2, -1, 128)
        return jnp.where(x == 0, both, both[::-1]).transpose(1, 2, 3, 0, 4, 5, 6)

    lead = ordered(lead, got[: lead.shape[0]])
    if even:
        tail = tail.reshape(-1, 128)
        if zhs == 2:
            tail = in_order(tail, swapped(tail, "zh"), "zh", 0)
        else:
            tail = lax.all_gather(tail, "zh", axis=0, tiled=True)
    if zhs == 2:
        first = joined_on(first, "y")
        second = joined_on(second, "zl")
    feat, lead, tail, first, second = lax.optimization_barrier((feat, lead, tail, first, second))

    count_all = jnp.sum(lead[..., 0, 0].astype(f32))
    kernel_one = lead[..., 16 : 16 + r1, :].reshape(3, 3, C0, C1 // 8)
    if even:
        tail = ordered(tail, swapped(tail, "x"))
        kernel_two = jnp.concatenate([lead[..., 16 + r1 :, :], tail], axis=5)
    else:
        low_two = lax.all_gather(tail.reshape(r2, C1), AXES, axis=0, tiled=True)
        low_two = low_two.reshape(-1, 8, C1)
        kernel_two = lax.dynamic_index_in_dim(low_two, member, axis=1, keepdims=False)
    kernel_two = kernel_two.reshape(3, 3, C1 // 8, C1)
    if zhs == 2:
        first = joined_on(first, "zl")
        second = joined_on(second, "y")
    bias_one = lax.dynamic_index_in_dim(
        biases[:C1].reshape(C1 // 8, 8), member, axis=1, keepdims=False
    )
    bias_two = biases[C1 : 2 * C1]
    bias_up = lax.dynamic_slice_in_dim(biases[2 * C1 : 2 * C1 + C0], core * (C0 // 2), C0 // 2)
    bias_three = lax.dynamic_slice_in_dim(
        biases[2 * C1 + C0 : 2 * C1 + 2 * C0], core * (C0 // 2), C0 // 2
    )
    bias_head = biases[2 * C1 + 2 * C0 :]
    head_low = lax.dynamic_slice_in_dim(
        head_weight.astype(bf16), core * (C0 // 2), C0 // 2, axis=0
    )

    pre_one = convolve(feat, kernel_one) + bias_one
    high, wide = pre_one.shape[1], pre_one.shape[2]
    row_at = jnp.arange(high)
    col_at = jnp.arange(wide)
    row_in = ((row_at > 0) | (zh > 0)) & ((row_at < high - 1) | (zh < size_of("zh") - 1))
    col_in = ((col_at > 0) | (x > 0)) & ((col_at < wide - 1) | (x < size_of("x") - 1))
    inside = (row_in[:, None] & col_in[None, :])[None, :, :, None]
    act_one = jnp.where(inside, jax.nn.gelu(pre_one), 0.0).astype(bf16)
    part_two = convolve(act_one, kernel_two)
    part_two, first, second = lax.optimization_barrier((part_two, first, second))
    if zhs == 2:
        merge_sources, up_source = (first, second), second
    else:
        low_chip = jnp.where(core == 0, low_chip, low_chip[::-1])
        low_chip = lax.all_gather(low_chip, CHIPS, axis=0, tiled=True)
        merge_sources = (low_chip[:, :r3].reshape(1, -1, HALF),)
        up_source = low_chip[:, r3:].reshape(1, -1, HALF)
    pre_two = group_scatter(part_two) + bias_two
    act_two = jax.nn.gelu(pre_two).astype(bf16)

    act_own = act_two[:, 0]
    ups, kernel_up, act_chip = up_on_chip(
        me, act_own, swapped(act_own, "core"), up_source, bias_up[None], up_pieces
    )
    ups, sides = halo(ups)
    head_wide = jnp.pad(head_low, ((0, 0), (0, 128 - CLASSES)))
    pre_three, logits, planes = merge_on_chip(
        me,
        ups,
        swapped(ups, "core"),
        sides,
        swapped(sides, "core"),
        skip,
        merge_sources,
        bias_three[None],
        head_wide,
        merge_pieces,
    )
    logits = (logits + swapped(logits, "core"))[:, :CLASSES] + bias_head
    logits = logits.reshape(2, 2, 2, 64, CLASSES)
    pre_three = pre_three.reshape(2, 2, 2, 64, HALF)
    act_three = jax.nn.gelu(pre_three).astype(bf16)

    scaled = marks[1].astype(f32)
    onehot = (marks[0][..., None] == jnp.arange(CLASSES, dtype=jnp.int32)).astype(f32)
    log_probs = jax.nn.log_softmax(logits, axis=-1)
    loss_part = -0.5 * jnp.sum(scaled * jnp.sum(onehot * log_probs, axis=-1))
    grad_logits = ((jnp.exp(log_probs) - onehot) * (scaled / count_all)[..., None]).astype(bf16)

    head_part = jnp.einsum("iabwc,iabwk->ck", act_three, grad_logits, preferred_element_type=f32)
    grad_act_three = jnp.einsum(
        "iabwk,ck->iabwc", grad_logits, head_low, preferred_element_type=f32
    )
    grad_pre_three = gelu_back(pre_three, grad_act_three).astype(bf16)
    border, border_sides = halo(grad_pre_three)
    split_three, shape_three = split_list(r3 * zhs // 2, zhs)
    merge_grad = merge_grad_on_chip(
        me, planes, grad_pre_three.reshape(512, HALF), split_three, shape_three
    )
    border, border_sides, merge_grad = lax.optimization_barrier((border, border_sides, merge_grad))
    merge_grad = first_sum(merge_grad)
    own_grad, away_grad = ups_grad_on_chip(me, border, border_sides, merge_sources, merge_pieces)
    grad_upper = (own_grad + swapped(away_grad, "core").astype(f32)).astype(bf16)
    grad_upper = grad_upper.reshape(2, 2, 2, 64, HALF)
    grad_act_two = jnp.einsum(
        "iabwo,abco->iwc",
        grad_upper,
        kernel_up.reshape(2, 2, C1, HALF),
        preferred_element_type=f32,
    )[:, None]
    grad_act_two = pair_scatter(grad_act_two, "core", 2, f32)
    grad_pre_two = gelu_back(pre_two, grad_act_two).astype(bf16)

    grad_two = group_gather(grad_pre_two)
    split_up, shape_up = split_list(ru * zhs // 2, zhs)
    up_grad = up_grad_on_chip(me, act_chip, grad_upper, split_up, shape_up)
    grad_two, merge_grad, up_grad = lax.optimization_barrier((grad_two, merge_grad, up_grad))
    spill = convolve(grad_two, turned(kernel_two), 2)
    inner = spill[:, 1:-1]
    inner = inner.at[:, :1].add(shifted(spill[:, -1:], "zh", 1))
    inner = inner.at[:, -1:].add(shifted(spill[:, :1], "zh", -1))
    inner, merge_grad, up_grad = lax.optimization_barrier((inner, merge_grad, up_grad))
    merge_grad, up_grad = second_sum(merge_grad), first_sum(up_grad)
    core_part = inner[:, :, 1:-1]
    core_part = core_part.at[:, :, :1].add(shifted(inner[:, :, -1:], "x", 1))
    core_part = core_part.at[:, :, -1:].add(shifted(inner[:, :, :1], "x", -1))
    core_part, grad_two, act_late = lax.optimization_barrier((core_part, grad_two, act_one))
    grad_pre_one = gelu_back(pre_one[:, 1:-1, 1:-1], core_part).astype(bf16)
    second_grad = kernel_grad(act_late, grad_two)
    first_grad = kernel_grad(feat[:, 1:-1, 1:-1], grad_pre_one)
    first_grad, merge_grad, up_grad = lax.optimization_barrier((first_grad, merge_grad, up_grad))
    up_grad = second_sum(up_grad)
    if zhs == 2:
        chip_parts = tuple(jnp.concatenate(pair, axis=1) for pair in zip(merge_grad, up_grad))
    else:
        chip_parts = (merge_grad[0], up_grad[0])

    if even:
        part_two = far_scatter(second_grad.astype(bf16).reshape(-1, 128))
        sq_two = jnp.sum(part_two * part_two)
        part_two = lax.all_to_all(part_two.astype(bf16), MEMBERS, 0, 0, tiled=True)
        part_two = part_two.reshape(8, r2 // 8, C1 // 128, 128).transpose(1, 0, 2, 3)
        share_two = part_two.reshape(-1).astype(f32)
    else:
        mine = jnp.arange(8)[None, :, None] == member
        part_two = jnp.where(mine, second_grad.astype(bf16)[:, None], 0)
        share_two = lax.psum_scatter(
            part_two.reshape(-1, C1), AXES, scatter_dimension=0, tiled=True
        ).reshape(-1).astype(f32)
        sq_two = jnp.sum(share_two * share_two)
    part_one = far_scatter(first_grad)
    sq_one = jnp.sum(part_one * part_one)
    part_one = lax.all_to_all(part_one.astype(bf16), MEMBERS, 0, 0, tiled=True)
    share_one = jnp.einsum("qrm,cqm->rc", part_one, sorting, preferred_element_type=f32).reshape(-1)
    if zhs == 2:
        part_chip = last_sum(cross_sum(chip_parts))
    else:
        part_chip = jnp.concatenate([last_sum(chip_parts[:1]), last_sum(chip_parts[1:])], axis=1)
    sq_chip = jnp.sum(part_chip * part_chip)
    part_chip = part_chip.astype(bf16)
    part_chip = in_order(part_chip[0], swapped(part_chip[1], "core"), "core", 1).astype(f32)
    share_merge = part_chip[:r3].reshape(-1)
    share_up = part_chip[r3:].reshape(-1)
    if even:
        part_two = far_scatter(second_grad.astype(bf16).reshape(-1, 128)).astype(bf16)
        part_two = lax.all_to_all(part_two, MEMBERS, 0, 0, tiled=True)
        part_two = part_two.reshape(8, r2 // 8, C1 // 128, 128).transpose(1, 0, 2, 3)
        share_two = part_two.reshape(-1).astype(f32)
    else:
        mine = jnp.arange(8)[None, :, None] == member
        part_two = jnp.where(mine, second_grad.astype(bf16)[:, None], 0)
        share_two = lax.psum_scatter(
            part_two.reshape(-1, C1), AXES, scatter_dimension=0, tiled=True
        ).reshape(-1).astype(f32)
    part_one = far_scatter(first_grad).astype(bf16)
    part_one = lax.all_to_all(part_one, MEMBERS, 0, 0, tiled=True)
    share_one = jnp.einsum("qrm,cqm->rc", part_one, sorting, preferred_element_type=f32).reshape(-1)

    share_sq = sq_one + sq_two + sq_chip
    spread_one = (
        jnp.where(jnp.arange(8)[None, :] == member, column_sum(grad_pre_one)[:, None], 0.0)
    ).reshape(-1)

    def half_of(values):
        shape = (2 * values.shape[0],) + values.shape[1:]
        return lax.dynamic_update_slice_in_dim(
            jnp.zeros(shape, f32), values, core * values.shape[0], axis=0
        )

    packed = jnp.concatenate(
        [
            spread_one,
            column_sum(grad_pre_two),
            half_of(column_sum(grad_upper)),
            half_of(column_sum(grad_pre_three)),
            0.5 * column_sum(grad_logits),
            half_of(head_part).reshape(-1),
            share_sq[None],
            loss_part[None],
        ]
    )
    packed = total(packed, ("core", "x", "y"))
    packed, share_one, share_two = lax.optimization_barrier((packed, share_one, share_two))
    packed = total(packed, ("zl", "zh"))
    bias_total = packed[: biases.shape[0]]
    head_total = packed[biases.shape[0] : -2].reshape(head_weight.shape)
    sq_total, loss_total = packed[-2], packed[-1]
    grad_norm = jnp.sqrt(
        sq_total + jnp.sum(bias_total * bias_total) + jnp.sum(head_total * head_total)
    )
    factor = clip_norm / jnp.maximum(grad_norm, clip_norm)
    outs = ()
    for weight, moment, second, grad, decay in (
        (conv_first, conv_first_mom, conv_first_sec, share_one, weight_decay),
        (conv_second, conv_second_mom, conv_second_sec, share_two, weight_decay),
        (up_conv, up_conv_mom, up_conv_sec, share_up, weight_decay),
        (conv_merge, conv_merge_mom, conv_merge_sec, share_merge, weight_decay),
        (head_weight, head_mom, head_sec, head_total, weight_decay),
        (biases, biases_mom, biases_sec, bias_total, 0.0),
    ):
        outs += adamw(weight, moment, second, grad * factor, decay)
    return outs + (loss_total, count_all, grad_norm)


def solution(mesh):
    rows, cols = mesh.shape["rows"], mesh.shape["cols"]
    split = Mesh(mesh.devices.reshape(rows // 4, 2, 2, cols // 2, 2), AXES)
    image = P(None, ROWS, ("x", "core"))
    flat = P(AXES)
    return jax.shard_map(
        shards,
        mesh=split,
        in_specs=(image,) * 5 + (flat,) * 12 + (P(),) * 6,
        out_specs=(flat,) * 12 + (P(),) * 9,
        check_vma=False,
    )
```

```python
import jax
import jax.numpy as jnp
from jax import lax
from jax.experimental import pallas as pl
from jax.experimental.pallas import tpu as pltpu
from jax.sharding import Mesh
from jax.sharding import PartitionSpec as P

C0 = 512
C1 = 1024
CLASSES = 2
STEP = 10

clip_norm = 0.05
learn_rate = 0.02
beta_first = 0.9
beta_second = 0.999
epsilon = 1e-08
weight_decay = 0.1

AXES = ("zh", "zl", "y", "x", "core")
MEMBERS = ("zl", "y", "core")
CHIPS = ("zh", "zl", "y", "x")
ROWS = ("zh", "zl", "y")
bf16 = jnp.bfloat16
f32 = jnp.float32


def size_of(axis):
    return lax.axis_size(axis)


def shifted(values, axis, step):
    count = size_of(axis)
    return lax.ppermute(
        values, axis, [(i, i + step) for i in range(count) if 0 <= i + step < count]
    )


def swapped(values, axis):
    return lax.ppermute(values, axis, [(0, 1), (1, 0)])


def padded(cells, axis, dim, width):
    head = lax.slice_in_dim(cells, 0, width, axis=dim)
    tail = lax.slice_in_dim(cells, cells.shape[dim] - width, cells.shape[dim], axis=dim)
    return jnp.concatenate(
        [shifted(tail, axis, 1), cells, shifted(head, axis, -1)], axis=dim
    )


def in_order(own, other, axis, dim):
    first = lax.axis_index(axis) == 0
    return jnp.concatenate(
        [jnp.where(first, own, other), jnp.where(first, other, own)], axis=dim
    )


def pair_gather(own, axis, dim):
    return in_order(own, swapped(own, axis), axis, dim)


def pair_half(values, axis, dim, index):
    width = values.shape[dim] // 2
    return lax.dynamic_slice_in_dim(values, index * width, width, axis=dim)


def pair_scatter(values, axis, dim, kind):
    me = lax.axis_index(axis)
    away = pair_half(values, axis, dim, 1 - me).astype(kind)
    return pair_half(values, axis, dim, me).astype(f32) + swapped(away, axis).astype(f32)


def total(values, axes=("core", "x", "y", "zl", "zh")):
    for axis in axes:
        if size_of(axis) == 2:
            values = values + swapped(values, axis)
        else:
            values = lax.psum(values, axis)
    return values


def convolve(values, kernel, pad=0):
    return lax.conv_general_dilated(
        values,
        kernel,
        (1, 1),
        ((pad, pad), (pad, pad)),
        dimension_numbers=("NHWC", "HWIO", "NHWC"),
        preferred_element_type=f32,
    )


def kernel_grad(cells, grad):
    rows_in, cols_in = (grad.shape[1], grad.shape[2])
    terms = [
        jnp.einsum(
            "nhwc,nhwo->co",
            cells[:, shift_h : shift_h + rows_in, shift_w : shift_w + cols_in],
            grad,
            preferred_element_type=f32,
        )
        for shift_h in range(3)
        for shift_w in range(3)
    ]
    return jnp.concatenate(terms, axis=0)


def turned(kernel):
    return jnp.swapaxes(kernel[::-1, ::-1], 2, 3)


def gelu_back(pre_act, upstream):
    return jax.vjp(jax.nn.gelu, pre_act)[1](upstream)[0]


def column_sum(values):
    return jnp.sum(values, axis=tuple(range(values.ndim - 1)), dtype=f32)


def group_gather(block):
    n, _, w, c = block.shape
    sent = jnp.broadcast_to(block[None], (8,) + block.shape)
    got = lax.all_to_all(sent, MEMBERS, 0, 0, tiled=True)
    got = got.reshape(4, 2, n, w, c)
    return got.transpose(2, 0, 1, 3, 4).reshape(n, 4, 2 * w, c)


def group_scatter(partial):
    n, _, w2, c = partial.shape
    sent = partial.astype(bf16).reshape(n, 4, 2, w2 // 2, c).transpose(1, 2, 0, 3, 4)
    got = lax.all_to_all(sent.reshape(8, n, w2 // 2, c), MEMBERS, 0, 0, tiled=True)
    return jnp.sum(got.astype(f32), axis=0)[:, None]


def over_zh(part):
    if size_of("zh") == 2:
        return pair_gather(part[None], "zh", 0)
    return lax.all_gather(part, "zh", axis=0)


def over_x(part):
    part = pair_gather(part[:, None], "x", 1)
    zh, _, _, r, o = part.shape
    return part.reshape(zh, 2, 2, 2, 2, r, o).transpose(0, 2, 3, 1, 4, 5, 6)


def far_scatter(grad, kind=bf16):
    zh = size_of("zh")
    o = grad.shape[1]
    r = grad.shape[0] // (16 * zh)
    split = grad.reshape(zh, 2, 2, 2, 2, r, o).transpose(3, 0, 1, 2, 4, 5, 6)
    split = pair_scatter(split, "x", 0, kind)[0]
    if zh == 2:
        split = pair_scatter(split, "zh", 0, kind)[0]
    else:
        split = lax.psum_scatter(split, "zh", scatter_dimension=0)
    return split.reshape(8, r, o)


VMEM_LIMIT = 60 * 1024 * 1024
HALF = C0 // 2


def joined_on(values, axis):
    return jnp.concatenate([values, swapped(values, axis)], axis=0)


def sent(parts, first_axis, second_axis):
    if len(parts) == 1:
        return parts
    return parts[0], swapped(parts[1], first_axis), parts[2], swapped(parts[3], second_axis)


def added(parts):
    out = ()
    for own, got in (parts[:2], parts[2:]):
        half = own.shape[0] // 2
        for v, w in ((own[:half], got[:half]), (own[half:], got[half:])):
            out += ((v.astype(f32) + w.astype(f32)).astype(bf16),)
    return out


def after(earlier, *parts):
    own = [part[::2] if isinstance(part, tuple) else (part,) for part in parts]
    earlier, own = lax.optimization_barrier((earlier, own))
    out = [earlier]
    for part, kept in zip(parts, own):
        if isinstance(part, tuple):
            out.append((kept[0], part[1], kept[1], part[3]))
        else:
            out.append(kept[0])
    return out


def place(chunk, me, first):
    bits = [me[i] if not (chunk >> (4 - i)) & 1 else 1 - me[i] for i in range(5)]
    zh, zl, y, x, core = bits
    high, low = (zl, y) if first == "y" else (y, zl)
    return high * 16 + low * 8 + x * 4 + zh * 2 + core


def chunk_list(r3, ru):
    cut = (r3 + ru) // 2
    merge, up = [], []
    for chunk in range(32):
        merge.append((0, (chunk, "y"), 0, cut, r3 * chunk))
        merge.append((2, (chunk, "zl"), 0, r3 - cut, r3 * chunk + cut))
        up.append((2, (chunk, "zl"), r3 - cut, ru, ru * chunk))
    return merge, up


def in_place(me, sources, merge_pieces, up_pieces):
    lists = (merge_pieces, up_pieces)
    count = len(merge_pieces) + len(up_pieces)

    def body(me_ref, *rest):
        source_refs, targets, sems = rest[:4], rest[4:6], rest[6]
        waits = []
        for pieces, target in zip(lists, targets):
            for which, spot, start, rows, to in pieces:
                sem = sems.at[len(waits)]
                here = target.at[pl.ds(to, rows), :]
                at = place(spot[0], me_ref, spot[1])
                for side in range(2):
                    inside = at - 16 * side

                    @pl.when((inside >= 0) & (inside < 16))
                    def _(source=source_refs[which + side], inside=inside, start=start, rows=rows, here=here, sem=sem):
                        there = source.at[inside, pl.ds(start, rows), :]
                        pltpu.make_async_copy(there, here, sem).start()

                there = source_refs[which].at[0, pl.ds(start, rows), :]
                waits.append(pltpu.make_async_copy(there, here, sem))
        for copy in waits:
            copy.wait()

    rows = [sum(piece[3] for piece in pieces) for pieces in lists]
    return on_chip(
        body,
        (me, *sources),
        tuple(jax.ShapeDtypeStruct((n, HALF), bf16) for n in rows),
        [pltpu.SemaphoreType.DMA((count,))],
        ("saaaa", "vv"),
        0,
    )


def send_out(pieces, me, targets, source, sems):
    made = []
    for i, (which, spot, _, count, to) in enumerate(pieces):
        at = 0 if spot is None else place(spot[0], me, spot[1])
        here = source.at[pl.ds(to, count), :]
        if spot is None:
            pltpu.make_async_copy(here, targets[which].at[0], sems.at[i]).start()
        else:
            for side in range(2):
                inside = at - 16 * side

                @pl.when((inside >= 0) & (inside < 16))
                def _(here=here, there=targets[which + side], inside=inside, i=i):
                    pltpu.make_async_copy(here, there.at[inside], sems.at[i]).start()

        made.append(pltpu.make_async_copy(here, targets[which].at[0], sems.at[i]))
    for copy in made:
        copy.wait()


def on_chip(body, ins, outs, scratch, spaces, flops):
    kinds = {"v": pltpu.VMEM, "s": pltpu.SMEM, "a": pl.ANY}
    moved = sum(v.size * v.dtype.itemsize for v in list(ins) + list(outs))
    return pl.pallas_call(
        body,
        out_shape=outs,
        in_specs=[pl.BlockSpec(memory_space=kinds[k]) for k in spaces[0]],
        out_specs=[pl.BlockSpec(memory_space=kinds[k]) for k in spaces[1]],
        scratch_shapes=scratch,
        compiler_params=pltpu.CompilerParams(vmem_limit_bytes=VMEM_LIMIT),
        cost_estimate=pl.CostEstimate(flops=flops, bytes_accessed=moved, transcendentals=0),
    )(*ins)


def up_on_chip(me, own, other, kernel, bias):
    def body(me_ref, own_ref, other_ref, kernel_ref, bias_ref, ups_ref, act_ref):
        core = me_ref[4]
        mine = pl.ds(pl.multiple_of(core * 32, 32), 32)
        yours = pl.ds(pl.multiple_of((1 - core) * 32, 32), 32)
        for image in range(2):
            act_ref[image, mine, :] = own_ref[image]
            act_ref[image, yours, :] = other_ref[image]
        values = act_ref[...].reshape(128, C1)
        for tap in range(4):
            got = jnp.dot(
                values, kernel_ref[tap * C1 : (tap + 1) * C1, :], preferred_element_type=f32
            )
            got = (got + bias_ref[...]).astype(bf16).reshape(2, 64, HALF)
            for image in range(2):
                ups_ref[image, tap // 2, tap % 2] = got[image]

    return on_chip(
        body,
        (me, own, other, kernel, bias),
        (
            jax.ShapeDtypeStruct((2, 2, 2, 64, HALF), bf16),
            jax.ShapeDtypeStruct((2, 64, C1), bf16),
        ),
        [],
        ("svvvv", "vv"),
        2 * 128 * C1 * 4 * HALF,
    )


def planes_in(target, lanes, rows_ref, sides_ref):
    line = lax.broadcasted_iota(jnp.int32, (64, 1), 0)
    for image in range(2):
        for row in range(4):
            even = rows_ref[image, row, 0]
            odd = rows_ref[image, row, 1]
            target[image, row, 1, :, lanes] = even
            target[image, row, 2, :, lanes] = odd
            left = sides_ref[0, image, row : row + 1, :].astype(f32)
            right = sides_ref[1, image, row : row + 1, :].astype(f32)
            moved = pltpu.roll(odd.astype(f32), 1, 0)
            target[image, row, 0, :, lanes] = jnp.where(line == 0, left, moved).astype(bf16)
            moved = pltpu.roll(even.astype(f32), 63, 0)
            target[image, row, 3, :, lanes] = jnp.where(line == 63, right, moved).astype(bf16)


def tapped(planes, image, tap, lanes):
    high, wide = tap // 3, tap % 3
    cells = planes[image, high : high + 2, wide : wide + 2, :, lanes]
    return cells.reshape(256, cells.shape[-1])


def merge_on_chip(me, own, other, own_sides, other_sides, skip, skip_sides, kernel, bias, head):
    def body(me_ref, own_ref, other_ref, own_sides_ref, other_sides_ref, skip_ref, skip_sides_ref, kernel_ref, bias_ref, head_ref, pre_ref, logits_ref, planes_ref):
        low, high = slice(0, HALF), slice(HALF, C0)

        @pl.when(me_ref[4] == 0)
        def _():
            planes_in(planes_ref, low, own_ref, own_sides_ref)
            planes_in(planes_ref, high, other_ref, other_sides_ref)

        @pl.when(me_ref[4] == 1)
        def _():
            planes_in(planes_ref, high, own_ref, own_sides_ref)
            planes_in(planes_ref, low, other_ref, other_sides_ref)

        planes_in(planes_ref, slice(C0, 2 * C0), skip_ref, skip_sides_ref)
        for image in range(2):
            total = jnp.broadcast_to(bias_ref[...], (256, HALF))
            for tap in range(9):
                total = total + jnp.dot(
                    tapped(planes_ref, image, tap, slice(0, 2 * C0)),
                    kernel_ref[tap * 2 * C0 : (tap + 1) * 2 * C0, :],
                    preferred_element_type=f32,
                )
            rows = slice(image * 256, (image + 1) * 256)
            pre_ref[rows, :] = total
            act = jax.nn.gelu(total).astype(bf16)
            logits_ref[rows, :] = jnp.dot(act, head_ref[...], preferred_element_type=f32)

    return on_chip(
        body,
        (me, own, other, own_sides, other_sides, skip, skip_sides, kernel, bias, head),
        (
            jax.ShapeDtypeStruct((512, HALF), f32),
            jax.ShapeDtypeStruct((512, 128), f32),
            jax.ShapeDtypeStruct((2, 4, 4, 64, 2 * C0), bf16),
        ),
        [],
        ("svvvvvvvvv", "vvv"),
        2 * 512 * 18 * C0 * HALF,
    )


def ups_grad_on_chip(me, rows, sides, kernel):
    def body(me_ref, rows_ref, sides_ref, kernel_ref, own_ref, away_ref, planes):
        core = me_ref[4]
        planes_in(planes, slice(0, HALF), rows_ref, sides_ref)
        for image in range(2):
            lines = slice(image * 256, (image + 1) * 256)
            for target, half in ((own_ref, core), (away_ref, 1 - core)):
                total = jnp.zeros((256, HALF), f32)
                for tap in range(9):
                    start = pl.multiple_of((8 - tap) * 2 * C0 + half * HALF, HALF)
                    total = total + lax.dot_general(
                        tapped(planes, image, tap, slice(0, HALF)),
                        kernel_ref[pl.ds(start, HALF), :],
                        (((1,), (1,)), ((), ())),
                        preferred_element_type=f32,
                    )
                target[lines, :] = total.astype(target.dtype)

    return on_chip(
        body,
        (me, rows, sides, kernel),
        (jax.ShapeDtypeStruct((512, HALF), f32), jax.ShapeDtypeStruct((512, HALF), bf16)),
        [pltpu.VMEM((2, 4, 4, 64, HALF), bf16)],
        ("svvv", "vv"),
        2 * 512 * 9 * C0 * HALF,
    )


def merge_grad_on_chip(me, planes, grad, pieces, shapes):
    def body(me_ref, planes_ref, grad_ref, *rest):
        out_refs = rest[: len(shapes)]
        whole, sems = rest[len(shapes) :]
        for tap in range(9):
            total = jnp.zeros((2 * C0, HALF), f32)
            for image in range(2):
                total = total + lax.dot_general(
                    tapped(planes_ref, image, tap, slice(0, 2 * C0)),
                    grad_ref[image * 256 : (image + 1) * 256, :],
                    (((0,), (0,)), ((), ())),
                    preferred_element_type=f32,
                )
            whole[tap * 2 * C0 : (tap + 1) * 2 * C0, :] = total.astype(bf16)
        send_out(pieces, me_ref, out_refs, whole, sems)

    return on_chip(
        body,
        (me, planes, grad),
        tuple(jax.ShapeDtypeStruct(shape, bf16) for shape in shapes),
        [pltpu.VMEM((18 * C0, HALF), bf16), pltpu.SemaphoreType.DMA((len(pieces),))],
        ("svv", "a" * len(shapes)),
        2 * 512 * 18 * C0 * HALF,
    )


def up_grad_on_chip(me, act, grad, pieces, shapes):
    def body(me_ref, act_ref, grad_ref, *rest):
        out_refs = rest[: len(shapes)]
        whole, sems = rest[len(shapes) :]
        values = act_ref[...].reshape(128, C1)
        for tap in range(4):
            cells = grad_ref[:, tap // 2, tap % 2].reshape(128, HALF)
            total = lax.dot_general(
                values, cells, (((0,), (0,)), ((), ())), preferred_element_type=f32
            )
            whole[tap * C1 : (tap + 1) * C1, :] = total.astype(bf16)
        send_out(pieces, me_ref, out_refs, whole, sems)

    return on_chip(
        body,
        (me, act, grad),
        tuple(jax.ShapeDtypeStruct(shape, bf16) for shape in shapes),
        [pltpu.VMEM((4 * C1, HALF), bf16), pltpu.SemaphoreType.DMA((len(pieces),))],
        ("svv", "a" * len(shapes)),
        2 * 128 * C1 * 4 * HALF,
    )


def side_list(first_rows, rows, chunks):
    return [
        ((chunk >> 1) & 1, (chunk >> 2) * 2 + (chunk & 1), rows * chunk, rows, first_rows)
        for chunk in range(chunks)
    ]


def two_ways(pieces, me, stays, goes, source, sems):
    for i, (side, at, start, count, to) in enumerate(pieces):
        here = source.at[pl.ds(start, count), :]
        for target, wanted in ((stays, side), (goes, 1 - side)):

            @pl.when(me[3] == wanted)
            def _(here=here, target=target, at=at, to=to, count=count, i=i):
                there = target.at[at, pl.ds(to, count), :]
                pltpu.make_async_copy(here, there, sems.at[i]).start()

    for i, (side, at, start, count, to) in enumerate(pieces):
        here = source.at[pl.ds(start, count), :]
        pltpu.make_async_copy(here, stays.at[at, pl.ds(to, count), :], sems.at[i]).wait()


def second_grad_on_chip(me, cells, grad, rows, chunks):
    images, width, outs = cells.shape[1], cells.shape[4], grad.shape[3]
    tiles = outs // 128
    pieces = side_list(0, rows, chunks)

    def body(me_ref, cells_ref, grad_ref, stays_ref, goes_ref, wide, narrow, sems):
        upstream = grad_ref[...].reshape(images * 256, outs)
        for tap in range(9):
            values = cells_ref[tap % 3, :, tap // 3 : tap // 3 + 4].reshape(images * 256, width)
            got = lax.dot_general(
                values, upstream, (((0,), (0,)), ((), ())), preferred_element_type=f32
            )
            for tile in range(tiles):
                wide[:, tile, :] = got[:, tile * 128 : (tile + 1) * 128]
            narrow[tap * width * tiles : (tap + 1) * width * tiles, :] = (
                wide[...].reshape(width * tiles, 128).astype(bf16)
            )
        two_ways(pieces, me_ref, stays_ref, goes_ref, narrow, sems)

    return on_chip(
        body,
        (me, cells, grad),
        (jax.ShapeDtypeStruct((chunks // 2, rows, 128), bf16),) * 2,
        [
            pltpu.VMEM((width, tiles, 128), f32),
            pltpu.VMEM((9 * width * tiles, 128), bf16),
            pltpu.SemaphoreType.DMA((chunks,)),
        ],
        ("svv", "aa"),
        2 * images * 256 * 9 * width * outs,
    )


def first_grad_on_chip(me, cells, grad, rows, chunks):
    images, width, outs = cells.shape[1], cells.shape[4], grad.shape[3]
    pieces = side_list(0, rows, chunks)

    def body(me_ref, cells_ref, grad_ref, stays_ref, goes_ref, narrow, sems):
        upstream = grad_ref[...].reshape(images * 256, outs)
        for tap in range(9):
            values = cells_ref[tap % 3, :, tap // 3 : tap // 3 + 4].reshape(images * 256, width)
            got = lax.dot_general(
                values, upstream, (((0,), (0,)), ((), ())), preferred_element_type=f32
            )
            narrow[tap * width : (tap + 1) * width, :] = got.astype(bf16)
        two_ways(pieces, me_ref, stays_ref, goes_ref, narrow, sems)

    return on_chip(
        body,
        (me, cells, grad),
        (jax.ShapeDtypeStruct((chunks // 2, rows, 128), bf16),) * 2,
        [pltpu.VMEM((9 * width, 128), bf16), pltpu.SemaphoreType.DMA((chunks,))],
        ("svv", "aa"),
        2 * images * 256 * 9 * width * outs,
    )


def by_shift(cells):
    return jnp.stack([cells[:, :, shift : shift + 64] for shift in range(3)])


def split_list(rows, zhs):
    if zhs != 2:
        return [(0, None, 0, 32 * rows, 0)], [(1, 32 * rows, HALF)]
    half = rows // 2
    pieces = []
    for chunk in range(32):
        pieces.append((0, (chunk, "y"), 0, half, rows * chunk))
        pieces.append((2, (chunk, "zl"), 0, half, rows * chunk + half))
    return pieces, [(16, half, HALF)] * 4


def last_sum(whole):
    whole = whole.reshape(8 * size_of("zh"), 2, -1, HALF)
    whole = lax.psum_scatter(whole, CHIPS, scatter_dimension=0)
    return in_order_back(whole).astype(f32)


def in_order_back(pair):
    own = lax.dynamic_index_in_dim(pair, lax.axis_index("core"), axis=0)
    away = lax.dynamic_index_in_dim(pair, 1 - lax.axis_index("core"), axis=0)
    return jnp.concatenate([own, away], axis=0)


def halo(cells):
    width = cells.shape[-1]
    left_chip = lax.axis_index("x") == 0
    edge = jnp.where(left_chip, cells[:, :, 1, 63], cells[:, :, 0, 0])
    beside = swapped(edge, "x")

    def with_side(row):
        return jnp.concatenate(
            [cells[:, row].reshape(-1, width), beside[:, row], jnp.zeros((14, width), bf16)], axis=0
        )

    above = shifted(with_side(1), ROWS, 1)
    below = shifted(with_side(0), ROWS, -1)
    shape = (2, 1, 2, 64, width)
    rows = jnp.concatenate(
        [above[:256].reshape(shape), cells, below[:256].reshape(shape)], axis=1
    )
    beside = jnp.concatenate(
        [above[256:258, None], beside, below[256:258, None]], axis=1
    )
    none = jnp.zeros_like(beside)
    sides = jnp.stack([jnp.where(left_chip, none, beside), jnp.where(left_chip, beside, none)])
    return rows, sides


def adamw(weight, moment, second, grad, decay):
    new_mom = beta_first * moment + (1.0 - beta_first) * grad
    new_sec = beta_second * second + (1.0 - beta_second) * grad * grad
    corrected = new_mom / (1.0 - beta_first**STEP)
    spread = jnp.sqrt(new_sec / (1.0 - beta_second**STEP))
    return (
        new_mom,
        new_sec,
        weight - learn_rate * (corrected / (spread + epsilon) + decay * weight),
    )


def shards(
    features,
    skip_feat,
    labels,
    pixel_weight,
    valid_mask,
    conv_first,
    conv_first_mom,
    conv_first_sec,
    conv_second,
    conv_second_mom,
    conv_second_sec,
    up_conv,
    up_conv_mom,
    up_conv_sec,
    conv_merge,
    conv_merge_mom,
    conv_merge_sec,
    head_weight,
    head_mom,
    head_sec,
    biases,
    biases_mom,
    biases_sec,
):
    core = lax.axis_index("core")
    member = (lax.axis_index("zl") * 2 + lax.axis_index("y")) * 2 + core
    zh, x = lax.axis_index("zh"), lax.axis_index("x")

    channel = jnp.arange(8)[:, None] + 8 * jnp.arange(C1 // 8)[None, :]
    sorting = (jnp.arange(C1)[:, None, None] == channel[None]).astype(bf16)
    r1 = conv_first.shape[0] // C1
    r2 = conv_second.shape[0] // C1
    even = r2 % 8 == 0
    count_own = jnp.sum(valid_mask).astype(bf16)
    low_one = jnp.einsum("rc,cqm->qrm", conv_first.astype(bf16).reshape(r1, C1), sorting)
    low_two = conv_second.astype(bf16)
    block = features.reshape(1, -1, 128)
    bundle = [jnp.full((8, 16, 128), count_own, bf16), low_one]
    kernel_rows = 16 + r1
    if even:
        low_two = low_two.reshape(r2 // 8, 8, C1 // 128, 128).transpose(1, 0, 2, 3)
        bundle.append(low_two.reshape(8, r2, 128))
        kernel_rows += r2
    bundle.append(jnp.broadcast_to(block, (8,) + block.shape[1:]))
    bundle, conv_merge, up_conv, skip_feat, labels, pixel_weight = lax.optimization_barrier(
        (jnp.concatenate(bundle, axis=1), conv_merge, up_conv, skip_feat, labels, pixel_weight)
    )

    bundle = lax.all_to_all(bundle, MEMBERS, 0, 0, tiled=True)
    r3 = conv_merge.shape[0] // C0
    ru = up_conv.shape[0] // C0
    zhs = size_of("zh")
    me = jnp.stack([lax.axis_index(axis) for axis in AXES]).astype(jnp.int32)
    low_chip = jnp.concatenate(
        [conv_merge.astype(bf16).reshape(r3, C0), up_conv.astype(bf16).reshape(ru, C0)], axis=0
    )
    low_chip = in_order_back(low_chip.reshape(r3 + ru, 2, HALF).transpose(1, 0, 2))
    low_chip = jnp.concatenate([low_chip[:1], swapped(low_chip[1:], "core")], axis=0)
    merge_pieces, up_pieces = chunk_list(r3, ru)
    if zhs == 2:
        low_chip = joined_on(low_chip, "zh")
    skip = skip_feat.reshape(2, 2, 32, 2, C0).swapaxes(2, 3)
    skip_cells = pair_gather(skip, "core", 3)
    marks = pair_gather(jnp.stack([labels, valid_mask * pixel_weight]), "core", 3)
    marks = marks.reshape(2, 2, 2, 64, 2).swapaxes(3, 4)
    bundle, low_chip, skip_cells = lax.optimization_barrier((bundle, low_chip, skip_cells))

    feat = bundle[:, kernel_rows:].reshape((4, 2) + features.shape[:1] + features.shape[2:])
    feat = feat.transpose(2, 0, 1, 3, 4)
    feat = feat.reshape(feat.shape[0], 4, 2 * feat.shape[3], C0)
    kernels = bundle[:, :kernel_rows].reshape(-1, 128)
    if zhs == 2:
        edge = jnp.where(zh == 0, feat[:, -2:], feat[:, :2])
        got = swapped(jnp.concatenate([kernels, edge.reshape(-1, 128)], axis=0), "zh")
        low_chip = joined_on(low_chip, "x")
        cut = (r3 + ru) // 2
        first, second = low_chip[:, :cut], low_chip[:, cut:]
        first, second = (first, swapped(first, "y")), (second, swapped(second, "zl"))
        feat, kernels, got = lax.optimization_barrier((feat, kernels, got))
        edge = got[8 * kernel_rows :].reshape(edge.shape)
        none = jnp.zeros_like(edge)
        feat = jnp.concatenate(
            [jnp.where(zh == 0, none, edge), feat, jnp.where(zh == 0, edge, none)], axis=1
        )
        kernels = in_order(kernels, got[: 8 * kernel_rows], "zh", 0)
    else:
        feat = padded(feat, "zh", 1, 2)
        kernels = lax.all_gather(kernels, "zh", axis=0, tiled=True)

    kernels = kernels.reshape(8 * zhs, kernel_rows, 128)
    lead = kernels[:, : 16 + r1].reshape(-1, 128)
    edge = jnp.where(x == 0, feat[:, :, -2:], feat[:, :, :2])
    got = swapped(jnp.concatenate([lead, edge.reshape(-1, 128)], axis=0), "x")
    if zhs == 2:
        got, first, second = lax.optimization_barrier((got, first, second))
    edge = got[lead.shape[0] :].reshape(edge.shape)
    none = jnp.zeros_like(edge)
    feat = jnp.concatenate(
        [jnp.where(x == 0, none, edge), feat, jnp.where(x == 0, edge, none)], axis=2
    )

    def ordered(own, other):
        both = jnp.stack([own, other]).reshape(2, zhs, 2, 2, 2, -1, 128)
        return jnp.where(x == 0, both, both[::-1]).transpose(1, 2, 3, 0, 4, 5, 6)

    lead = ordered(lead, got[: lead.shape[0]])
    count_all = jnp.sum(lead[..., 0, 0].astype(f32))
    kernel_one = lead[..., 16:, :].reshape(3, 3, C0, C1 // 8)
    if even:
        kernel_two = kernels[:, 16 + r1 :].reshape(-1, 128)
        kernel_two = ordered(kernel_two, swapped(kernel_two, "x"))
    else:
        low_two = lax.all_gather(low_two.reshape(r2, C1), AXES, axis=0, tiled=True)
        low_two = low_two.reshape(-1, 8, C1)
        kernel_two = lax.dynamic_index_in_dim(low_two, member, axis=1, keepdims=False)
    kernel_two = kernel_two.reshape(3, 3, C1 // 8, C1)
    if zhs == 2:
        first, second = jnp.concatenate(first, axis=0), jnp.concatenate(second, axis=0)
        first = (first, swapped(first, "zl"))
        second = (second, swapped(second, "y"))
    else:
        first = second = jnp.zeros((), bf16)

    bias_one = lax.dynamic_index_in_dim(
        biases[:C1].reshape(C1 // 8, 8), member, axis=1, keepdims=False
    )
    bias_two = biases[C1 : 2 * C1]
    bias_up = lax.dynamic_slice_in_dim(biases[2 * C1 : 2 * C1 + C0], core * (C0 // 2), C0 // 2)
    bias_three = lax.dynamic_slice_in_dim(
        biases[2 * C1 + C0 : 2 * C1 + 2 * C0], core * (C0 // 2), C0 // 2
    )
    bias_head = biases[2 * C1 + 2 * C0 :]
    head_low = lax.dynamic_slice_in_dim(
        head_weight.astype(bf16), core * (C0 // 2), C0 // 2, axis=0
    )

    pre_one = convolve(feat, kernel_one) + bias_one
    high, wide = pre_one.shape[1], pre_one.shape[2]
    row_at = jnp.arange(high)
    col_at = jnp.arange(wide)
    row_in = ((row_at > 0) | (zh > 0)) & ((row_at < high - 1) | (zh < size_of("zh") - 1))
    col_in = ((col_at > 0) | (x > 0)) & ((col_at < wide - 1) | (x < size_of("x") - 1))
    inside = (row_in[:, None] & col_in[None, :])[None, :, :, None]
    act_one = jnp.where(inside, jax.nn.gelu(pre_one), 0.0).astype(bf16)
    part_two = convolve(act_one, kernel_two)
    feat_shifts, act_shifts = by_shift(feat[:, 1:-1, 1:-1]), by_shift(act_one)
    skip, skip_sides = halo(skip_cells)
    part_two, first, second, skip, skip_sides, marks = lax.optimization_barrier(
        (part_two, first, second, skip, skip_sides, marks)
    )
    if zhs == 2:
        kernel_merge, kernel_up = in_place(me, first + second, merge_pieces, up_pieces)
    else:
        low_chip = jnp.where(core == 0, low_chip, low_chip[::-1])
        low_chip = lax.all_gather(low_chip, CHIPS, axis=0, tiled=True)
        kernel_merge = low_chip[:, :r3].reshape(-1, HALF)
        kernel_up = low_chip[:, r3:].reshape(-1, HALF)
    pre_two = group_scatter(part_two) + bias_two
    act_two = jax.nn.gelu(pre_two).astype(bf16)
    act_two, kernel_merge, kernel_up = lax.optimization_barrier((act_two, kernel_merge, kernel_up))

    act_own = act_two[:, 0]
    ups, act_chip = up_on_chip(me, act_own, swapped(act_own, "core"), kernel_up, bias_up[None])
    ups, sides = halo(ups)
    head_wide = jnp.pad(head_low, ((0, 0), (0, 128 - CLASSES)))
    pre_three, logits, planes = merge_on_chip(
        me,
        ups,
        swapped(ups, "core"),
        sides,
        swapped(sides, "core"),
        skip,
        skip_sides,
        kernel_merge,
        bias_three[None],
        head_wide,
    )
    logits = (logits + swapped(logits, "core"))[:, :CLASSES] + bias_head
    logits = logits.reshape(2, 2, 2, 64, CLASSES)
    pre_three = pre_three.reshape(2, 2, 2, 64, HALF)
    act_three = jax.nn.gelu(pre_three).astype(bf16)

    scaled = marks[1].astype(f32)
    onehot = (marks[0][..., None] == jnp.arange(CLASSES, dtype=jnp.int32)).astype(f32)
    log_probs = jax.nn.log_softmax(logits, axis=-1)
    loss_part = -0.5 * jnp.sum(scaled * jnp.sum(onehot * log_probs, axis=-1))
    grad_logits = ((jnp.exp(log_probs) - onehot) * (scaled / count_all)[..., None]).astype(bf16)

    head_part = jnp.einsum("iabwc,iabwk->ck", act_three, grad_logits, preferred_element_type=f32)
    grad_act_three = jnp.einsum(
        "iabwk,ck->iabwc", grad_logits, head_low, preferred_element_type=f32
    )
    grad_pre_three = gelu_back(pre_three, grad_act_three).astype(bf16)
    border, border_sides = halo(grad_pre_three)
    split_three, shape_three = split_list(r3 * zhs // 2, zhs)
    merge_grad = merge_grad_on_chip(
        me, planes, grad_pre_three.reshape(512, HALF), split_three, shape_three
    )
    border, border_sides, merge_grad = lax.optimization_barrier((border, border_sides, merge_grad))
    own_grad, away_grad = ups_grad_on_chip(me, border, border_sides, kernel_merge)
    grad_upper = (own_grad + swapped(away_grad, "core").astype(f32)).astype(bf16)
    grad_upper = grad_upper.reshape(2, 2, 2, 64, HALF)
    grad_act_two = jnp.einsum(
        "iabwo,abco->iwc",
        grad_upper,
        kernel_up.reshape(2, 2, C1, HALF),
        preferred_element_type=f32,
    )[:, None]
    grad_act_two = pair_scatter(grad_act_two, "core", 2, f32)
    grad_pre_two = gelu_back(pre_two, grad_act_two).astype(bf16)

    grad_two = group_gather(grad_pre_two)
    split_up, shape_up = split_list(ru * zhs // 2, zhs)
    up_grad = up_grad_on_chip(me, act_chip, grad_upper, split_up, shape_up)
    grad_two, merge_grad, up_grad = lax.optimization_barrier((grad_two, merge_grad, up_grad))
    if zhs == 2:
        second_grad = second_grad_on_chip(me, act_shifts, grad_two, r2, 16 * zhs)
    else:
        second_grad = kernel_grad(act_one, grad_two)
    spill = convolve(grad_two, turned(kernel_two), 2)
    if zhs == 2:
        row = jnp.where(zh == 0, spill[:, -1:], spill[:, :1])
        column = jnp.where(x == 0, spill[:, 1:-1, -1:], spill[:, 1:-1, :1])
        corner = jnp.where(x == 0, row[:, :, -1:], row[:, :, :1])
        corner = lax.ppermute(corner, ("zh", "x"), [(i, 3 - i) for i in range(4)])
        row = swapped(row[:, :, 1:-1], "zh")
        column = swapped(column, "x")
        row, column, corner, merge_grad, up_grad = lax.optimization_barrier(
            (row, column, corner, merge_grad, up_grad)
        )
        at_row = jnp.arange(4)[None, :, None, None] == jnp.where(zh == 0, 3, 0)
        at_column = jnp.arange(64)[None, None, :, None] == jnp.where(x == 0, 63, 0)
        core_part = (
            spill[:, 1:-1, 1:-1]
            + jnp.where(at_row, row, 0.0)
            + jnp.where(at_column, column, 0.0)
            + jnp.where(at_row & at_column, corner, 0.0)
        )
    else:
        inner = spill[:, 1:-1]
        inner = inner.at[:, :1].add(shifted(spill[:, -1:], "zh", 1))
        inner = inner.at[:, -1:].add(shifted(spill[:, :1], "zh", -1))
        core_part = inner[:, :, 1:-1]
        core_part = core_part.at[:, :, :1].add(shifted(inner[:, :, -1:], "x", 1))
        core_part = core_part.at[:, :, -1:].add(shifted(inner[:, :, :1], "x", -1))
    merge_grad, up_grad = sent(merge_grad, "zl", "y"), sent(up_grad, "zl", "y")
    grad_pre_one = gelu_back(pre_one[:, 1:-1, 1:-1], core_part).astype(bf16)
    tiled = zhs == 2
    if tiled:
        grad_pre_one, second_grad = lax.optimization_barrier((grad_pre_one, second_grad))
        first_grad = first_grad_on_chip(me, feat_shifts, grad_pre_one, r1, 16 * zhs)
        stays, goes = (jnp.concatenate(pair, axis=1) for pair in zip(first_grad, second_grad))
        part = stays.astype(f32) + swapped(goes, "x").astype(f32)
        part = part.reshape(2, 8, r1 + r2, 128)
        away = lax.dynamic_index_in_dim(part, 1 - zh, axis=0, keepdims=False).astype(bf16)
        own = lax.dynamic_index_in_dim(part, zh, axis=0, keepdims=False)
        got = swapped(away, "zh")
        merge_grad, up_grad = added(merge_grad), added(up_grad)
        merge_grad, up_grad = sent(merge_grad, "y", "zl"), sent(up_grad, "y", "zl")
        away, merge_grad, up_grad = after(away, merge_grad, up_grad)
        merge_grad, up_grad = added(merge_grad), added(up_grad)
        chip_stays, chip_goes = (
            jnp.concatenate([merge_grad[i], merge_grad[i + 2], up_grad[i], up_grad[i + 2]], axis=1)
            for i in range(2)
        )
        chip_got = swapped(chip_goes, "x")
        own = after(chip_goes, own)[1]
        part = own + got.astype(f32)
        part_low = part.astype(bf16)
        chip_stays = after(part_low, chip_stays)[1]
        chip_parts = chip_stays.astype(f32) + chip_got.astype(f32)
        part_chip = chip_parts[:2] + swapped(chip_parts[2:].astype(bf16), "zh").astype(f32)
        sq_kernels = jnp.sum(part * part)
        part = lax.all_to_all(part_low, MEMBERS, 0, 0, tiled=True)
        part_one, part_two = part[:, :r1], part[:, r1:]
        part_two = part_two.reshape(8, r2 // 8, C1 // 128, 128).transpose(1, 0, 2, 3)
        share_two = part_two.reshape(-1).astype(f32)
    else:
        first_grad = kernel_grad(feat[:, 1:-1, 1:-1], grad_pre_one)
        mine = jnp.arange(8)[None, :, None] == member
        part_two = jnp.where(mine, second_grad.astype(bf16)[:, None], 0)
        share_two = lax.psum_scatter(
            part_two.reshape(-1, C1), AXES, scatter_dimension=0, tiled=True
        ).reshape(-1).astype(f32)
        part_one = far_scatter(first_grad)
        sq_kernels = jnp.sum(share_two * share_two) + jnp.sum(part_one * part_one)
        part_one = lax.all_to_all(part_one.astype(bf16), MEMBERS, 0, 0, tiled=True)
        part_chip = jnp.concatenate(
            [last_sum(merge_grad[0]), last_sum(up_grad[0])], axis=1
        )
    share_one = jnp.einsum("qrm,cqm->rc", part_one, sorting, preferred_element_type=f32).reshape(-1)
    sq_chip = jnp.sum(part_chip * part_chip)
    part_chip = part_chip.astype(bf16)
    part_chip = in_order(part_chip[0], swapped(part_chip[1], "core"), "core", 1).astype(f32)
    share_merge = part_chip[:r3].reshape(-1)
    share_up = part_chip[r3:].reshape(-1)
    share_sq = sq_kernels + sq_chip
    spread_one = (
        jnp.where(jnp.arange(8)[None, :] == member, column_sum(grad_pre_one)[:, None], 0.0)
    ).reshape(-1)

    def half_of(values):
        shape = (2 * values.shape[0],) + values.shape[1:]
        return lax.dynamic_update_slice_in_dim(
            jnp.zeros(shape, f32), values, core * values.shape[0], axis=0
        )

    packed = jnp.concatenate(
        [
            spread_one,
            column_sum(grad_pre_two),
            half_of(column_sum(grad_upper)),
            half_of(column_sum(grad_pre_three)),
            0.5 * column_sum(grad_logits),
            half_of(head_part).reshape(-1),
            share_sq[None],
            loss_part[None],
        ]
    )
    packed = total(packed, ("core", "x", "y"))
    packed, share_one, share_two = lax.optimization_barrier((packed, share_one, share_two))
    packed = total(packed, ("zl", "zh"))
    bias_total = packed[: biases.shape[0]]
    head_total = packed[biases.shape[0] : -2].reshape(head_weight.shape)
    sq_total, loss_total = packed[-2], packed[-1]
    grad_norm = jnp.sqrt(
        sq_total + jnp.sum(bias_total * bias_total) + jnp.sum(head_total * head_total)
    )
    factor = clip_norm / jnp.maximum(grad_norm, clip_norm)
    outs = ()
    for weight, moment, second, grad, decay in (
        (conv_first, conv_first_mom, conv_first_sec, share_one, weight_decay),
        (conv_second, conv_second_mom, conv_second_sec, share_two, weight_decay),
        (up_conv, up_conv_mom, up_conv_sec, share_up, weight_decay),
        (conv_merge, conv_merge_mom, conv_merge_sec, share_merge, weight_decay),
        (head_weight, head_mom, head_sec, head_total, weight_decay),
        (biases, biases_mom, biases_sec, bias_total, 0.0),
    ):
        outs += adamw(weight, moment, second, grad * factor, decay)
    return outs + (loss_total, count_all, grad_norm)


def solution(mesh):
    rows, cols = mesh.shape["rows"], mesh.shape["cols"]
    split = Mesh(mesh.devices.reshape(rows // 4, 2, 2, cols // 2, 2), AXES)
    image = P(None, ROWS, ("x", "core"))
    flat = P(AXES)
    return jax.shard_map(
        shards,
        mesh=split,
        in_specs=(image,) * 5 + (flat,) * 12 + (P(),) * 6,
        out_specs=(flat,) * 12 + (P(),) * 9,
        check_vma=False,
    )
```

```python
import math

import jax
import jax.numpy as jnp
from jax import lax
from jax.experimental import pallas as pl
from jax.experimental.pallas import tpu as pltpu
from jax.sharding import Mesh
from jax.sharding import PartitionSpec as P

C0 = 512
C1 = 1024
CLASSES = 2
STEP = 10

clip_norm = 0.05
learn_rate = 0.02
beta_first = 0.9
beta_second = 0.999
epsilon = 1e-08
weight_decay = 0.1

AXES = ("zh", "zl", "y", "x", "core")
MEMBERS = ("zl", "y", "core")
CHIPS = ("zh", "zl", "y", "x")
ROWS = ("zh", "zl", "y")
bf16 = jnp.bfloat16
f32 = jnp.float32


def size_of(axis):
    return lax.axis_size(axis)


def shifted(values, axis, step):
    count = size_of(axis)
    return lax.ppermute(
        values, axis, [(i, i + step) for i in range(count) if 0 <= i + step < count]
    )


def swapped(values, axis):
    return lax.ppermute(values, axis, [(0, 1), (1, 0)])


def padded(cells, axis, dim, width):
    head = lax.slice_in_dim(cells, 0, width, axis=dim)
    tail = lax.slice_in_dim(cells, cells.shape[dim] - width, cells.shape[dim], axis=dim)
    return jnp.concatenate(
        [shifted(tail, axis, 1), cells, shifted(head, axis, -1)], axis=dim
    )


def in_order(own, other, axis, dim):
    first = lax.axis_index(axis) == 0
    return jnp.concatenate(
        [jnp.where(first, own, other), jnp.where(first, other, own)], axis=dim
    )


def pair_gather(own, axis, dim):
    return in_order(own, swapped(own, axis), axis, dim)


def pair_half(values, axis, dim, index):
    width = values.shape[dim] // 2
    return lax.dynamic_slice_in_dim(values, index * width, width, axis=dim)


def pair_scatter(values, axis, dim, kind):
    me = lax.axis_index(axis)
    away = pair_half(values, axis, dim, 1 - me).astype(kind)
    return pair_half(values, axis, dim, me).astype(f32) + swapped(away, axis).astype(f32)


def total(values, axes=("core", "x", "y", "zl", "zh")):
    for axis in axes:
        if size_of(axis) == 2:
            values = values + swapped(values, axis)
        else:
            values = lax.psum(values, axis)
    return values


def convolve(values, kernel, pad=0):
    return lax.conv_general_dilated(
        values,
        kernel,
        (1, 1),
        ((pad, pad), (pad, pad)),
        dimension_numbers=("NHWC", "HWIO", "NHWC"),
        preferred_element_type=f32,
    )


def kernel_grad(cells, grad):
    rows_in, cols_in = (grad.shape[1], grad.shape[2])
    terms = [
        jnp.einsum(
            "nhwc,nhwo->co",
            cells[:, shift_h : shift_h + rows_in, shift_w : shift_w + cols_in],
            grad,
            preferred_element_type=f32,
        )
        for shift_h in range(3)
        for shift_w in range(3)
    ]
    return jnp.concatenate(terms, axis=0)


def turned(kernel):
    return jnp.swapaxes(kernel[::-1, ::-1], 2, 3)


def gelu_back(pre_act, upstream):
    return jax.vjp(jax.nn.gelu, pre_act)[1](upstream)[0]


def column_sum(values):
    return jnp.sum(values, axis=tuple(range(values.ndim - 1)), dtype=f32)


def group_gather(block):
    return lax.all_to_all(
        jnp.broadcast_to(block[None], (8,) + block.shape), MEMBERS, 0, 0, tiled=True
    )


def group_scatter(partial):
    n, _, w2, c = partial.shape
    sent = partial.astype(bf16).reshape(n, 4, 2, w2 // 2, c).transpose(1, 2, 0, 3, 4)
    got = lax.all_to_all(sent.reshape(8, n, w2 // 2, c), MEMBERS, 0, 0, tiled=True)
    return jnp.sum(got.astype(f32), axis=0)[:, None]


def over_zh(part):
    if size_of("zh") == 2:
        return pair_gather(part[None], "zh", 0)
    return lax.all_gather(part, "zh", axis=0)


def over_x(part):
    part = pair_gather(part[:, None], "x", 1)
    zh, _, _, r, o = part.shape
    return part.reshape(zh, 2, 2, 2, 2, r, o).transpose(0, 2, 3, 1, 4, 5, 6)


def far_scatter(grad, kind=bf16):
    zh = size_of("zh")
    o = grad.shape[1]
    r = grad.shape[0] // (16 * zh)
    split = grad.reshape(zh, 2, 2, 2, 2, r, o).transpose(3, 0, 1, 2, 4, 5, 6)
    split = pair_scatter(split, "x", 0, kind)[0]
    if zh == 2:
        split = pair_scatter(split, "zh", 0, kind)[0]
    else:
        split = lax.psum_scatter(split, "zh", scatter_dimension=0)
    return split.reshape(8, r, o)


HALF = C0 // 2


def joined_on(values, axis):
    return jnp.concatenate([values, swapped(values, axis)], axis=0)


def sent(parts, first_axis, second_axis):
    if len(parts) == 1:
        return parts
    return parts[0], swapped(parts[1], first_axis), parts[2], swapped(parts[3], second_axis)


def added(parts):
    out = ()
    for own, got in (parts[:2], parts[2:]):
        half = own.shape[0] // 2
        for v, w in ((own[:half], got[:half]), (own[half:], got[half:])):
            out += ((v.astype(f32) + w.astype(f32)).astype(bf16),)
    return out


def after(earlier, *parts):
    own = [part[::2] if isinstance(part, tuple) else (part,) for part in parts]
    earlier, own = lax.optimization_barrier((earlier, own))
    out = [earlier]
    for part, kept in zip(parts, own):
        if isinstance(part, tuple):
            out.append((kept[0], part[1], kept[1], part[3]))
        else:
            out.append(kept[0])
    return out


def place(chunk, me, first):
    bits = [me[i] if not (chunk >> (4 - i)) & 1 else 1 - me[i] for i in range(5)]
    zh, zl, y, x, core = bits
    high, low = (zl, y) if first == "y" else (y, zl)
    return high * 16 + low * 8 + x * 4 + zh * 2 + core


def chunk_list(r3, ru):
    cut = (r3 + ru) // 2
    merge, up = [], []
    for chunk in range(32):
        merge.append((0, (chunk, "y"), 0, cut, r3 * chunk))
        merge.append((2, (chunk, "zl"), 0, r3 - cut, r3 * chunk + cut))
        up.append((2, (chunk, "zl"), r3 - cut, ru, ru * chunk))
    return merge, up


def in_place(me, sources, merge_pieces, up_pieces):
    lists = (merge_pieces, up_pieces)
    count = len(merge_pieces) + len(up_pieces)

    def body(me_ref, *rest):
        source_refs, targets, sems = rest[:4], rest[4:6], rest[6]
        waits = []
        for pieces, target in zip(lists, targets):
            for which, spot, start, rows, to in pieces:
                sem = sems.at[len(waits)]
                here = target.at[pl.ds(to, rows), :]
                at = place(spot[0], me_ref, spot[1])
                for side in range(2):
                    inside = at - 16 * side

                    @pl.when((inside >= 0) & (inside < 16))
                    def _(source=source_refs[which + side], inside=inside, start=start, rows=rows, here=here, sem=sem):
                        there = source.at[inside, pl.ds(start, rows), :]
                        pltpu.make_async_copy(there, here, sem).start()

                there = source_refs[which].at[0, pl.ds(start, rows), :]
                waits.append(pltpu.make_async_copy(there, here, sem))
        for copy in waits:
            copy.wait()

    rows = [sum(piece[3] for piece in pieces) for pieces in lists]
    return on_chip(
        body,
        (me, *sources),
        tuple(jax.ShapeDtypeStruct((n, HALF), bf16) for n in rows),
        [pltpu.SemaphoreType.DMA((count,))],
        ("saaaa", "vv"),
        0,
    )


def on_chip(body, ins, outs, scratch, spaces, flops):
    kinds = {"v": pltpu.VMEM, "s": pltpu.SMEM, "a": pl.ANY}
    held = [v for v, k in zip(list(ins) + list(outs), spaces[0] + spaces[1]) if k == "v"]
    held += [v for v in scratch if len(v.shape) > 1]
    room = sum(math.prod(v.shape) * jnp.dtype(v.dtype).itemsize for v in held)
    return pl.pallas_call(
        body,
        out_shape=outs,
        in_specs=[pl.BlockSpec(memory_space=kinds[k]) for k in spaces[0]],
        out_specs=[pl.BlockSpec(memory_space=kinds[k]) for k in spaces[1]],
        scratch_shapes=scratch,
        compiler_params=pltpu.CompilerParams(vmem_limit_bytes=int(1.25 * room) + 6 * 1024 * 1024),
        cost_estimate=pl.CostEstimate(flops=0, bytes_accessed=0, transcendentals=0),
    )(*ins)


def up_on_chip(me, own, other, kernel, bias):
    def body(me_ref, own_ref, other_ref, kernel_ref, bias_ref, ups_ref, act_ref):
        core = me_ref[4]
        mine = pl.ds(pl.multiple_of(core * 32, 32), 32)
        yours = pl.ds(pl.multiple_of((1 - core) * 32, 32), 32)
        for image in range(2):
            act_ref[image, mine, :] = own_ref[image]
            act_ref[image, yours, :] = other_ref[image]
        values = act_ref[...].reshape(128, C1)
        for tap in range(4):
            got = jnp.dot(
                values, kernel_ref[tap * C1 : (tap + 1) * C1, :], preferred_element_type=f32
            )
            got = (got + bias_ref[...]).astype(bf16).reshape(2, 64, HALF)
            for image in range(2):
                ups_ref[image, tap // 2, tap % 2] = got[image]

    return on_chip(
        body,
        (me, own, other, kernel, bias),
        (
            jax.ShapeDtypeStruct((2, 2, 2, 64, HALF), bf16),
            jax.ShapeDtypeStruct((2, 64, C1), bf16),
        ),
        [],
        ("svvvv", "vv"),
        2 * 128 * C1 * 4 * HALF,
    )


def planes_in(target, lanes, rows_ref, sides_ref):
    line = lax.broadcasted_iota(jnp.int32, (64, 1), 0)
    for image in range(2):
        for row in range(4):
            even = rows_ref[image, row, 0]
            odd = rows_ref[image, row, 1]
            target[image, row, 1, :, lanes] = even
            target[image, row, 2, :, lanes] = odd
            left = sides_ref[0, image, row : row + 1, :].astype(f32)
            right = sides_ref[1, image, row : row + 1, :].astype(f32)
            moved = pltpu.roll(odd.astype(f32), 1, 0)
            target[image, row, 0, :, lanes] = jnp.where(line == 0, left, moved).astype(bf16)
            moved = pltpu.roll(even.astype(f32), 63, 0)
            target[image, row, 3, :, lanes] = jnp.where(line == 63, right, moved).astype(bf16)


def tapped(planes, image, tap, lanes):
    high, wide = tap // 3, tap % 3
    cells = planes[image, high : high + 2, wide : wide + 2, :, lanes]
    return cells.reshape(256, cells.shape[-1])


def merge_on_chip(me, own, other, own_sides, other_sides, skip, skip_sides, kernel, bias, head):
    def body(me_ref, own_ref, other_ref, own_sides_ref, other_sides_ref, skip_ref, skip_sides_ref, kernel_ref, bias_ref, head_ref, pre_ref, logits_ref, planes_ref):
        low, high = slice(0, HALF), slice(HALF, C0)

        @pl.when(me_ref[4] == 0)
        def _():
            planes_in(planes_ref, low, own_ref, own_sides_ref)
            planes_in(planes_ref, high, other_ref, other_sides_ref)

        @pl.when(me_ref[4] == 1)
        def _():
            planes_in(planes_ref, high, own_ref, own_sides_ref)
            planes_in(planes_ref, low, other_ref, other_sides_ref)

        planes_in(planes_ref, slice(C0, 2 * C0), skip_ref, skip_sides_ref)
        for image in range(2):
            total = jnp.broadcast_to(bias_ref[...], (256, HALF))
            for tap in range(9):
                total = total + jnp.dot(
                    tapped(planes_ref, image, tap, slice(0, 2 * C0)),
                    kernel_ref[tap * 2 * C0 : (tap + 1) * 2 * C0, :],
                    preferred_element_type=f32,
                )
            pre_ref[image * 256 : (image + 1) * 256, :] = total
        act = jax.nn.gelu(pre_ref[...]).astype(bf16)
        logits_ref[...] = jnp.dot(act, head_ref[...], preferred_element_type=f32)

    return on_chip(
        body,
        (me, own, other, own_sides, other_sides, skip, skip_sides, kernel, bias, head),
        (
            jax.ShapeDtypeStruct((512, HALF), f32),
            jax.ShapeDtypeStruct((512, 128), f32),
            jax.ShapeDtypeStruct((2, 4, 4, 64, 2 * C0), bf16),
        ),
        [],
        ("svvvvvvvvv", "vvv"),
        2 * 512 * 18 * C0 * HALF,
    )


def ups_grad_on_chip(me, rows, sides, kernel):
    def body(me_ref, rows_ref, sides_ref, kernel_ref, own_ref, away_ref, planes):
        core = me_ref[4]
        planes_in(planes, slice(0, HALF), rows_ref, sides_ref)
        for image in range(2):
            lines = slice(image * 256, (image + 1) * 256)
            for target, half in ((own_ref, core), (away_ref, 1 - core)):
                total = jnp.zeros((256, HALF), f32)
                for tap in range(9):
                    start = pl.multiple_of((8 - tap) * 2 * C0 + half * HALF, HALF)
                    total = total + lax.dot_general(
                        tapped(planes, image, tap, slice(0, HALF)),
                        kernel_ref[pl.ds(start, HALF), :],
                        (((1,), (1,)), ((), ())),
                        preferred_element_type=f32,
                    )
                target[lines, :] = total.astype(target.dtype)

    return on_chip(
        body,
        (me, rows, sides, kernel),
        (jax.ShapeDtypeStruct((512, HALF), f32), jax.ShapeDtypeStruct((512, HALF), bf16)),
        [pltpu.VMEM((2, 4, 4, 64, HALF), bf16)],
        ("svvv", "vv"),
        2 * 512 * 9 * C0 * HALF,
    )


def chip_grads(me, planes, grad, act, ups_grad, r3, ru):
    high, low = r3 // 2, ru // 2
    pieces = []
    for chunk in range(32):
        pieces.append((0, 0, (chunk, "y"), r3 * chunk, high, 0))
        pieces.append((0, 2, (chunk, "zl"), r3 * chunk + high, high, 0))
        pieces.append((1, 0, (chunk, "y"), ru * chunk, low, high))
        pieces.append((1, 2, (chunk, "zl"), ru * chunk + low, low, high))

    def body(me_ref, planes_ref, grad_ref, act_ref, ups_grad_ref, *rest):
        targets, wholes, sems = rest[:4], rest[4:6], rest[6]
        values = act_ref[...].reshape(128, C1)
        for tap in range(4):
            cells = ups_grad_ref[:, tap // 2, tap % 2].reshape(128, HALF)
            total = lax.dot_general(
                values, cells, (((0,), (0,)), ((), ())), preferred_element_type=f32
            )
            wholes[1][tap * C1 : (tap + 1) * C1, :] = total.astype(bf16)
        for tap in range(9):
            total = jnp.zeros((2 * C0, HALF), f32)
            for image in range(2):
                total = total + lax.dot_general(
                    tapped(planes_ref, image, tap, slice(0, 2 * C0)),
                    grad_ref[image * 256 : (image + 1) * 256, :],
                    (((0,), (0,)), ((), ())),
                    preferred_element_type=f32,
                )
            wholes[0][tap * 2 * C0 : (tap + 1) * 2 * C0, :] = total.astype(bf16)
        waits = []
        for i, (whole, pair, spot, start, rows, to) in enumerate(pieces):
            here = wholes[whole].at[pl.ds(start, rows), :]
            at = place(spot[0], me_ref, spot[1])
            for side in range(2):
                inside = at - 16 * side

                @pl.when((inside >= 0) & (inside < 16))
                def _(here=here, target=targets[pair + side], inside=inside, rows=rows, to=to, i=i):
                    there = target.at[inside, pl.ds(to, rows), :]
                    pltpu.make_async_copy(here, there, sems.at[i]).start()

            there = targets[pair].at[0, pl.ds(to, rows), :]
            waits.append(pltpu.make_async_copy(here, there, sems.at[i]))
        for copy in waits:
            copy.wait()

    return on_chip(
        body,
        (me, planes, grad, act, ups_grad),
        (jax.ShapeDtypeStruct((16, high + low, HALF), bf16),) * 4,
        [
            pltpu.VMEM((18 * C0, HALF), bf16),
            pltpu.VMEM((4 * C1, HALF), bf16),
            pltpu.SemaphoreType.DMA((len(pieces),)),
        ],
        ("svvvv", "aaaa"),
        0,
    )


def side_list(first_rows, rows, chunks):
    return [
        ((chunk >> 1) & 1, (chunk >> 2) * 2 + (chunk & 1), rows * chunk, rows, first_rows)
        for chunk in range(chunks)
    ]


def two_ways(pieces, me, stays, goes, source, sems):
    for i, (side, at, start, count, to) in enumerate(pieces):
        here = source.at[pl.ds(start, count), :]
        for target, wanted in ((stays, side), (goes, 1 - side)):

            @pl.when(me[3] == wanted)
            def _(here=here, target=target, at=at, to=to, count=count, i=i):
                there = target.at[at, pl.ds(to, count), :]
                pltpu.make_async_copy(here, there, sems.at[i]).start()

    for i, (side, at, start, count, to) in enumerate(pieces):
        here = source.at[pl.ds(start, count), :]
        pltpu.make_async_copy(here, stays.at[at, pl.ds(to, count), :], sems.at[i]).wait()


def second_grad_on_chip(me, cells, grad, rows, chunks):
    images, width, outs = cells.shape[1], cells.shape[4], grad.shape[3]
    tiles = outs // 128
    pieces = side_list(0, rows, chunks)

    def body(me_ref, cells_ref, grad_ref, stays_ref, goes_ref, wide, narrow, sems):
        upstream = grad_ref[...].reshape(images * 256, outs)
        for tap in range(9):
            values = cells_ref[tap % 3, :, tap // 3 : tap // 3 + 4].reshape(images * 256, width)
            got = lax.dot_general(
                values, upstream, (((0,), (0,)), ((), ())), preferred_element_type=f32
            )
            for tile in range(tiles):
                wide[:, tile, :] = got[:, tile * 128 : (tile + 1) * 128]
            narrow[tap * width * tiles : (tap + 1) * width * tiles, :] = (
                wide[...].reshape(width * tiles, 128).astype(bf16)
            )
        two_ways(pieces, me_ref, stays_ref, goes_ref, narrow, sems)

    return on_chip(
        body,
        (me, cells, grad),
        (jax.ShapeDtypeStruct((chunks // 2, rows, 128), bf16),) * 2,
        [
            pltpu.VMEM((width, tiles, 128), f32),
            pltpu.VMEM((9 * width * tiles, 128), bf16),
            pltpu.SemaphoreType.DMA((chunks,)),
        ],
        ("svv", "aa"),
        2 * images * 256 * 9 * width * outs,
    )


def first_grad_on_chip(me, cells, grad, rows, chunks):
    images, width, outs = cells.shape[1], cells.shape[4], grad.shape[3]
    pieces = side_list(0, rows, chunks)

    def body(me_ref, cells_ref, grad_ref, stays_ref, goes_ref, narrow, sems):
        upstream = grad_ref[...].reshape(images * 256, outs)
        for tap in range(9):
            values = cells_ref[tap % 3, :, tap // 3 : tap // 3 + 4].reshape(images * 256, width)
            got = lax.dot_general(
                values, upstream, (((0,), (0,)), ((), ())), preferred_element_type=f32
            )
            narrow[tap * width : (tap + 1) * width, :] = got.astype(bf16)
        two_ways(pieces, me_ref, stays_ref, goes_ref, narrow, sems)

    return on_chip(
        body,
        (me, cells, grad),
        (jax.ShapeDtypeStruct((chunks // 2, rows, 128), bf16),) * 2,
        [pltpu.VMEM((9 * width, 128), bf16), pltpu.SemaphoreType.DMA((chunks,))],
        ("svv", "aa"),
        2 * images * 256 * 9 * width * outs,
    )


def second_back_on_chip(grad, kernel):
    images = grad.shape[1]

    def body(grad_ref, kernel_ref, order_ref, inner_ref, sides_ref, parts):
        for member in range(8):
            row, core = member // 2, member % 2
            for image in range(images):
                order_ref[image, row, core * 32 : (core + 1) * 32] = grad_ref[member, image, 0]
        parts[...] = jnp.zeros(parts.shape, f32)
        for image in range(images):
            values = order_ref[image].reshape(256, C1)
            for tap in range(9):
                got = lax.dot_general(
                    values,
                    kernel_ref[tap * 128 : (tap + 1) * 128, :],
                    (((1,), (1,)), ((), ())),
                    preferred_element_type=f32,
                )
                high = tap // 3
                parts[tap % 3, image, high : high + 4] += got.reshape(4, 64, 128)
        line = lax.broadcasted_iota(jnp.int32, (64, 1), 0)
        for image in range(images):
            for row in range(6):
                before = pltpu.roll(parts[0, image, row], 63, 0)
                later = pltpu.roll(parts[2, image, row], 1, 0)
                inner_ref[image, row] = (
                    parts[1, image, row]
                    + jnp.where(line == 63, 0.0, before)
                    + jnp.where(line == 0, 0.0, later)
                )
                sides_ref[0, image, row : row + 1, :] = parts[0, image, row, 0:1, :]
                sides_ref[1, image, row : row + 1, :] = parts[2, image, row, 63:64, :]

    return on_chip(
        body,
        (grad, kernel),
        (
            jax.ShapeDtypeStruct((images, 4, 64, C1), bf16),
            jax.ShapeDtypeStruct((images, 6, 64, 128), f32),
            jax.ShapeDtypeStruct((2, images, 6, 128), f32),
        ),
        [pltpu.VMEM((3, images, 6, 64, 128), f32)],
        ("vv", "vvv"),
        0,
    )


def by_shift(cells):
    return jnp.stack([cells[:, :, shift : shift + 64] for shift in range(3)])


def last_sum(whole):
    whole = whole.reshape(8 * size_of("zh"), 2, -1, HALF)
    whole = lax.psum_scatter(whole, CHIPS, scatter_dimension=0)
    return in_order_back(whole).astype(f32)


def in_order_back(pair):
    own = lax.dynamic_index_in_dim(pair, lax.axis_index("core"), axis=0)
    away = lax.dynamic_index_in_dim(pair, 1 - lax.axis_index("core"), axis=0)
    return jnp.concatenate([own, away], axis=0)


def halo(cells):
    width = cells.shape[-1]
    left_chip = lax.axis_index("x") == 0
    edge = jnp.where(left_chip, cells[:, :, 1, 63], cells[:, :, 0, 0])
    beside = swapped(edge, "x")

    def with_side(row):
        return jnp.concatenate(
            [cells[:, row].reshape(-1, width), beside[:, row], jnp.zeros((14, width), bf16)], axis=0
        )

    above = shifted(with_side(1), ROWS, 1)
    below = shifted(with_side(0), ROWS, -1)
    shape = (2, 1, 2, 64, width)
    rows = jnp.concatenate(
        [above[:256].reshape(shape), cells, below[:256].reshape(shape)], axis=1
    )
    beside = jnp.concatenate(
        [above[256:258, None], beside, below[256:258, None]], axis=1
    )
    none = jnp.zeros_like(beside)
    sides = jnp.stack([jnp.where(left_chip, none, beside), jnp.where(left_chip, beside, none)])
    return rows, sides


def adamw(weight, moment, second, grad, decay):
    new_mom = beta_first * moment + (1.0 - beta_first) * grad
    new_sec = beta_second * second + (1.0 - beta_second) * grad * grad
    corrected = new_mom / (1.0 - beta_first**STEP)
    spread = jnp.sqrt(new_sec / (1.0 - beta_second**STEP))
    return (
        new_mom,
        new_sec,
        weight - learn_rate * (corrected / (spread + epsilon) + decay * weight),
    )


def shards(
    features,
    skip_feat,
    labels,
    pixel_weight,
    valid_mask,
    conv_first,
    conv_first_mom,
    conv_first_sec,
    conv_second,
    conv_second_mom,
    conv_second_sec,
    up_conv,
    up_conv_mom,
    up_conv_sec,
    conv_merge,
    conv_merge_mom,
    conv_merge_sec,
    head_weight,
    head_mom,
    head_sec,
    biases,
    biases_mom,
    biases_sec,
):
    core = lax.axis_index("core")
    member = (lax.axis_index("zl") * 2 + lax.axis_index("y")) * 2 + core
    zh, x = lax.axis_index("zh"), lax.axis_index("x")

    channel = jnp.arange(8)[:, None] + 8 * jnp.arange(C1 // 8)[None, :]
    sorting = (jnp.arange(C1)[:, None, None] == channel[None]).astype(bf16)
    r1 = conv_first.shape[0] // C1
    r2 = conv_second.shape[0] // C1
    even = r2 % 8 == 0
    count_own = jnp.sum(valid_mask).astype(bf16)
    low_one = jnp.einsum("rc,cqm->qrm", conv_first.astype(bf16).reshape(r1, C1), sorting)
    low_two = conv_second.astype(bf16)
    block = features.reshape(1, -1, 128)
    bundle = [jnp.full((8, 16, 128), count_own, bf16), low_one]
    kernel_rows = 16 + r1
    if even:
        low_two = low_two.reshape(r2 // 8, 8, C1 // 128, 128).transpose(1, 0, 2, 3)
        bundle.append(low_two.reshape(8, r2, 128))
        kernel_rows += r2
    bundle.append(jnp.broadcast_to(block, (8,) + block.shape[1:]))
    bundle, conv_merge, up_conv, skip_feat, labels, pixel_weight = lax.optimization_barrier(
        (jnp.concatenate(bundle, axis=1), conv_merge, up_conv, skip_feat, labels, pixel_weight)
    )

    bundle = lax.all_to_all(bundle, MEMBERS, 0, 0, tiled=True)
    r3 = conv_merge.shape[0] // C0
    ru = up_conv.shape[0] // C0
    zhs = size_of("zh")
    me = jnp.stack([lax.axis_index(axis) for axis in AXES]).astype(jnp.int32)
    low_chip = jnp.concatenate(
        [conv_merge.astype(bf16).reshape(r3, C0), up_conv.astype(bf16).reshape(ru, C0)], axis=0
    )
    low_chip = in_order_back(low_chip.reshape(r3 + ru, 2, HALF).transpose(1, 0, 2))
    low_chip = jnp.concatenate([low_chip[:1], swapped(low_chip[1:], "core")], axis=0)
    merge_pieces, up_pieces = chunk_list(r3, ru)
    if zhs == 2:
        low_chip = joined_on(low_chip, "zh")
    skip = skip_feat.reshape(2, 2, 32, 2, C0).swapaxes(2, 3)
    skip_cells = pair_gather(skip, "core", 3)
    marks = pair_gather(jnp.stack([labels, valid_mask * pixel_weight]), "core", 3)
    marks = marks.reshape(2, 2, 2, 64, 2).swapaxes(3, 4)
    bundle, low_chip, skip_cells = lax.optimization_barrier((bundle, low_chip, skip_cells))

    feat = bundle[:, kernel_rows:].reshape((4, 2) + features.shape[:1] + features.shape[2:])
    feat = feat.transpose(2, 0, 1, 3, 4)
    feat = feat.reshape(feat.shape[0], 4, 2 * feat.shape[3], C0)
    kernels = bundle[:, :kernel_rows].reshape(-1, 128)
    if zhs == 2:
        edge = jnp.where(zh == 0, feat[:, -2:], feat[:, :2])
        got = swapped(jnp.concatenate([kernels, edge.reshape(-1, 128)], axis=0), "zh")
        low_chip = joined_on(low_chip, "x")
        cut = (r3 + ru) // 2
        first, second = low_chip[:, :cut], low_chip[:, cut:]
        first, second = (first, swapped(first, "y")), (second, swapped(second, "zl"))
        feat, kernels, got = lax.optimization_barrier((feat, kernels, got))
        edge = got[8 * kernel_rows :].reshape(edge.shape)
        none = jnp.zeros_like(edge)
        feat = jnp.concatenate(
            [jnp.where(zh == 0, none, edge), feat, jnp.where(zh == 0, edge, none)], axis=1
        )
        kernels = in_order(kernels, got[: 8 * kernel_rows], "zh", 0)
    else:
        feat = padded(feat, "zh", 1, 2)
        kernels = lax.all_gather(kernels, "zh", axis=0, tiled=True)

    kernels = kernels.reshape(8 * zhs, kernel_rows, 128)
    lead = kernels[:, : 16 + r1].reshape(-1, 128)
    edge = jnp.where(x == 0, feat[:, :, -2:], feat[:, :, :2])
    got = swapped(jnp.concatenate([lead, edge.reshape(-1, 128)], axis=0), "x")
    if zhs == 2:
        got, first, second = lax.optimization_barrier((got, first, second))
    edge = got[lead.shape[0] :].reshape(edge.shape)
    none = jnp.zeros_like(edge)
    feat = jnp.concatenate(
        [jnp.where(x == 0, none, edge), feat, jnp.where(x == 0, edge, none)], axis=2
    )

    def ordered(own, other):
        both = jnp.stack([own, other]).reshape(2, zhs, 2, 2, 2, -1, 128)
        return jnp.where(x == 0, both, both[::-1]).transpose(1, 2, 3, 0, 4, 5, 6)

    lead = ordered(lead, got[: lead.shape[0]])
    count_all = jnp.sum(lead[..., 0, 0].astype(f32))
    kernel_one = lead[..., 16:, :].reshape(3, 3, C0, C1 // 8)
    if even:
        kernel_two = kernels[:, 16 + r1 :].reshape(-1, 128)
        kernel_two = ordered(kernel_two, swapped(kernel_two, "x"))
    else:
        low_two = lax.all_gather(low_two.reshape(r2, C1), AXES, axis=0, tiled=True)
        low_two = low_two.reshape(-1, 8, C1)
        kernel_two = lax.dynamic_index_in_dim(low_two, member, axis=1, keepdims=False)
    kernel_two = kernel_two.reshape(3, 3, C1 // 8, C1)
    if zhs == 2:
        first, second = jnp.concatenate(first, axis=0), jnp.concatenate(second, axis=0)
        first = (first, swapped(first, "zl"))
        second = (second, swapped(second, "y"))
    else:
        first = second = jnp.zeros((), bf16)

    bias_one = lax.dynamic_index_in_dim(
        biases[:C1].reshape(C1 // 8, 8), member, axis=1, keepdims=False
    )
    bias_two = biases[C1 : 2 * C1]
    bias_up = lax.dynamic_slice_in_dim(biases[2 * C1 : 2 * C1 + C0], core * (C0 // 2), C0 // 2)
    bias_three = lax.dynamic_slice_in_dim(
        biases[2 * C1 + C0 : 2 * C1 + 2 * C0], core * (C0 // 2), C0 // 2
    )
    bias_head = biases[2 * C1 + 2 * C0 :]
    head_low = lax.dynamic_slice_in_dim(
        head_weight.astype(bf16), core * (C0 // 2), C0 // 2, axis=0
    )

    pre_one = convolve(feat, kernel_one) + bias_one
    high, wide = pre_one.shape[1], pre_one.shape[2]
    row_at = jnp.arange(high)
    col_at = jnp.arange(wide)
    row_in = ((row_at > 0) | (zh > 0)) & ((row_at < high - 1) | (zh < size_of("zh") - 1))
    col_in = ((col_at > 0) | (x > 0)) & ((col_at < wide - 1) | (x < size_of("x") - 1))
    inside = (row_in[:, None] & col_in[None, :])[None, :, :, None]
    act_one = jnp.where(inside, jax.nn.gelu(pre_one), 0.0).astype(bf16)
    part_two = convolve(act_one, kernel_two)
    feat_shifts, act_shifts = by_shift(feat[:, 1:-1, 1:-1]), by_shift(act_one)
    skip, skip_sides = halo(skip_cells)
    part_two, first, second, skip, skip_sides, marks = lax.optimization_barrier(
        (part_two, first, second, skip, skip_sides, marks)
    )
    if zhs == 2:
        kernel_merge, kernel_up = in_place(me, first + second, merge_pieces, up_pieces)
    else:
        low_chip = jnp.where(core == 0, low_chip, low_chip[::-1])
        low_chip = lax.all_gather(low_chip, CHIPS, axis=0, tiled=True)
        kernel_merge = low_chip[:, :r3].reshape(-1, HALF)
        kernel_up = low_chip[:, r3:].reshape(-1, HALF)
    pre_two = group_scatter(part_two) + bias_two
    act_two = jax.nn.gelu(pre_two).astype(bf16)
    act_two, kernel_merge, kernel_up = lax.optimization_barrier((act_two, kernel_merge, kernel_up))

    act_own = act_two[:, 0]
    ups, act_chip = up_on_chip(me, act_own, swapped(act_own, "core"), kernel_up, bias_up[None])
    ups, sides = halo(ups)
    head_wide = jnp.pad(head_low, ((0, 0), (0, 128 - CLASSES)))
    pre_three, logits, planes = merge_on_chip(
        me,
        ups,
        swapped(ups, "core"),
        sides,
        swapped(sides, "core"),
        skip,
        skip_sides,
        kernel_merge,
        bias_three[None],
        head_wide,
    )
    logits = (logits + swapped(logits, "core"))[:, :CLASSES] + bias_head
    logits = logits.reshape(2, 2, 2, 64, CLASSES)
    pre_three = pre_three.reshape(2, 2, 2, 64, HALF)
    act_three = jax.nn.gelu(pre_three).astype(bf16)

    scaled = marks[1].astype(f32)
    onehot = (marks[0][..., None] == jnp.arange(CLASSES, dtype=jnp.int32)).astype(f32)
    log_probs = jax.nn.log_softmax(logits, axis=-1)
    loss_part = -0.5 * jnp.sum(scaled * jnp.sum(onehot * log_probs, axis=-1))
    grad_logits = ((jnp.exp(log_probs) - onehot) * (scaled / count_all)[..., None]).astype(bf16)

    head_part = jnp.einsum("iabwc,iabwk->ck", act_three, grad_logits, preferred_element_type=f32)
    grad_act_three = jnp.einsum(
        "iabwk,ck->iabwc", grad_logits, head_low, preferred_element_type=f32
    )
    grad_pre_three = gelu_back(pre_three, grad_act_three).astype(bf16)
    border, border_sides = halo(grad_pre_three)
    own_grad, away_grad = ups_grad_on_chip(me, border, border_sides, kernel_merge)
    grad_upper = (own_grad + swapped(away_grad, "core").astype(f32)).astype(bf16)
    grad_upper = grad_upper.reshape(2, 2, 2, 64, HALF)
    grad_act_two = jnp.einsum(
        "iabwo,abco->iwc",
        grad_upper,
        kernel_up.reshape(2, 2, C1, HALF),
        preferred_element_type=f32,
    )[:, None]
    grad_act_two = pair_scatter(grad_act_two, "core", 2, f32)
    grad_pre_two = gelu_back(pre_two, grad_act_two).astype(bf16)

    grad_two = group_gather(grad_pre_two)
    if zhs == 2:
        grad_two, inner, sides = second_back_on_chip(grad_two, kernel_two.reshape(-1, C1))
        grad_two, inner, sides, planes = lax.optimization_barrier((grad_two, inner, sides, planes))
        chip_parts = chip_grads(
            me, planes, grad_pre_three.reshape(512, HALF), act_chip, grad_upper, r3, ru
        )
        chip_parts, act_shifts = lax.optimization_barrier((chip_parts, act_shifts))
        second_grad = second_grad_on_chip(me, act_shifts, grad_two, r2, 16 * zhs)
        row = jnp.where(zh == 0, inner[:, 5:], inner[:, :1])
        column = jnp.where(x == 0, sides[1], sides[0])
        corner = jnp.where(zh == 0, column[:, 5:], column[:, :1])[:, :, None]
        column = swapped(column[:, 1:5, None], "x")
        corner = lax.ppermute(corner, ("zh", "x"), [(i, 3 - i) for i in range(4)])
        row = swapped(row, "zh")
        row, column, corner, chip_parts = lax.optimization_barrier(
            (row, column, corner, chip_parts)
        )
        at_row = jnp.arange(4)[None, :, None, None] == jnp.where(zh == 0, 3, 0)
        at_column = jnp.arange(64)[None, None, :, None] == jnp.where(x == 0, 63, 0)
        core_part = (
            inner[:, 1:5]
            + jnp.where(at_row, row, 0.0)
            + jnp.where(at_column, column, 0.0)
            + jnp.where(at_row & at_column, corner, 0.0)
        )
    else:
        cells = planes.reshape(2, 4, 4, 64, 2 * C0)
        chip_parts = (
            jnp.concatenate(
                [
                    jnp.einsum(
                        "iabwc,iabwo->co",
                        cells[:, high : high + 2, wide : wide + 2],
                        grad_pre_three,
                        preferred_element_type=f32,
                    )
                    for high in range(3)
                    for wide in range(3)
                ]
            ).astype(bf16),
            jnp.einsum(
                "iwc,iabwo->abco", act_chip, grad_upper, preferred_element_type=f32
            ).astype(bf16),
        )
        images, width = grad_two.shape[1], grad_two.shape[3]
        grad_two = grad_two.reshape(4, 2, images, width, C1).transpose(2, 0, 1, 3, 4)
        grad_two = grad_two.reshape(images, 4, 2 * width, C1)
        second_grad = kernel_grad(act_one, grad_two)
        spill = convolve(grad_two, turned(kernel_two), 2)
        inner = spill[:, 1:-1]
        inner = inner.at[:, :1].add(shifted(spill[:, -1:], "zh", 1))
        inner = inner.at[:, -1:].add(shifted(spill[:, :1], "zh", -1))
        core_part = inner[:, :, 1:-1]
        core_part = core_part.at[:, :, :1].add(shifted(inner[:, :, -1:], "x", 1))
        core_part = core_part.at[:, :, -1:].add(shifted(inner[:, :, :1], "x", -1))
    grad_pre_one = gelu_back(pre_one[:, 1:-1, 1:-1], core_part).astype(bf16)
    tiled = zhs == 2
    if tiled:
        grad_pre_one, second_grad = lax.optimization_barrier((grad_pre_one, second_grad))
        first_grad = first_grad_on_chip(me, feat_shifts, grad_pre_one, r1, 16 * zhs)
        def shard_sum(own, got):
            return (own.astype(f32) + got.astype(f32)).reshape(2, 8, -1, 128)

        def leave(part):
            away = lax.dynamic_index_in_dim(part, 1 - zh, axis=0, keepdims=False).astype(bf16)
            own = lax.dynamic_index_in_dim(part, zh, axis=0, keepdims=False)
            return own, away, swapped(away, "zh")

        chip_parts = sent(chip_parts, "zl", "y")
        chip_parts = sent(added(chip_parts), "y", "zl")
        second_stays = after(chip_parts[0], second_grad[0])[1]
        two_own, two_away, two_got = leave(shard_sum(second_stays, swapped(second_grad[1], "x")))
        two_away, first_stays = after(two_away, first_grad[0])
        one_own, one_away, one_got = leave(shard_sum(first_stays, swapped(first_grad[1], "x")))
        one_away, chip_parts = after(one_away, chip_parts)
        chip_parts = added(chip_parts)
        chip_stays, chip_goes = (
            jnp.concatenate([chip_parts[i], chip_parts[i + 2]], axis=1) for i in range(2)
        )
        chip_got = swapped(chip_goes, "x")
        chip_goes, two_own = after(chip_goes, two_own)
        part_two = two_own + two_got.astype(f32)
        two_low, chip_stays, one_own = after(part_two.astype(bf16), chip_stays, one_own)
        chip_parts = chip_stays.astype(f32) + chip_got.astype(f32)
        chip_goes = chip_parts[2:].astype(bf16)
        part_chip = chip_parts[:2] + swapped(chip_goes, "zh").astype(f32)
        chip_goes, one_own = after(chip_goes, one_own)
        part_one = one_own + one_got.astype(f32)
        one_low = part_one.astype(bf16)
        sq_kernels = jnp.sum(part_one * part_one) + jnp.sum(part_two * part_two)
        part = jnp.concatenate([one_low, two_low], axis=1)
        part = lax.all_to_all(part, MEMBERS, 0, 0, tiled=True)
        part_one, part_two = part[:, :r1], part[:, r1:]
        half = r3 // 2
        part_chip = jnp.concatenate(
            [
                part_chip[:, :half],
                part_chip[:, half + ru // 2 : r3 + ru // 2],
                part_chip[:, half : half + ru // 2],
                part_chip[:, r3 + ru // 2 :],
            ],
            axis=1,
        )
        part_two = part_two.reshape(8, r2 // 8, C1 // 128, 128).transpose(1, 0, 2, 3)
        share_two = part_two.reshape(-1).astype(f32)
    else:
        first_grad = kernel_grad(feat[:, 1:-1, 1:-1], grad_pre_one)
        mine = jnp.arange(8)[None, :, None] == member
        part_two = jnp.where(mine, second_grad.astype(bf16)[:, None], 0)
        share_two = lax.psum_scatter(
            part_two.reshape(-1, C1), AXES, scatter_dimension=0, tiled=True
        ).reshape(-1).astype(f32)
        part_one = far_scatter(first_grad)
        sq_kernels = jnp.sum(share_two * share_two) + jnp.sum(part_one * part_one)
        part_one = lax.all_to_all(part_one.astype(bf16), MEMBERS, 0, 0, tiled=True)
        part_chip = jnp.concatenate(
            [last_sum(chip_parts[0]), last_sum(chip_parts[1])], axis=1
        )
    share_one = jnp.einsum("qrm,cqm->rc", part_one, sorting, preferred_element_type=f32).reshape(-1)
    sq_chip = jnp.sum(part_chip * part_chip)
    part_chip = part_chip.astype(bf16)
    part_chip = in_order(part_chip[0], swapped(part_chip[1], "core"), "core", 1).astype(f32)
    share_merge = part_chip[:r3].reshape(-1)
    share_up = part_chip[r3:].reshape(-1)
    share_sq = sq_kernels + sq_chip
    spread_one = (
        jnp.where(jnp.arange(8)[None, :] == member, column_sum(grad_pre_one)[:, None], 0.0)
    ).reshape(-1)

    def half_of(values):
        shape = (2 * values.shape[0],) + values.shape[1:]
        return lax.dynamic_update_slice_in_dim(
            jnp.zeros(shape, f32), values, core * values.shape[0], axis=0
        )

    packed = jnp.concatenate(
        [
            spread_one,
            column_sum(grad_pre_two),
            half_of(column_sum(grad_upper)),
            half_of(column_sum(grad_pre_three)),
            0.5 * column_sum(grad_logits),
            half_of(head_part).reshape(-1),
            share_sq[None],
            loss_part[None],
        ]
    )
    packed = total(packed, ("core", "x", "y"))
    packed, share_one, share_two = lax.optimization_barrier((packed, share_one, share_two))
    packed = total(packed, ("zl", "zh"))
    bias_total = packed[: biases.shape[0]]
    head_total = packed[biases.shape[0] : -2].reshape(head_weight.shape)
    sq_total, loss_total = packed[-2], packed[-1]
    grad_norm = jnp.sqrt(sq_total + jnp.sum(jnp.square(packed[:-2])))
    factor = clip_norm / jnp.maximum(grad_norm, clip_norm)
    outs = ()
    for weight, moment, second, grad, decay in (
        (conv_first, conv_first_mom, conv_first_sec, share_one, weight_decay),
        (conv_second, conv_second_mom, conv_second_sec, share_two, weight_decay),
        (up_conv, up_conv_mom, up_conv_sec, share_up, weight_decay),
        (conv_merge, conv_merge_mom, conv_merge_sec, share_merge, weight_decay),
        (head_weight, head_mom, head_sec, head_total, weight_decay),
        (biases, biases_mom, biases_sec, bias_total, 0.0),
    ):
        outs += adamw(weight, moment, second, grad * factor, decay)
    return outs + (loss_total, count_all, grad_norm)


def solution(mesh):
    rows, cols = mesh.shape["rows"], mesh.shape["cols"]
    split = Mesh(mesh.devices.reshape(rows // 4, 2, 2, cols // 2, 2), AXES)
    image = P(None, ROWS, ("x", "core"))
    flat = P(AXES)
    return jax.shard_map(
        shards,
        mesh=split,
        in_specs=(image,) * 5 + (flat,) * 12 + (P(),) * 6,
        out_specs=(flat,) * 12 + (P(),) * 9,
        check_vma=False,
    )
```

```python
import math

import jax
import jax.numpy as jnp
from jax import lax
from jax.experimental import pallas as pl
from jax.experimental.pallas import tpu as pltpu
from jax.sharding import Mesh
from jax.sharding import PartitionSpec as P

C0 = 512
C1 = 1024
CLASSES = 2
STEP = 10

clip_norm = 0.05
learn_rate = 0.02
beta_first = 0.9
beta_second = 0.999
epsilon = 1e-08
weight_decay = 0.1

AXES = ("zh", "zl", "y", "x", "core")
MEMBERS = ("zl", "y", "core")
CHIPS = ("zh", "zl", "y", "x")
ROWS = ("zh", "zl", "y")
bf16 = jnp.bfloat16
f32 = jnp.float32


def size_of(axis):
    return lax.axis_size(axis)


def shifted(values, axis, step):
    count = size_of(axis)
    return lax.ppermute(
        values, axis, [(i, i + step) for i in range(count) if 0 <= i + step < count]
    )


def swapped(values, axis):
    return lax.ppermute(values, axis, [(0, 1), (1, 0)])


def padded(cells, axis, dim, width):
    head = lax.slice_in_dim(cells, 0, width, axis=dim)
    tail = lax.slice_in_dim(cells, cells.shape[dim] - width, cells.shape[dim], axis=dim)
    return jnp.concatenate(
        [shifted(tail, axis, 1), cells, shifted(head, axis, -1)], axis=dim
    )


def in_order(own, other, axis, dim):
    first = lax.axis_index(axis) == 0
    return jnp.concatenate(
        [jnp.where(first, own, other), jnp.where(first, other, own)], axis=dim
    )


def pair_gather(own, axis, dim):
    return in_order(own, swapped(own, axis), axis, dim)


def pair_half(values, axis, dim, index):
    width = values.shape[dim] // 2
    return lax.dynamic_slice_in_dim(values, index * width, width, axis=dim)


def pair_scatter(values, axis, dim, kind):
    me = lax.axis_index(axis)
    away = pair_half(values, axis, dim, 1 - me).astype(kind)
    return pair_half(values, axis, dim, me).astype(f32) + swapped(away, axis).astype(f32)


def total(values, axes=("core", "x", "y", "zl", "zh")):
    for axis in axes:
        if size_of(axis) == 2:
            values = values + swapped(values, axis)
        else:
            values = lax.psum(values, axis)
    return values


def convolve(values, kernel, pad=0):
    return lax.conv_general_dilated(
        values,
        kernel,
        (1, 1),
        ((pad, pad), (pad, pad)),
        dimension_numbers=("NHWC", "HWIO", "NHWC"),
        preferred_element_type=f32,
    )


def kernel_grad(cells, grad):
    rows_in, cols_in = (grad.shape[1], grad.shape[2])
    terms = [
        jnp.einsum(
            "nhwc,nhwo->co",
            cells[:, shift_h : shift_h + rows_in, shift_w : shift_w + cols_in],
            grad,
            preferred_element_type=f32,
        )
        for shift_h in range(3)
        for shift_w in range(3)
    ]
    return jnp.concatenate(terms, axis=0)


def turned(kernel):
    return jnp.swapaxes(kernel[::-1, ::-1], 2, 3)


def gelu_back(pre_act, upstream):
    return jax.vjp(jax.nn.gelu, pre_act)[1](upstream)[0]


def column_sum(values):
    return jnp.sum(values, axis=tuple(range(values.ndim - 1)), dtype=f32)


def group_gather(block):
    return lax.all_to_all(
        jnp.broadcast_to(block[None], (8,) + block.shape), MEMBERS, 0, 0, tiled=True
    )


def group_scatter(partial):
    n, _, w2, c = partial.shape
    sent = partial.astype(bf16).reshape(n, 4, 2, w2 // 2, c).transpose(1, 2, 0, 3, 4)
    got = lax.all_to_all(sent.reshape(8, n, w2 // 2, c), MEMBERS, 0, 0, tiled=True)
    return jnp.sum(got.astype(f32), axis=0)[:, None]


def over_zh(part):
    if size_of("zh") == 2:
        return pair_gather(part[None], "zh", 0)
    return lax.all_gather(part, "zh", axis=0)


def over_x(part):
    part = pair_gather(part[:, None], "x", 1)
    zh, _, _, r, o = part.shape
    return part.reshape(zh, 2, 2, 2, 2, r, o).transpose(0, 2, 3, 1, 4, 5, 6)


def far_scatter(grad, kind=bf16):
    zh = size_of("zh")
    o = grad.shape[1]
    r = grad.shape[0] // (16 * zh)
    split = grad.reshape(zh, 2, 2, 2, 2, r, o).transpose(3, 0, 1, 2, 4, 5, 6)
    split = pair_scatter(split, "x", 0, kind)[0]
    if zh == 2:
        split = pair_scatter(split, "zh", 0, kind)[0]
    else:
        split = lax.psum_scatter(split, "zh", scatter_dimension=0)
    return split.reshape(8, r, o)


HALF = C0 // 2


def joined_on(values, axis):
    return jnp.concatenate([values, swapped(values, axis)], axis=0)


def sent(parts, first_axis, second_axis):
    if len(parts) == 1:
        return parts
    return parts[0], swapped(parts[1], first_axis), parts[2], swapped(parts[3], second_axis)


def added(parts):
    out = ()
    for own, got in (parts[:2], parts[2:]):
        half = own.shape[0] // 2
        for v, w in ((own[:half], got[:half]), (own[half:], got[half:])):
            out += ((v.astype(f32) + w.astype(f32)).astype(bf16),)
    return out


def after(earlier, *parts):
    own = [part[::2] if isinstance(part, tuple) else (part,) for part in parts]
    earlier, own = lax.optimization_barrier((earlier, own))
    out = [earlier]
    for part, kept in zip(parts, own):
        if isinstance(part, tuple):
            out.append((kept[0], part[1], kept[1], part[3]))
        else:
            out.append(kept[0])
    return out


def place(chunk, me, first):
    bits = [me[i] if not (chunk >> (4 - i)) & 1 else 1 - me[i] for i in range(5)]
    zh, zl, y, x, core = bits
    high, low = (zl, y) if first == "y" else (y, zl)
    return high * 16 + low * 8 + x * 4 + zh * 2 + core


def chunk_list(r3, ru):
    cut = (r3 + ru) // 2
    merge, up = [], []
    for chunk in range(32):
        merge.append((0, (chunk, "y"), 0, cut, r3 * chunk))
        merge.append((2, (chunk, "zl"), 0, r3 - cut, r3 * chunk + cut))
        up.append((2, (chunk, "zl"), r3 - cut, ru, ru * chunk))
    return merge, up


def in_place(me, sources, merge_pieces, up_pieces):
    lists = (merge_pieces, up_pieces)
    count = len(merge_pieces) + len(up_pieces)

    def body(me_ref, *rest):
        source_refs, targets, sems = rest[:4], rest[4:6], rest[6]
        waits = []
        for pieces, target in zip(lists, targets):
            for which, spot, start, rows, to in pieces:
                sem = sems.at[len(waits)]
                here = target.at[pl.ds(to, rows), :]
                at = place(spot[0], me_ref, spot[1])
                for side in range(2):
                    inside = at - 16 * side

                    @pl.when((inside >= 0) & (inside < 16))
                    def _(source=source_refs[which + side], inside=inside, start=start, rows=rows, here=here, sem=sem):
                        there = source.at[inside, pl.ds(start, rows), :]
                        pltpu.make_async_copy(there, here, sem).start()

                there = source_refs[which].at[0, pl.ds(start, rows), :]
                waits.append(pltpu.make_async_copy(there, here, sem))
        for copy in waits:
            copy.wait()

    rows = [sum(piece[3] for piece in pieces) for pieces in lists]
    return on_chip(
        body,
        (me, *sources),
        tuple(jax.ShapeDtypeStruct((n, HALF), bf16) for n in rows),
        [pltpu.SemaphoreType.DMA((count,))],
        ("saaaa", "vv"),
        0,
    )


def on_chip(body, ins, outs, scratch, spaces, flops, aliases=()):
    kinds = {"v": pltpu.VMEM, "s": pltpu.SMEM, "a": pl.ANY}
    held = [v for v, k in zip(list(ins) + list(outs), spaces[0] + spaces[1]) if k == "v"]
    held += [v for v in scratch if len(v.shape) > 1]
    room = sum(math.prod(v.shape) * jnp.dtype(v.dtype).itemsize for v in held)
    limit = 58 * 1024 * 1024 if "a" in spaces[1] else int(1.25 * room) + 6 * 1024 * 1024
    return pl.pallas_call(
        body,
        out_shape=outs,
        in_specs=[pl.BlockSpec(memory_space=kinds[k]) for k in spaces[0]],
        out_specs=[pl.BlockSpec(memory_space=kinds[k]) for k in spaces[1]],
        scratch_shapes=scratch,
        input_output_aliases=dict(aliases),
        compiler_params=pltpu.CompilerParams(vmem_limit_bytes=limit),
        cost_estimate=pl.CostEstimate(flops=0, bytes_accessed=0, transcendentals=0),
    )(*ins)


def up_on_chip(me, own, other, kernel, bias):
    def body(me_ref, own_ref, other_ref, kernel_ref, bias_ref, ups_ref, act_ref):
        core = me_ref[4]
        mine = pl.ds(pl.multiple_of(core * 32, 32), 32)
        yours = pl.ds(pl.multiple_of((1 - core) * 32, 32), 32)
        for image in range(2):
            act_ref[image, mine, :] = own_ref[image]
            act_ref[image, yours, :] = other_ref[image]
        values = act_ref[...].reshape(128, C1)
        for tap in range(4):
            got = jnp.dot(
                values, kernel_ref[tap * C1 : (tap + 1) * C1, :], preferred_element_type=f32
            )
            got = (got + bias_ref[...]).astype(bf16).reshape(2, 64, HALF)
            for image in range(2):
                ups_ref[image, tap // 2, tap % 2] = got[image]

    return on_chip(
        body,
        (me, own, other, kernel, bias),
        (
            jax.ShapeDtypeStruct((2, 2, 2, 64, HALF), bf16),
            jax.ShapeDtypeStruct((2, 64, C1), bf16),
        ),
        [],
        ("svvvv", "vv"),
        2 * 128 * C1 * 4 * HALF,
    )


def planes_in(target, lanes, rows_ref, sides_ref):
    line = lax.broadcasted_iota(jnp.int32, (64, 1), 0)
    for image in range(2):
        for row in range(4):
            even = rows_ref[image, row, 0]
            odd = rows_ref[image, row, 1]
            target[image, row, 1, :, lanes] = even
            target[image, row, 2, :, lanes] = odd
            left = sides_ref[0, image, row : row + 1, :].astype(f32)
            right = sides_ref[1, image, row : row + 1, :].astype(f32)
            moved = pltpu.roll(odd.astype(f32), 1, 0)
            target[image, row, 0, :, lanes] = jnp.where(line == 0, left, moved).astype(bf16)
            moved = pltpu.roll(even.astype(f32), 63, 0)
            target[image, row, 3, :, lanes] = jnp.where(line == 63, right, moved).astype(bf16)


def tapped(planes, image, tap, lanes):
    high, wide = tap // 3, tap % 3
    cells = planes[image, high : high + 2, wide : wide + 2, :, lanes]
    return cells.reshape(256, cells.shape[-1])


def merge_on_chip(me, own, other, own_sides, other_sides, skip, skip_sides, kernel, bias, head):
    def body(me_ref, own_ref, other_ref, own_sides_ref, other_sides_ref, skip_ref, skip_sides_ref, kernel_ref, bias_ref, head_ref, pre_ref, logits_ref, planes_ref):
        low, high = slice(0, HALF), slice(HALF, C0)

        @pl.when(me_ref[4] == 0)
        def _():
            planes_in(planes_ref, low, own_ref, own_sides_ref)
            planes_in(planes_ref, high, other_ref, other_sides_ref)

        @pl.when(me_ref[4] == 1)
        def _():
            planes_in(planes_ref, high, own_ref, own_sides_ref)
            planes_in(planes_ref, low, other_ref, other_sides_ref)

        planes_in(planes_ref, slice(C0, 2 * C0), skip_ref, skip_sides_ref)
        for image in range(2):
            total = jnp.broadcast_to(bias_ref[...], (256, HALF))
            for tap in range(9):
                total = total + jnp.dot(
                    tapped(planes_ref, image, tap, slice(0, 2 * C0)),
                    kernel_ref[tap * 2 * C0 : (tap + 1) * 2 * C0, :],
                    preferred_element_type=f32,
                )
            pre_ref[image * 256 : (image + 1) * 256, :] = total
        act = jax.nn.gelu(pre_ref[...]).astype(bf16)
        logits_ref[...] = jnp.dot(act, head_ref[...], preferred_element_type=f32)

    return on_chip(
        body,
        (me, own, other, own_sides, other_sides, skip, skip_sides, kernel, bias, head),
        (
            jax.ShapeDtypeStruct((512, HALF), f32),
            jax.ShapeDtypeStruct((512, 128), f32),
            jax.ShapeDtypeStruct((2, 4, 4, 64, 2 * C0), bf16),
        ),
        [],
        ("svvvvvvvvv", "vvv"),
        2 * 512 * 18 * C0 * HALF,
    )


def ups_grad_on_chip(me, rows, sides, kernel):
    def body(me_ref, rows_ref, sides_ref, kernel_ref, own_ref, away_ref, planes):
        core = me_ref[4]
        planes_in(planes, slice(0, HALF), rows_ref, sides_ref)
        for image in range(2):
            lines = slice(image * 256, (image + 1) * 256)
            for target, half in ((own_ref, core), (away_ref, 1 - core)):
                total = jnp.zeros((256, HALF), f32)
                for tap in range(9):
                    start = pl.multiple_of((8 - tap) * 2 * C0 + half * HALF, HALF)
                    total = total + lax.dot_general(
                        tapped(planes, image, tap, slice(0, HALF)),
                        kernel_ref[pl.ds(start, HALF), :],
                        (((1,), (1,)), ((), ())),
                        preferred_element_type=f32,
                    )
                target[lines, :] = total.astype(target.dtype)

    return on_chip(
        body,
        (me, rows, sides, kernel),
        (jax.ShapeDtypeStruct((512, HALF), f32), jax.ShapeDtypeStruct((512, HALF), bf16)),
        [pltpu.VMEM((2, 4, 4, 64, HALF), bf16)],
        ("svvv", "vv"),
        2 * 512 * 9 * C0 * HALF,
    )


def chunk_writes(me_ref, pieces, whole, targets, sems):
    waits = []
    for i, (pair, spot, start, rows, to) in enumerate(pieces):
        here = whole.at[pl.ds(start, rows), :]
        at = place(spot[0], me_ref, spot[1])
        for side in range(2):
            inside = at - 16 * side

            @pl.when((inside >= 0) & (inside < 16))
            def _(here=here, target=targets[pair + side], inside=inside, rows=rows, to=to, i=i):
                there = target.at[inside, pl.ds(to, rows), :]
                pltpu.make_async_copy(here, there, sems.at[i]).start()

        there = targets[pair].at[0, pl.ds(to, rows), :]
        waits.append(pltpu.make_async_copy(here, there, sems.at[i]))
    for copy in waits:
        copy.wait()


def halves(rows, to):
    pieces = []
    for chunk in range(32):
        pieces.append((0, (chunk, "y"), rows * chunk, rows // 2, to))
        pieces.append((2, (chunk, "zl"), rows * chunk + rows // 2, rows // 2, to))
    return pieces


def merge_grads(me, planes, grad, r3, ru):
    pieces = halves(r3, 0)

    def body(me_ref, planes_ref, grad_ref, *rest):
        targets, whole, sems = rest[:4], rest[4], rest[5]
        for tap in range(9):
            total = jnp.zeros((2 * C0, HALF), f32)
            for image in range(2):
                total = total + lax.dot_general(
                    tapped(planes_ref, image, tap, slice(0, 2 * C0)),
                    grad_ref[image * 256 : (image + 1) * 256, :],
                    (((0,), (0,)), ((), ())),
                    preferred_element_type=f32,
                )
            whole[tap * 2 * C0 : (tap + 1) * 2 * C0, :] = total.astype(bf16)
        chunk_writes(me_ref, pieces, whole, targets, sems)

    return on_chip(
        body,
        (me, planes, grad),
        (jax.ShapeDtypeStruct((16, (r3 + ru) // 2, HALF), bf16),) * 4,
        [pltpu.VMEM((18 * C0, HALF), bf16), pltpu.SemaphoreType.DMA((len(pieces),))],
        ("svv", "aaaa"),
        0,
    )


def up_grads(me, act, ups_grad, parts, r3, ru):
    pieces = halves(ru, r3 // 2)

    def body(me_ref, act_ref, ups_grad_ref, *rest):
        targets, whole, sems = rest[4:8], rest[8], rest[9]
        values = act_ref[...].reshape(128, C1)
        for tap in range(4):
            cells = ups_grad_ref[:, tap // 2, tap % 2].reshape(128, HALF)
            total = lax.dot_general(
                values, cells, (((0,), (0,)), ((), ())), preferred_element_type=f32
            )
            whole[tap * C1 : (tap + 1) * C1, :] = total.astype(bf16)
        chunk_writes(me_ref, pieces, whole, targets, sems)

    return on_chip(
        body,
        (me, act, ups_grad, *parts),
        (jax.ShapeDtypeStruct((16, (r3 + ru) // 2, HALF), bf16),) * 4,
        [pltpu.VMEM((4 * C1, HALF), bf16), pltpu.SemaphoreType.DMA((len(pieces),))],
        ("svvaaaa", "aaaa"),
        0,
        {3 + i: i for i in range(4)},
    )


def side_list(first_rows, rows, chunks):
    return [
        ((chunk >> 1) & 1, (chunk >> 2) * 2 + (chunk & 1), rows * chunk, rows, first_rows)
        for chunk in range(chunks)
    ]


def two_ways(pieces, me, stays, goes, source, sems):
    for i, (side, at, start, count, to) in enumerate(pieces):
        here = source.at[pl.ds(start, count), :]
        for target, wanted in ((stays, side), (goes, 1 - side)):

            @pl.when(me[3] == wanted)
            def _(here=here, target=target, at=at, to=to, count=count, i=i):
                there = target.at[at, pl.ds(to, count), :]
                pltpu.make_async_copy(here, there, sems.at[i]).start()

    for i, (side, at, start, count, to) in enumerate(pieces):
        here = source.at[pl.ds(start, count), :]
        pltpu.make_async_copy(here, stays.at[at, pl.ds(to, count), :], sems.at[i]).wait()


def second_grad_on_chip(me, cells, grad, rows, chunks):
    images, width, outs = cells.shape[1], cells.shape[4], grad.shape[3]
    tiles = outs // 128
    pieces = side_list(0, rows, chunks)

    def body(me_ref, cells_ref, grad_ref, stays_ref, goes_ref, wide, narrow, sems):
        upstream = grad_ref[...].reshape(images * 256, outs)
        for tap in range(9):
            values = cells_ref[tap % 3, :, tap // 3 : tap // 3 + 4].reshape(images * 256, width)
            got = lax.dot_general(
                values, upstream, (((0,), (0,)), ((), ())), preferred_element_type=f32
            )
            for tile in range(tiles):
                wide[:, tile, :] = got[:, tile * 128 : (tile + 1) * 128]
            narrow[tap * width * tiles : (tap + 1) * width * tiles, :] = (
                wide[...].reshape(width * tiles, 128).astype(bf16)
            )
        two_ways(pieces, me_ref, stays_ref, goes_ref, narrow, sems)

    return on_chip(
        body,
        (me, cells, grad),
        (jax.ShapeDtypeStruct((chunks // 2, rows, 128), bf16),) * 2,
        [
            pltpu.VMEM((width, tiles, 128), f32),
            pltpu.VMEM((9 * width * tiles, 128), bf16),
            pltpu.SemaphoreType.DMA((chunks,)),
        ],
        ("svv", "aa"),
        2 * images * 256 * 9 * width * outs,
    )


def first_grad_on_chip(me, cells, grad, rows, chunks):
    images, width, outs = cells.shape[1], cells.shape[4], grad.shape[3]
    pieces = side_list(0, rows, chunks)

    def body(me_ref, cells_ref, grad_ref, stays_ref, goes_ref, narrow, sems):
        upstream = grad_ref[...].reshape(images * 256, outs)
        for tap in range(9):
            values = cells_ref[tap % 3, :, tap // 3 : tap // 3 + 4].reshape(images * 256, width)
            got = lax.dot_general(
                values, upstream, (((0,), (0,)), ((), ())), preferred_element_type=f32
            )
            narrow[tap * width : (tap + 1) * width, :] = got.astype(bf16)
        two_ways(pieces, me_ref, stays_ref, goes_ref, narrow, sems)

    return on_chip(
        body,
        (me, cells, grad),
        (jax.ShapeDtypeStruct((chunks // 2, rows, 128), bf16),) * 2,
        [pltpu.VMEM((9 * width, 128), bf16), pltpu.SemaphoreType.DMA((chunks,))],
        ("svv", "aa"),
        2 * images * 256 * 9 * width * outs,
    )


def second_back_on_chip(grad, kernel):
    images = grad.shape[1]

    def body(grad_ref, kernel_ref, order_ref, inner_ref, sides_ref, parts):
        for member in range(8):
            row, core = member // 2, member % 2
            for image in range(images):
                order_ref[image, row, core * 32 : (core + 1) * 32] = grad_ref[member, image, 0]
        parts[...] = jnp.zeros(parts.shape, f32)
        for image in range(images):
            values = order_ref[image].reshape(256, C1)
            for tap in range(9):
                got = lax.dot_general(
                    values,
                    kernel_ref[tap * 128 : (tap + 1) * 128, :],
                    (((1,), (1,)), ((), ())),
                    preferred_element_type=f32,
                )
                high = tap // 3
                parts[tap % 3, image, high : high + 4] += got.reshape(4, 64, 128)
        line = lax.broadcasted_iota(jnp.int32, (64, 1), 0)
        for image in range(images):
            for row in range(6):
                before = pltpu.roll(parts[0, image, row], 63, 0)
                later = pltpu.roll(parts[2, image, row], 1, 0)
                inner_ref[image, row] = (
                    parts[1, image, row]
                    + jnp.where(line == 63, 0.0, before)
                    + jnp.where(line == 0, 0.0, later)
                )
                sides_ref[0, image, row : row + 1, :] = parts[0, image, row, 0:1, :]
                sides_ref[1, image, row : row + 1, :] = parts[2, image, row, 63:64, :]

    return on_chip(
        body,
        (grad, kernel),
        (
            jax.ShapeDtypeStruct((images, 4, 64, C1), bf16),
            jax.ShapeDtypeStruct((images, 6, 64, 128), f32),
            jax.ShapeDtypeStruct((2, images, 6, 128), f32),
        ),
        [pltpu.VMEM((3, images, 6, 64, 128), f32)],
        ("vv", "vvv"),
        0,
    )


def by_shift(cells):
    return jnp.stack([cells[:, :, shift : shift + 64] for shift in range(3)])


def last_sum(whole):
    whole = whole.reshape(8 * size_of("zh"), 2, -1, HALF)
    whole = lax.psum_scatter(whole, CHIPS, scatter_dimension=0)
    return in_order_back(whole).astype(f32)


def in_order_back(pair):
    own = lax.dynamic_index_in_dim(pair, lax.axis_index("core"), axis=0)
    away = lax.dynamic_index_in_dim(pair, 1 - lax.axis_index("core"), axis=0)
    return jnp.concatenate([own, away], axis=0)


def halo(cells):
    width = cells.shape[-1]
    left_chip = lax.axis_index("x") == 0
    edge = jnp.where(left_chip, cells[:, :, 1, 63], cells[:, :, 0, 0])
    beside = swapped(edge, "x")

    def with_side(row):
        return jnp.concatenate(
            [cells[:, row].reshape(-1, width), beside[:, row], jnp.zeros((14, width), bf16)], axis=0
        )

    above = shifted(with_side(1), ROWS, 1)
    below = shifted(with_side(0), ROWS, -1)
    shape = (2, 1, 2, 64, width)
    rows = jnp.concatenate(
        [above[:256].reshape(shape), cells, below[:256].reshape(shape)], axis=1
    )
    beside = jnp.concatenate(
        [above[256:258, None], beside, below[256:258, None]], axis=1
    )
    none = jnp.zeros_like(beside)
    sides = jnp.stack([jnp.where(left_chip, none, beside), jnp.where(left_chip, beside, none)])
    return rows, sides


def adamw(weight, moment, second, grad, decay):
    new_mom = beta_first * moment + (1.0 - beta_first) * grad
    new_sec = beta_second * second + (1.0 - beta_second) * grad * grad
    corrected = new_mom / (1.0 - beta_first**STEP)
    spread = jnp.sqrt(new_sec / (1.0 - beta_second**STEP))
    return (
        new_mom,
        new_sec,
        weight - learn_rate * (corrected / (spread + epsilon) + decay * weight),
    )


def shards(
    features,
    skip_feat,
    labels,
    pixel_weight,
    valid_mask,
    conv_first,
    conv_first_mom,
    conv_first_sec,
    conv_second,
    conv_second_mom,
    conv_second_sec,
    up_conv,
    up_conv_mom,
    up_conv_sec,
    conv_merge,
    conv_merge_mom,
    conv_merge_sec,
    head_weight,
    head_mom,
    head_sec,
    biases,
    biases_mom,
    biases_sec,
):
    core = lax.axis_index("core")
    member = (lax.axis_index("zl") * 2 + lax.axis_index("y")) * 2 + core
    zh, x = lax.axis_index("zh"), lax.axis_index("x")

    channel = jnp.arange(8)[:, None] + 8 * jnp.arange(C1 // 8)[None, :]
    sorting = (jnp.arange(C1)[:, None, None] == channel[None]).astype(bf16)
    r1 = conv_first.shape[0] // C1
    r2 = conv_second.shape[0] // C1
    even = r2 % 8 == 0
    count_own = jnp.sum(valid_mask).astype(bf16)
    low_one = jnp.einsum("rc,cqm->qrm", conv_first.astype(bf16).reshape(r1, C1), sorting)
    low_two = conv_second.astype(bf16)
    block = features.reshape(1, -1, 128)
    bundle = [jnp.full((8, 16, 128), count_own, bf16), low_one]
    kernel_rows = 16 + r1
    if even:
        low_two = low_two.reshape(r2 // 8, 8, C1 // 128, 128).transpose(1, 0, 2, 3)
        bundle.append(low_two.reshape(8, r2, 128))
        kernel_rows += r2
    bundle.append(jnp.broadcast_to(block, (8,) + block.shape[1:]))
    bundle, conv_merge, up_conv, skip_feat, labels, pixel_weight = lax.optimization_barrier(
        (jnp.concatenate(bundle, axis=1), conv_merge, up_conv, skip_feat, labels, pixel_weight)
    )

    bundle = lax.all_to_all(bundle, MEMBERS, 0, 0, tiled=True)
    r3 = conv_merge.shape[0] // C0
    ru = up_conv.shape[0] // C0
    zhs = size_of("zh")
    me = jnp.stack([lax.axis_index(axis) for axis in AXES]).astype(jnp.int32)
    low_chip = jnp.concatenate(
        [conv_merge.astype(bf16).reshape(r3, C0), up_conv.astype(bf16).reshape(ru, C0)], axis=0
    )
    low_chip = in_order_back(low_chip.reshape(r3 + ru, 2, HALF).transpose(1, 0, 2))
    low_chip = jnp.concatenate([low_chip[:1], swapped(low_chip[1:], "core")], axis=0)
    merge_pieces, up_pieces = chunk_list(r3, ru)
    if zhs == 2:
        low_chip = joined_on(low_chip, "zh")
    skip = skip_feat.reshape(2, 2, 32, 2, C0).swapaxes(2, 3)
    skip_cells = pair_gather(skip, "core", 3)
    marks = pair_gather(jnp.stack([labels, valid_mask * pixel_weight]), "core", 3)
    marks = marks.reshape(2, 2, 2, 64, 2).swapaxes(3, 4)
    bundle, low_chip, skip_cells = lax.optimization_barrier((bundle, low_chip, skip_cells))

    feat = bundle[:, kernel_rows:].reshape((4, 2) + features.shape[:1] + features.shape[2:])
    feat = feat.transpose(2, 0, 1, 3, 4)
    feat = feat.reshape(feat.shape[0], 4, 2 * feat.shape[3], C0)
    kernels = bundle[:, :kernel_rows].reshape(-1, 128)
    if zhs == 2:
        edge = jnp.where(zh == 0, feat[:, -2:], feat[:, :2])
        got = swapped(jnp.concatenate([kernels, edge.reshape(-1, 128)], axis=0), "zh")
        low_chip = joined_on(low_chip, "x")
        cut = (r3 + ru) // 2
        first, second = low_chip[:, :cut], low_chip[:, cut:]
        first, second = (first, swapped(first, "y")), (second, swapped(second, "zl"))
        feat, kernels, got = lax.optimization_barrier((feat, kernels, got))
        edge = got[8 * kernel_rows :].reshape(edge.shape)
        none = jnp.zeros_like(edge)
        feat = jnp.concatenate(
            [jnp.where(zh == 0, none, edge), feat, jnp.where(zh == 0, edge, none)], axis=1
        )
        kernels = in_order(kernels, got[: 8 * kernel_rows], "zh", 0)
    else:
        feat = padded(feat, "zh", 1, 2)
        kernels = lax.all_gather(kernels, "zh", axis=0, tiled=True)

    kernels = kernels.reshape(8 * zhs, kernel_rows, 128)
    lead = kernels[:, : 16 + r1].reshape(-1, 128)
    edge = jnp.where(x == 0, feat[:, :, -2:], feat[:, :, :2])
    got = swapped(jnp.concatenate([lead, edge.reshape(-1, 128)], axis=0), "x")
    if zhs == 2:
        got, first, second = lax.optimization_barrier((got, first, second))
    edge = got[lead.shape[0] :].reshape(edge.shape)
    none = jnp.zeros_like(edge)
    feat = jnp.concatenate(
        [jnp.where(x == 0, none, edge), feat, jnp.where(x == 0, edge, none)], axis=2
    )

    def ordered(own, other):
        both = jnp.stack([own, other]).reshape(2, zhs, 2, 2, 2, -1, 128)
        return jnp.where(x == 0, both, both[::-1]).transpose(1, 2, 3, 0, 4, 5, 6)

    lead = ordered(lead, got[: lead.shape[0]])
    count_all = jnp.sum(lead[..., 0, 0].astype(f32))
    kernel_one = lead[..., 16:, :].reshape(3, 3, C0, C1 // 8)
    if even:
        kernel_two = kernels[:, 16 + r1 :].reshape(-1, 128)
        kernel_two = ordered(kernel_two, swapped(kernel_two, "x"))
    else:
        low_two = lax.all_gather(low_two.reshape(r2, C1), AXES, axis=0, tiled=True)
        low_two = low_two.reshape(-1, 8, C1)
        kernel_two = lax.dynamic_index_in_dim(low_two, member, axis=1, keepdims=False)
    kernel_two = kernel_two.reshape(3, 3, C1 // 8, C1)
    if zhs == 2:
        first, second = jnp.concatenate(first, axis=0), jnp.concatenate(second, axis=0)
        first = (first, swapped(first, "zl"))
        second = (second, swapped(second, "y"))
    else:
        first = second = jnp.zeros((), bf16)

    bias_one = lax.dynamic_index_in_dim(
        biases[:C1].reshape(C1 // 8, 8), member, axis=1, keepdims=False
    )
    bias_two = biases[C1 : 2 * C1]
    bias_up = lax.dynamic_slice_in_dim(biases[2 * C1 : 2 * C1 + C0], core * (C0 // 2), C0 // 2)
    bias_three = lax.dynamic_slice_in_dim(
        biases[2 * C1 + C0 : 2 * C1 + 2 * C0], core * (C0 // 2), C0 // 2
    )
    bias_head = biases[2 * C1 + 2 * C0 :]
    head_low = lax.dynamic_slice_in_dim(
        head_weight.astype(bf16), core * (C0 // 2), C0 // 2, axis=0
    )

    pre_one = convolve(feat, kernel_one) + bias_one
    high, wide = pre_one.shape[1], pre_one.shape[2]
    row_at = jnp.arange(high)
    col_at = jnp.arange(wide)
    row_in = ((row_at > 0) | (zh > 0)) & ((row_at < high - 1) | (zh < size_of("zh") - 1))
    col_in = ((col_at > 0) | (x > 0)) & ((col_at < wide - 1) | (x < size_of("x") - 1))
    inside = (row_in[:, None] & col_in[None, :])[None, :, :, None]
    act_one = jnp.where(inside, jax.nn.gelu(pre_one), 0.0).astype(bf16)
    part_two = convolve(act_one, kernel_two)
    feat_shifts, act_shifts = by_shift(feat[:, 1:-1, 1:-1]), by_shift(act_one)
    skip, skip_sides = halo(skip_cells)
    part_two, first, second, skip, skip_sides, marks = lax.optimization_barrier(
        (part_two, first, second, skip, skip_sides, marks)
    )
    if zhs == 2:
        kernel_merge, kernel_up = in_place(me, first + second, merge_pieces, up_pieces)
    else:
        low_chip = jnp.where(core == 0, low_chip, low_chip[::-1])
        low_chip = lax.all_gather(low_chip, CHIPS, axis=0, tiled=True)
        kernel_merge = low_chip[:, :r3].reshape(-1, HALF)
        kernel_up = low_chip[:, r3:].reshape(-1, HALF)
    pre_two = group_scatter(part_two) + bias_two
    act_two = jax.nn.gelu(pre_two).astype(bf16)
    act_two, kernel_merge, kernel_up = lax.optimization_barrier((act_two, kernel_merge, kernel_up))

    act_own = act_two[:, 0]
    ups, act_chip = up_on_chip(me, act_own, swapped(act_own, "core"), kernel_up, bias_up[None])
    ups, sides = halo(ups)
    head_wide = jnp.pad(head_low, ((0, 0), (0, 128 - CLASSES)))
    pre_three, logits, planes = merge_on_chip(
        me,
        ups,
        swapped(ups, "core"),
        sides,
        swapped(sides, "core"),
        skip,
        skip_sides,
        kernel_merge,
        bias_three[None],
        head_wide,
    )
    logits = (logits + swapped(logits, "core"))[:, :CLASSES] + bias_head
    logits = logits.reshape(2, 2, 2, 64, CLASSES)
    pre_three = pre_three.reshape(2, 2, 2, 64, HALF)
    act_three = jax.nn.gelu(pre_three).astype(bf16)

    scaled = marks[1].astype(f32)
    onehot = (marks[0][..., None] == jnp.arange(CLASSES, dtype=jnp.int32)).astype(f32)
    log_probs = jax.nn.log_softmax(logits, axis=-1)
    loss_part = -0.5 * jnp.sum(scaled * jnp.sum(onehot * log_probs, axis=-1))
    grad_logits = ((jnp.exp(log_probs) - onehot) * (scaled / count_all)[..., None]).astype(bf16)

    head_part = jnp.einsum("iabwc,iabwk->ck", act_three, grad_logits, preferred_element_type=f32)
    grad_act_three = jnp.einsum(
        "iabwk,ck->iabwc", grad_logits, head_low, preferred_element_type=f32
    )
    grad_pre_three = gelu_back(pre_three, grad_act_three).astype(bf16)
    border, border_sides = halo(grad_pre_three)
    own_grad, away_grad = ups_grad_on_chip(me, border, border_sides, kernel_merge)
    grad_upper = (own_grad + swapped(away_grad, "core").astype(f32)).astype(bf16)
    grad_upper = grad_upper.reshape(2, 2, 2, 64, HALF)
    grad_act_two = jnp.einsum(
        "iabwo,abco->iwc",
        grad_upper,
        kernel_up.reshape(2, 2, C1, HALF),
        preferred_element_type=f32,
    )[:, None]
    grad_act_two = pair_scatter(grad_act_two, "core", 2, f32)
    grad_pre_two = gelu_back(pre_two, grad_act_two).astype(bf16)

    grad_two = group_gather(grad_pre_two)
    if zhs == 2:
        planes = lax.optimization_barrier((planes, grad_pre_two))[0]
        chip_parts = merge_grads(me, planes, grad_pre_three.reshape(512, HALF), r3, ru)
        grad_two, chip_parts = lax.optimization_barrier((grad_two, chip_parts))
        grad_two, inner, sides = second_back_on_chip(grad_two, kernel_two.reshape(-1, C1))
        grad_two, inner, sides, act_chip = lax.optimization_barrier(
            (grad_two, inner, sides, act_chip)
        )
        chip_parts = up_grads(me, act_chip, grad_upper, chip_parts, r3, ru)
        chip_parts, act_shifts = lax.optimization_barrier((chip_parts, act_shifts))
        second_grad = second_grad_on_chip(me, act_shifts, grad_two, r2, 16 * zhs)
        row = jnp.where(zh == 0, inner[:, 5:], inner[:, :1])
        column = jnp.where(x == 0, sides[1], sides[0])
        corner = jnp.where(zh == 0, column[:, 5:], column[:, :1])[:, :, None]
        column = swapped(column[:, 1:5, None], "x")
        corner = lax.ppermute(corner, ("zh", "x"), [(i, 3 - i) for i in range(4)])
        row = swapped(row, "zh")
        row, column, corner, chip_parts = lax.optimization_barrier(
            (row, column, corner, chip_parts)
        )
        at_row = jnp.arange(4)[None, :, None, None] == jnp.where(zh == 0, 3, 0)
        at_column = jnp.arange(64)[None, None, :, None] == jnp.where(x == 0, 63, 0)
        core_part = (
            inner[:, 1:5]
            + jnp.where(at_row, row, 0.0)
            + jnp.where(at_column, column, 0.0)
            + jnp.where(at_row & at_column, corner, 0.0)
        )
    else:
        cells = planes.reshape(2, 4, 4, 64, 2 * C0)
        chip_parts = (
            jnp.concatenate(
                [
                    jnp.einsum(
                        "iabwc,iabwo->co",
                        cells[:, high : high + 2, wide : wide + 2],
                        grad_pre_three,
                        preferred_element_type=f32,
                    )
                    for high in range(3)
                    for wide in range(3)
                ]
            ).astype(bf16),
            jnp.einsum(
                "iwc,iabwo->abco", act_chip, grad_upper, preferred_element_type=f32
            ).astype(bf16),
        )
        images, width = grad_two.shape[1], grad_two.shape[3]
        grad_two = grad_two.reshape(4, 2, images, width, C1).transpose(2, 0, 1, 3, 4)
        grad_two = grad_two.reshape(images, 4, 2 * width, C1)
        second_grad = kernel_grad(act_one, grad_two)
        spill = convolve(grad_two, turned(kernel_two), 2)
        inner = spill[:, 1:-1]
        inner = inner.at[:, :1].add(shifted(spill[:, -1:], "zh", 1))
        inner = inner.at[:, -1:].add(shifted(spill[:, :1], "zh", -1))
        core_part = inner[:, :, 1:-1]
        core_part = core_part.at[:, :, :1].add(shifted(inner[:, :, -1:], "x", 1))
        core_part = core_part.at[:, :, -1:].add(shifted(inner[:, :, :1], "x", -1))
    grad_pre_one = gelu_back(pre_one[:, 1:-1, 1:-1], core_part).astype(bf16)
    tiled = zhs == 2
    if tiled:
        grad_pre_one, second_grad = lax.optimization_barrier((grad_pre_one, second_grad))
        first_grad = first_grad_on_chip(me, feat_shifts, grad_pre_one, r1, 16 * zhs)
        def shard_sum(own, got):
            return (own.astype(f32) + got.astype(f32)).reshape(2, 8, -1, 128)

        def leave(part):
            away = lax.dynamic_index_in_dim(part, 1 - zh, axis=0, keepdims=False).astype(bf16)
            own = lax.dynamic_index_in_dim(part, zh, axis=0, keepdims=False)
            return own, away, swapped(away, "zh")

        chip_parts = sent(chip_parts, "zl", "y")
        chip_parts = sent(added(chip_parts), "y", "zl")
        second_stays = after(chip_parts[0], second_grad[0])[1]
        two_own, two_away, two_got = leave(shard_sum(second_stays, swapped(second_grad[1], "x")))
        two_away, first_stays = after(two_away, first_grad[0])
        one_own, one_away, one_got = leave(shard_sum(first_stays, swapped(first_grad[1], "x")))
        one_away, chip_parts = after(one_away, chip_parts)
        chip_parts = added(chip_parts)
        chip_stays, chip_goes = (
            jnp.concatenate([chip_parts[i], chip_parts[i + 2]], axis=1) for i in range(2)
        )
        chip_got = swapped(chip_goes, "x")
        chip_goes, two_own = after(chip_goes, two_own)
        part_two = two_own + two_got.astype(f32)
        two_low, chip_stays, one_own = after(part_two.astype(bf16), chip_stays, one_own)
        chip_parts = chip_stays.astype(f32) + chip_got.astype(f32)
        chip_goes = chip_parts[2:].astype(bf16)
        part_chip = chip_parts[:2] + swapped(chip_goes, "zh").astype(f32)
        chip_goes, one_own = after(chip_goes, one_own)
        part_one = one_own + one_got.astype(f32)
        one_low = part_one.astype(bf16)
        sq_kernels = jnp.sum(part_one * part_one) + jnp.sum(part_two * part_two)
        part = jnp.concatenate([one_low, two_low], axis=1)
        part = lax.all_to_all(part, MEMBERS, 0, 0, tiled=True)
        part_one, part_two = part[:, :r1], part[:, r1:]
        half = r3 // 2
        part_chip = jnp.concatenate(
            [
                part_chip[:, :half],
                part_chip[:, half + ru // 2 : r3 + ru // 2],
                part_chip[:, half : half + ru // 2],
                part_chip[:, r3 + ru // 2 :],
            ],
            axis=1,
        )
        part_two = part_two.reshape(8, r2 // 8, C1 // 128, 128).transpose(1, 0, 2, 3)
        share_two = part_two.reshape(-1).astype(f32)
    else:
        first_grad = kernel_grad(feat[:, 1:-1, 1:-1], grad_pre_one)
        mine = jnp.arange(8)[None, :, None] == member
        part_two = jnp.where(mine, second_grad.astype(bf16)[:, None], 0)
        share_two = lax.psum_scatter(
            part_two.reshape(-1, C1), AXES, scatter_dimension=0, tiled=True
        ).reshape(-1).astype(f32)
        part_one = far_scatter(first_grad)
        sq_kernels = jnp.sum(share_two * share_two) + jnp.sum(part_one * part_one)
        part_one = lax.all_to_all(part_one.astype(bf16), MEMBERS, 0, 0, tiled=True)
        part_chip = jnp.concatenate(
            [last_sum(chip_parts[0]), last_sum(chip_parts[1])], axis=1
        )
    share_one = jnp.einsum("qrm,cqm->rc", part_one, sorting, preferred_element_type=f32).reshape(-1)
    sq_chip = jnp.sum(part_chip * part_chip)
    part_chip = part_chip.astype(bf16)
    part_chip = in_order(part_chip[0], swapped(part_chip[1], "core"), "core", 1).astype(f32)
    share_merge = part_chip[:r3].reshape(-1)
    share_up = part_chip[r3:].reshape(-1)
    share_sq = sq_kernels + sq_chip
    spread_one = (
        jnp.where(jnp.arange(8)[None, :] == member, column_sum(grad_pre_one)[:, None], 0.0)
    ).reshape(-1)

    def half_of(values):
        shape = (2 * values.shape[0],) + values.shape[1:]
        return lax.dynamic_update_slice_in_dim(
            jnp.zeros(shape, f32), values, core * values.shape[0], axis=0
        )

    packed = jnp.concatenate(
        [
            spread_one,
            column_sum(grad_pre_two),
            half_of(column_sum(grad_upper)),
            half_of(column_sum(grad_pre_three)),
            0.5 * column_sum(grad_logits),
            half_of(head_part).reshape(-1),
            share_sq[None],
            loss_part[None],
        ]
    )
    packed = total(packed, ("core", "x", "y"))
    packed, share_one, share_two = lax.optimization_barrier((packed, share_one, share_two))
    packed = total(packed, ("zl", "zh"))
    bias_total = packed[: biases.shape[0]]
    head_total = packed[biases.shape[0] : -2].reshape(head_weight.shape)
    sq_total, loss_total = packed[-2], packed[-1]
    grad_norm = jnp.sqrt(sq_total + jnp.sum(jnp.square(packed[:-2])))
    factor = clip_norm / jnp.maximum(grad_norm, clip_norm)
    outs = ()
    for weight, moment, second, grad, decay in (
        (conv_first, conv_first_mom, conv_first_sec, share_one, weight_decay),
        (conv_second, conv_second_mom, conv_second_sec, share_two, weight_decay),
        (up_conv, up_conv_mom, up_conv_sec, share_up, weight_decay),
        (conv_merge, conv_merge_mom, conv_merge_sec, share_merge, weight_decay),
        (head_weight, head_mom, head_sec, head_total, weight_decay),
        (biases, biases_mom, biases_sec, bias_total, 0.0),
    ):
        outs += adamw(weight, moment, second, grad * factor, decay)
    return outs + (loss_total, count_all, grad_norm)


def solution(mesh):
    rows, cols = mesh.shape["rows"], mesh.shape["cols"]
    split = Mesh(mesh.devices.reshape(rows // 4, 2, 2, cols // 2, 2), AXES)
    image = P(None, ROWS, ("x", "core"))
    flat = P(AXES)
    return jax.shard_map(
        shards,
        mesh=split,
        in_specs=(image,) * 5 + (flat,) * 12 + (P(),) * 6,
        out_specs=(flat,) * 12 + (P(),) * 9,
        check_vma=False,
    )
```

```python
import math

import jax
import jax.numpy as jnp
from jax import lax
from jax.experimental import pallas as pl
from jax.experimental.pallas import tpu as pltpu
from jax.sharding import Mesh
from jax.sharding import PartitionSpec as P

C0 = 512
C1 = 1024
CLASSES = 2
STEP = 10

clip_norm = 0.05
learn_rate = 0.02
beta_first = 0.9
beta_second = 0.999
epsilon = 1e-08
weight_decay = 0.1

AXES = ("zh", "zl", "y", "x", "core")
MEMBERS = ("zl", "y", "core")
CHIPS = ("zh", "zl", "y", "x")
ROWS = ("zh", "zl", "y")
bf16 = jnp.bfloat16
f32 = jnp.float32


def size_of(axis):
    return lax.axis_size(axis)


def shifted(values, axis, step):
    count = size_of(axis)
    return lax.ppermute(
        values, axis, [(i, i + step) for i in range(count) if 0 <= i + step < count]
    )


def swapped(values, axis):
    return lax.ppermute(values, axis, [(0, 1), (1, 0)])


def padded(cells, axis, dim, width):
    head = lax.slice_in_dim(cells, 0, width, axis=dim)
    tail = lax.slice_in_dim(cells, cells.shape[dim] - width, cells.shape[dim], axis=dim)
    return jnp.concatenate(
        [shifted(tail, axis, 1), cells, shifted(head, axis, -1)], axis=dim
    )


def in_order(own, other, axis, dim):
    first = lax.axis_index(axis) == 0
    return jnp.concatenate(
        [jnp.where(first, own, other), jnp.where(first, other, own)], axis=dim
    )


def pair_gather(own, axis, dim):
    return in_order(own, swapped(own, axis), axis, dim)


def pair_half(values, axis, dim, index):
    width = values.shape[dim] // 2
    return lax.dynamic_slice_in_dim(values, index * width, width, axis=dim)


def pair_scatter(values, axis, dim, kind):
    me = lax.axis_index(axis)
    away = pair_half(values, axis, dim, 1 - me).astype(kind)
    return pair_half(values, axis, dim, me).astype(f32) + swapped(away, axis).astype(f32)


def total(values, axes=("core", "x", "y", "zl", "zh")):
    for axis in axes:
        if size_of(axis) == 2:
            values = values + swapped(values, axis)
        else:
            values = lax.psum(values, axis)
    return values


def convolve(values, kernel, pad=0):
    return lax.conv_general_dilated(
        values,
        kernel,
        (1, 1),
        ((pad, pad), (pad, pad)),
        dimension_numbers=("NHWC", "HWIO", "NHWC"),
        preferred_element_type=f32,
    )


def kernel_grad(cells, grad):
    rows_in, cols_in = (grad.shape[1], grad.shape[2])
    terms = [
        jnp.einsum(
            "nhwc,nhwo->co",
            cells[:, shift_h : shift_h + rows_in, shift_w : shift_w + cols_in],
            grad,
            preferred_element_type=f32,
        )
        for shift_h in range(3)
        for shift_w in range(3)
    ]
    return jnp.concatenate(terms, axis=0)


def turned(kernel):
    return jnp.swapaxes(kernel[::-1, ::-1], 2, 3)


def gelu_back(pre_act, upstream):
    return jax.vjp(jax.nn.gelu, pre_act)[1](upstream)[0]


def column_sum(values):
    return jnp.sum(values, axis=tuple(range(values.ndim - 1)), dtype=f32)


def group_gather(block):
    return lax.all_to_all(
        jnp.broadcast_to(block[None], (8,) + block.shape), MEMBERS, 0, 0, tiled=True
    )


def group_scatter(partial):
    n, _, w2, c = partial.shape
    sent = partial.astype(bf16).reshape(n, 4, 2, w2 // 2, c).transpose(1, 2, 0, 3, 4)
    got = lax.all_to_all(sent.reshape(8, n, w2 // 2, c), MEMBERS, 0, 0, tiled=True)
    return jnp.sum(got.astype(f32), axis=0)[:, None]


def over_zh(part):
    if size_of("zh") == 2:
        return pair_gather(part[None], "zh", 0)
    return lax.all_gather(part, "zh", axis=0)


def over_x(part):
    part = pair_gather(part[:, None], "x", 1)
    zh, _, _, r, o = part.shape
    return part.reshape(zh, 2, 2, 2, 2, r, o).transpose(0, 2, 3, 1, 4, 5, 6)


def far_scatter(grad, kind=bf16):
    zh = size_of("zh")
    o = grad.shape[1]
    r = grad.shape[0] // (16 * zh)
    split = grad.reshape(zh, 2, 2, 2, 2, r, o).transpose(3, 0, 1, 2, 4, 5, 6)
    split = pair_scatter(split, "x", 0, kind)[0]
    if zh == 2:
        split = pair_scatter(split, "zh", 0, kind)[0]
    else:
        split = lax.psum_scatter(split, "zh", scatter_dimension=0)
    return split.reshape(8, r, o)


HALF = C0 // 2


def joined_on(values, axis):
    return jnp.concatenate([values, swapped(values, axis)], axis=0)


def sent(parts, first_axis, second_axis):
    if len(parts) == 1:
        return parts
    return parts[0], swapped(parts[1], first_axis), parts[2], swapped(parts[3], second_axis)


def halves_of(own, got):
    half = own.shape[0] // 2
    return tuple(
        (v.astype(f32) + w.astype(f32)).astype(bf16)
        for v, w in ((own[:half], got[:half]), (own[half:], got[half:]))
    )


def added(parts):
    return halves_of(*parts[:2]) + halves_of(*parts[2:])


def after(earlier, *parts):
    own = [part[::2] if isinstance(part, tuple) else (part,) for part in parts]
    earlier, own = lax.optimization_barrier((earlier, own))
    out = [earlier]
    for part, kept in zip(parts, own):
        if isinstance(part, tuple):
            out.append((kept[0], part[1], kept[1], part[3]))
        else:
            out.append(kept[0])
    return out


def place(chunk, me, first):
    bits = [me[i] if not (chunk >> (4 - i)) & 1 else 1 - me[i] for i in range(5)]
    zh, zl, y, x, core = bits
    high, low = (zl, y) if first == "y" else (y, zl)
    return high * 16 + low * 8 + x * 4 + zh * 2 + core


def chunk_list(r3, ru):
    cut = (r3 + ru) // 2
    merge, up = [], []
    for chunk in range(32):
        merge.append((0, (chunk, "y"), 0, cut, r3 * chunk))
        merge.append((2, (chunk, "zl"), 0, r3 - cut, r3 * chunk + cut))
        up.append((2, (chunk, "zl"), r3 - cut, ru, ru * chunk))
    return merge, up


def in_place(me, sources, merge_pieces, up_pieces):
    lists = (merge_pieces, up_pieces)
    count = len(merge_pieces) + len(up_pieces)

    def body(me_ref, *rest):
        source_refs, targets, sems = rest[:4], rest[4:6], rest[6]
        waits = []
        for pieces, target in zip(lists, targets):
            for which, spot, start, rows, to in pieces:
                sem = sems.at[len(waits)]
                here = target.at[pl.ds(to, rows), :]
                at = place(spot[0], me_ref, spot[1])
                for side in range(2):
                    inside = at - 16 * side

                    @pl.when((inside >= 0) & (inside < 16))
                    def _(source=source_refs[which + side], inside=inside, start=start, rows=rows, here=here, sem=sem):
                        there = source.at[inside, pl.ds(start, rows), :]
                        pltpu.make_async_copy(there, here, sem).start()

                there = source_refs[which].at[0, pl.ds(start, rows), :]
                waits.append(pltpu.make_async_copy(there, here, sem))
        for copy in waits:
            copy.wait()

    rows = [sum(piece[3] for piece in pieces) for pieces in lists]
    return on_chip(
        body,
        (me, *sources),
        tuple(jax.ShapeDtypeStruct((n, HALF), bf16) for n in rows),
        [pltpu.SemaphoreType.DMA((count,))],
        ("saaaa", "vv"),
        0,
    )


def on_chip(body, ins, outs, scratch, spaces, flops, aliases=()):
    kinds = {"v": pltpu.VMEM, "s": pltpu.SMEM, "a": pl.ANY}
    held = [v for v, k in zip(list(ins) + list(outs), spaces[0] + spaces[1]) if k == "v"]
    held += [v for v in scratch if len(v.shape) > 1]
    room = sum(math.prod(v.shape) * jnp.dtype(v.dtype).itemsize for v in held)
    limit = 58 * 1024 * 1024 if "a" in spaces[1] else int(1.25 * room) + 6 * 1024 * 1024
    return pl.pallas_call(
        body,
        out_shape=outs,
        in_specs=[pl.BlockSpec(memory_space=kinds[k]) for k in spaces[0]],
        out_specs=[pl.BlockSpec(memory_space=kinds[k]) for k in spaces[1]],
        scratch_shapes=scratch,
        input_output_aliases=dict(aliases),
        compiler_params=pltpu.CompilerParams(vmem_limit_bytes=limit),
        cost_estimate=pl.CostEstimate(flops=0, bytes_accessed=0, transcendentals=0),
    )(*ins)


def up_on_chip(me, own, other, kernel, bias):
    def body(me_ref, own_ref, other_ref, kernel_ref, bias_ref, ups_ref, act_ref):
        core = me_ref[4]
        mine = pl.ds(pl.multiple_of(core * 32, 32), 32)
        yours = pl.ds(pl.multiple_of((1 - core) * 32, 32), 32)
        for image in range(2):
            act_ref[image, mine, :] = own_ref[image]
            act_ref[image, yours, :] = other_ref[image]
        values = act_ref[...].reshape(128, C1)
        for tap in range(4):
            got = jnp.dot(
                values, kernel_ref[tap * C1 : (tap + 1) * C1, :], preferred_element_type=f32
            )
            got = (got + bias_ref[...]).astype(bf16).reshape(2, 64, HALF)
            for image in range(2):
                ups_ref[image, tap // 2, tap % 2] = got[image]

    return on_chip(
        body,
        (me, own, other, kernel, bias),
        (
            jax.ShapeDtypeStruct((2, 2, 2, 64, HALF), bf16),
            jax.ShapeDtypeStruct((2, 64, C1), bf16),
        ),
        [],
        ("svvvv", "vv"),
        2 * 128 * C1 * 4 * HALF,
    )


def planes_in(target, lanes, rows_ref, sides_ref):
    line = lax.broadcasted_iota(jnp.int32, (64, 1), 0)
    for image in range(2):
        for row in range(4):
            even = rows_ref[image, row, 0]
            odd = rows_ref[image, row, 1]
            target[image, row, 1, :, lanes] = even
            target[image, row, 2, :, lanes] = odd
            left = sides_ref[0, image, row : row + 1, :].astype(f32)
            right = sides_ref[1, image, row : row + 1, :].astype(f32)
            moved = pltpu.roll(odd.astype(f32), 1, 0)
            target[image, row, 0, :, lanes] = jnp.where(line == 0, left, moved).astype(bf16)
            moved = pltpu.roll(even.astype(f32), 63, 0)
            target[image, row, 3, :, lanes] = jnp.where(line == 63, right, moved).astype(bf16)


def tapped(planes, image, tap, lanes):
    high, wide = tap // 3, tap % 3
    cells = planes[image, high : high + 2, wide : wide + 2, :, lanes]
    return cells.reshape(256, cells.shape[-1])


def merge_on_chip(me, own, other, own_sides, other_sides, skip, skip_sides, kernel, bias, head):
    def body(me_ref, own_ref, other_ref, own_sides_ref, other_sides_ref, skip_ref, skip_sides_ref, kernel_ref, bias_ref, head_ref, pre_ref, logits_ref, planes_ref):
        low, high = slice(0, HALF), slice(HALF, C0)

        @pl.when(me_ref[4] == 0)
        def _():
            planes_in(planes_ref, low, own_ref, own_sides_ref)
            planes_in(planes_ref, high, other_ref, other_sides_ref)

        @pl.when(me_ref[4] == 1)
        def _():
            planes_in(planes_ref, high, own_ref, own_sides_ref)
            planes_in(planes_ref, low, other_ref, other_sides_ref)

        planes_in(planes_ref, slice(C0, 2 * C0), skip_ref, skip_sides_ref)
        for image in range(2):
            total = jnp.broadcast_to(bias_ref[...], (256, HALF))
            for tap in range(9):
                total = total + jnp.dot(
                    tapped(planes_ref, image, tap, slice(0, 2 * C0)),
                    kernel_ref[tap * 2 * C0 : (tap + 1) * 2 * C0, :],
                    preferred_element_type=f32,
                )
            pre_ref[image * 256 : (image + 1) * 256, :] = total
        act = jax.nn.gelu(pre_ref[...]).astype(bf16)
        logits_ref[...] = jnp.dot(act, head_ref[...], preferred_element_type=f32)

    return on_chip(
        body,
        (me, own, other, own_sides, other_sides, skip, skip_sides, kernel, bias, head),
        (
            jax.ShapeDtypeStruct((512, HALF), f32),
            jax.ShapeDtypeStruct((512, 128), f32),
            jax.ShapeDtypeStruct((2, 4, 4, 64, 2 * C0), bf16),
        ),
        [],
        ("svvvvvvvvv", "vvv"),
        2 * 512 * 18 * C0 * HALF,
    )


def ups_grad_on_chip(me, rows, sides, kernel):
    def body(me_ref, rows_ref, sides_ref, kernel_ref, own_ref, away_ref, planes):
        core = me_ref[4]
        planes_in(planes, slice(0, HALF), rows_ref, sides_ref)
        for image in range(2):
            lines = slice(image * 256, (image + 1) * 256)
            for target, half in ((own_ref, core), (away_ref, 1 - core)):
                total = jnp.zeros((256, HALF), f32)
                for tap in range(9):
                    start = pl.multiple_of((8 - tap) * 2 * C0 + half * HALF, HALF)
                    total = total + lax.dot_general(
                        tapped(planes, image, tap, slice(0, HALF)),
                        kernel_ref[pl.ds(start, HALF), :],
                        (((1,), (1,)), ((), ())),
                        preferred_element_type=f32,
                    )
                target[lines, :] = total.astype(target.dtype)

    return on_chip(
        body,
        (me, rows, sides, kernel),
        (jax.ShapeDtypeStruct((512, HALF), f32), jax.ShapeDtypeStruct((512, HALF), bf16)),
        [pltpu.VMEM((2, 4, 4, 64, HALF), bf16)],
        ("svvv", "vv"),
        2 * 512 * 9 * C0 * HALF,
    )


def chunk_writes(me_ref, pieces, whole, targets, sems):
    waits = []
    for i, (pair, spot, start, rows, to) in enumerate(pieces):
        here = whole.at[pl.ds(start, rows), :]
        at = place(spot[0], me_ref, spot[1])
        for side in range(2):
            inside = at - 16 * side

            @pl.when((inside >= 0) & (inside < 16))
            def _(here=here, target=targets[pair + side], inside=inside, rows=rows, to=to, i=i):
                there = target.at[inside, pl.ds(to, rows), :]
                pltpu.make_async_copy(here, there, sems.at[i]).start()

        there = targets[pair].at[0, pl.ds(to, rows), :]
        waits.append(pltpu.make_async_copy(here, there, sems.at[i]))
    for copy in waits:
        copy.wait()


def halves(rows, to):
    pieces = []
    for chunk in range(32):
        pieces.append((0, (chunk, "y"), rows * chunk, rows // 2, to))
        pieces.append((2, (chunk, "zl"), rows * chunk + rows // 2, rows // 2, to))
    return pieces


def merge_grads(me, planes, grad, r3, ru):
    pieces = halves(r3, 0)

    def body(me_ref, planes_ref, grad_ref, *rest):
        targets, whole, sems = rest[:4], rest[4], rest[5]
        for tap in range(9):
            total = jnp.zeros((2 * C0, HALF), f32)
            for image in range(2):
                total = total + lax.dot_general(
                    tapped(planes_ref, image, tap, slice(0, 2 * C0)),
                    grad_ref[image * 256 : (image + 1) * 256, :],
                    (((0,), (0,)), ((), ())),
                    preferred_element_type=f32,
                )
            whole[tap * 2 * C0 : (tap + 1) * 2 * C0, :] = total.astype(bf16)
        chunk_writes(me_ref, pieces, whole, targets, sems)

    return on_chip(
        body,
        (me, planes, grad),
        (jax.ShapeDtypeStruct((16, (r3 + ru) // 2, HALF), bf16),) * 4,
        [pltpu.VMEM((18 * C0, HALF), bf16), pltpu.SemaphoreType.DMA((len(pieces),))],
        ("svv", "aaaa"),
        0,
    )


def up_grads(me, act, ups_grad, parts, r3, ru):
    pieces = halves(ru, r3 // 2)

    def body(me_ref, act_ref, ups_grad_ref, *rest):
        targets, whole, sems = rest[4:8], rest[8], rest[9]
        values = act_ref[...].reshape(128, C1)
        for tap in range(4):
            cells = ups_grad_ref[:, tap // 2, tap % 2].reshape(128, HALF)
            total = lax.dot_general(
                values, cells, (((0,), (0,)), ((), ())), preferred_element_type=f32
            )
            whole[tap * C1 : (tap + 1) * C1, :] = total.astype(bf16)
        chunk_writes(me_ref, pieces, whole, targets, sems)

    return on_chip(
        body,
        (me, act, ups_grad, *parts),
        (jax.ShapeDtypeStruct((16, (r3 + ru) // 2, HALF), bf16),) * 4,
        [pltpu.VMEM((4 * C1, HALF), bf16), pltpu.SemaphoreType.DMA((len(pieces),))],
        ("svvaaaa", "aaaa"),
        0,
        {3 + i: i for i in range(4)},
    )


def side_list(first_rows, rows, chunks):
    return [
        ((chunk >> 1) & 1, (chunk >> 2) * 2 + (chunk & 1), rows * chunk, rows, first_rows)
        for chunk in range(chunks)
    ]


def two_ways(pieces, me, stays, goes, source, sems):
    for i, (side, at, start, count, to) in enumerate(pieces):
        here = source.at[pl.ds(start, count), :]
        for target, wanted in ((stays, side), (goes, 1 - side)):

            @pl.when(me[3] == wanted)
            def _(here=here, target=target, at=at, to=to, count=count, i=i):
                there = target.at[at, pl.ds(to, count), :]
                pltpu.make_async_copy(here, there, sems.at[i]).start()

    for i, (side, at, start, count, to) in enumerate(pieces):
        here = source.at[pl.ds(start, count), :]
        pltpu.make_async_copy(here, stays.at[at, pl.ds(to, count), :], sems.at[i]).wait()


def second_grad_on_chip(me, cells, grad, rows, chunks):
    images, width, outs = cells.shape[1], cells.shape[4], grad.shape[3]
    tiles = outs // 128
    pieces = side_list(0, rows, chunks)

    def body(me_ref, cells_ref, grad_ref, stays_ref, goes_ref, wide, narrow, sems):
        upstream = grad_ref[...].reshape(images * 256, outs)
        for tap in range(9):
            values = cells_ref[tap % 3, :, tap // 3 : tap // 3 + 4].reshape(images * 256, width)
            got = lax.dot_general(
                values, upstream, (((0,), (0,)), ((), ())), preferred_element_type=f32
            )
            for tile in range(tiles):
                wide[:, tile, :] = got[:, tile * 128 : (tile + 1) * 128]
            narrow[tap * width * tiles : (tap + 1) * width * tiles, :] = (
                wide[...].reshape(width * tiles, 128).astype(bf16)
            )
        two_ways(pieces, me_ref, stays_ref, goes_ref, narrow, sems)

    return on_chip(
        body,
        (me, cells, grad),
        (jax.ShapeDtypeStruct((chunks // 2, rows, 128), bf16),) * 2,
        [
            pltpu.VMEM((width, tiles, 128), f32),
            pltpu.VMEM((9 * width * tiles, 128), bf16),
            pltpu.SemaphoreType.DMA((chunks,)),
        ],
        ("svv", "aa"),
        2 * images * 256 * 9 * width * outs,
    )


def first_grad_on_chip(me, cells, grad, rows, chunks):
    images, width, outs = cells.shape[1], cells.shape[4], grad.shape[3]
    pieces = side_list(0, rows, chunks)

    def body(me_ref, cells_ref, grad_ref, stays_ref, goes_ref, narrow, sems):
        upstream = grad_ref[...].reshape(images * 256, outs)
        for tap in range(9):
            values = cells_ref[tap % 3, :, tap // 3 : tap // 3 + 4].reshape(images * 256, width)
            got = lax.dot_general(
                values, upstream, (((0,), (0,)), ((), ())), preferred_element_type=f32
            )
            narrow[tap * width : (tap + 1) * width, :] = got.astype(bf16)
        two_ways(pieces, me_ref, stays_ref, goes_ref, narrow, sems)

    return on_chip(
        body,
        (me, cells, grad),
        (jax.ShapeDtypeStruct((chunks // 2, rows, 128), bf16),) * 2,
        [pltpu.VMEM((9 * width, 128), bf16), pltpu.SemaphoreType.DMA((chunks,))],
        ("svv", "aa"),
        2 * images * 256 * 9 * width * outs,
    )


def second_back_on_chip(grad, kernel):
    images = grad.shape[1]

    def body(grad_ref, kernel_ref, order_ref, inner_ref, sides_ref, parts):
        for member in range(8):
            row, core = member // 2, member % 2
            for image in range(images):
                order_ref[image, row, core * 32 : (core + 1) * 32] = grad_ref[member, image, 0]
        parts[...] = jnp.zeros(parts.shape, f32)
        for image in range(images):
            values = order_ref[image].reshape(256, C1)
            for tap in range(9):
                got = lax.dot_general(
                    values,
                    kernel_ref[tap * 128 : (tap + 1) * 128, :],
                    (((1,), (1,)), ((), ())),
                    preferred_element_type=f32,
                )
                high = tap // 3
                parts[tap % 3, image, high : high + 4] += got.reshape(4, 64, 128)
        line = lax.broadcasted_iota(jnp.int32, (64, 1), 0)
        for image in range(images):
            for row in range(6):
                before = pltpu.roll(parts[0, image, row], 63, 0)
                later = pltpu.roll(parts[2, image, row], 1, 0)
                inner_ref[image, row] = (
                    parts[1, image, row]
                    + jnp.where(line == 63, 0.0, before)
                    + jnp.where(line == 0, 0.0, later)
                )
                sides_ref[0, image, row : row + 1, :] = parts[0, image, row, 0:1, :]
                sides_ref[1, image, row : row + 1, :] = parts[2, image, row, 63:64, :]

    return on_chip(
        body,
        (grad, kernel),
        (
            jax.ShapeDtypeStruct((images, 4, 64, C1), bf16),
            jax.ShapeDtypeStruct((images, 6, 64, 128), f32),
            jax.ShapeDtypeStruct((2, images, 6, 128), f32),
        ),
        [pltpu.VMEM((3, images, 6, 64, 128), f32)],
        ("vv", "vvv"),
        0,
    )


def by_shift(cells):
    return jnp.stack([cells[:, :, shift : shift + 64] for shift in range(3)])


def last_sum(whole):
    whole = whole.reshape(8 * size_of("zh"), 2, -1, HALF)
    whole = lax.psum_scatter(whole, CHIPS, scatter_dimension=0)
    return in_order_back(whole).astype(f32)


def in_order_back(pair):
    own = lax.dynamic_index_in_dim(pair, lax.axis_index("core"), axis=0)
    away = lax.dynamic_index_in_dim(pair, 1 - lax.axis_index("core"), axis=0)
    return jnp.concatenate([own, away], axis=0)


def halo(cells):
    width = cells.shape[-1]
    left_chip = lax.axis_index("x") == 0
    edge = jnp.where(left_chip, cells[:, :, 1, 63], cells[:, :, 0, 0])
    beside = swapped(edge, "x")

    def with_side(row):
        return jnp.concatenate(
            [cells[:, row].reshape(-1, width), beside[:, row], jnp.zeros((14, width), bf16)], axis=0
        )

    above = shifted(with_side(1), ROWS, 1)
    below = shifted(with_side(0), ROWS, -1)
    shape = (2, 1, 2, 64, width)
    rows = jnp.concatenate(
        [above[:256].reshape(shape), cells, below[:256].reshape(shape)], axis=1
    )
    beside = jnp.concatenate(
        [above[256:258, None], beside, below[256:258, None]], axis=1
    )
    none = jnp.zeros_like(beside)
    sides = jnp.stack([jnp.where(left_chip, none, beside), jnp.where(left_chip, beside, none)])
    return rows, sides


def adamw(weight, moment, second, grad, decay):
    new_mom = beta_first * moment + (1.0 - beta_first) * grad
    new_sec = beta_second * second + (1.0 - beta_second) * grad * grad
    corrected = new_mom / (1.0 - beta_first**STEP)
    spread = jnp.sqrt(new_sec / (1.0 - beta_second**STEP))
    return (
        new_mom,
        new_sec,
        weight - learn_rate * (corrected / (spread + epsilon) + decay * weight),
    )


def shards(
    features,
    skip_feat,
    labels,
    pixel_weight,
    valid_mask,
    conv_first,
    conv_first_mom,
    conv_first_sec,
    conv_second,
    conv_second_mom,
    conv_second_sec,
    up_conv,
    up_conv_mom,
    up_conv_sec,
    conv_merge,
    conv_merge_mom,
    conv_merge_sec,
    head_weight,
    head_mom,
    head_sec,
    biases,
    biases_mom,
    biases_sec,
):
    core = lax.axis_index("core")
    member = (lax.axis_index("zl") * 2 + lax.axis_index("y")) * 2 + core
    zh, x = lax.axis_index("zh"), lax.axis_index("x")

    channel = jnp.arange(8)[:, None] + 8 * jnp.arange(C1 // 8)[None, :]
    sorting = (jnp.arange(C1)[:, None, None] == channel[None]).astype(bf16)
    r1 = conv_first.shape[0] // C1
    r2 = conv_second.shape[0] // C1
    even = r2 % 8 == 0
    count_own = jnp.sum(valid_mask).astype(bf16)
    low_one = jnp.einsum("rc,cqm->qrm", conv_first.astype(bf16).reshape(r1, C1), sorting)
    low_two = conv_second.astype(bf16)
    block = features.reshape(1, -1, 128)
    bundle = [jnp.full((8, 16, 128), count_own, bf16), low_one]
    kernel_rows = 16 + r1
    if even:
        low_two = low_two.reshape(r2 // 8, 8, C1 // 128, 128).transpose(1, 0, 2, 3)
        bundle.append(low_two.reshape(8, r2, 128))
        kernel_rows += r2
    bundle.append(jnp.broadcast_to(block, (8,) + block.shape[1:]))
    bundle, conv_merge, up_conv, skip_feat, labels, pixel_weight = lax.optimization_barrier(
        (jnp.concatenate(bundle, axis=1), conv_merge, up_conv, skip_feat, labels, pixel_weight)
    )

    bundle = lax.all_to_all(bundle, MEMBERS, 0, 0, tiled=True)
    r3 = conv_merge.shape[0] // C0
    ru = up_conv.shape[0] // C0
    zhs = size_of("zh")
    me = jnp.stack([lax.axis_index(axis) for axis in AXES]).astype(jnp.int32)
    low_chip = jnp.concatenate(
        [conv_merge.astype(bf16).reshape(r3, C0), up_conv.astype(bf16).reshape(ru, C0)], axis=0
    )
    low_chip = in_order_back(low_chip.reshape(r3 + ru, 2, HALF).transpose(1, 0, 2))
    low_chip = jnp.concatenate([low_chip[:1], swapped(low_chip[1:], "core")], axis=0)
    merge_pieces, up_pieces = chunk_list(r3, ru)
    if zhs == 2:
        low_chip = joined_on(low_chip, "zh")
    skip = skip_feat.reshape(2, 2, 32, 2, C0).swapaxes(2, 3)
    skip_cells = pair_gather(skip, "core", 3)
    marks = pair_gather(jnp.stack([labels, valid_mask * pixel_weight]), "core", 3)
    marks = marks.reshape(2, 2, 2, 64, 2).swapaxes(3, 4)
    bundle, low_chip, skip_cells = lax.optimization_barrier((bundle, low_chip, skip_cells))

    feat = bundle[:, kernel_rows:].reshape((4, 2) + features.shape[:1] + features.shape[2:])
    feat = feat.transpose(2, 0, 1, 3, 4)
    feat = feat.reshape(feat.shape[0], 4, 2 * feat.shape[3], C0)
    kernels = bundle[:, :kernel_rows].reshape(-1, 128)
    if zhs == 2:
        edge = jnp.where(zh == 0, feat[:, -2:], feat[:, :2])
        got = swapped(jnp.concatenate([kernels, edge.reshape(-1, 128)], axis=0), "zh")
        low_chip = joined_on(low_chip, "x")
        cut = (r3 + ru) // 2
        first, second = low_chip[:, :cut], low_chip[:, cut:]
        first, second = (first, swapped(first, "y")), (second, swapped(second, "zl"))
        feat, kernels, got = lax.optimization_barrier((feat, kernels, got))
        edge = got[8 * kernel_rows :].reshape(edge.shape)
        none = jnp.zeros_like(edge)
        feat = jnp.concatenate(
            [jnp.where(zh == 0, none, edge), feat, jnp.where(zh == 0, edge, none)], axis=1
        )
        kernels = in_order(kernels, got[: 8 * kernel_rows], "zh", 0)
    else:
        feat = padded(feat, "zh", 1, 2)
        kernels = lax.all_gather(kernels, "zh", axis=0, tiled=True)

    kernels = kernels.reshape(8 * zhs, kernel_rows, 128)
    lead = kernels[:, : 16 + r1].reshape(-1, 128)
    edge = jnp.where(x == 0, feat[:, :, -2:], feat[:, :, :2])
    got = swapped(jnp.concatenate([lead, edge.reshape(-1, 128)], axis=0), "x")
    if zhs == 2:
        got, first, second = lax.optimization_barrier((got, first, second))
    edge = got[lead.shape[0] :].reshape(edge.shape)
    none = jnp.zeros_like(edge)
    feat = jnp.concatenate(
        [jnp.where(x == 0, none, edge), feat, jnp.where(x == 0, edge, none)], axis=2
    )

    def ordered(own, other):
        both = jnp.stack([own, other]).reshape(2, zhs, 2, 2, 2, -1, 128)
        return jnp.where(x == 0, both, both[::-1]).transpose(1, 2, 3, 0, 4, 5, 6)

    lead = ordered(lead, got[: lead.shape[0]])
    count_all = jnp.sum(lead[..., 0, 0].astype(f32))
    kernel_one = lead[..., 16:, :].reshape(3, 3, C0, C1 // 8)
    if even:
        kernel_two = kernels[:, 16 + r1 :].reshape(-1, 128)
        kernel_two = ordered(kernel_two, swapped(kernel_two, "x"))
    else:
        low_two = lax.all_gather(low_two.reshape(r2, C1), AXES, axis=0, tiled=True)
        low_two = low_two.reshape(-1, 8, C1)
        kernel_two = lax.dynamic_index_in_dim(low_two, member, axis=1, keepdims=False)
    kernel_two = kernel_two.reshape(3, 3, C1 // 8, C1)
    if zhs == 2:
        first, second = jnp.concatenate(first, axis=0), jnp.concatenate(second, axis=0)
        first = (first, swapped(first, "zl"))
        second = (second, swapped(second, "y"))
    else:
        first = second = jnp.zeros((), bf16)

    bias_one = lax.dynamic_index_in_dim(
        biases[:C1].reshape(C1 // 8, 8), member, axis=1, keepdims=False
    )
    bias_two = biases[C1 : 2 * C1]
    bias_up = lax.dynamic_slice_in_dim(biases[2 * C1 : 2 * C1 + C0], core * (C0 // 2), C0 // 2)
    bias_three = lax.dynamic_slice_in_dim(
        biases[2 * C1 + C0 : 2 * C1 + 2 * C0], core * (C0 // 2), C0 // 2
    )
    bias_head = biases[2 * C1 + 2 * C0 :]
    head_low = lax.dynamic_slice_in_dim(
        head_weight.astype(bf16), core * (C0 // 2), C0 // 2, axis=0
    )

    pre_one = convolve(feat, kernel_one) + bias_one
    high, wide = pre_one.shape[1], pre_one.shape[2]
    row_at = jnp.arange(high)
    col_at = jnp.arange(wide)
    row_in = ((row_at > 0) | (zh > 0)) & ((row_at < high - 1) | (zh < size_of("zh") - 1))
    col_in = ((col_at > 0) | (x > 0)) & ((col_at < wide - 1) | (x < size_of("x") - 1))
    inside = (row_in[:, None] & col_in[None, :])[None, :, :, None]
    act_one = jnp.where(inside, jax.nn.gelu(pre_one), 0.0).astype(bf16)
    part_two = convolve(act_one, kernel_two)
    feat_shifts, act_shifts = by_shift(feat[:, 1:-1, 1:-1]), by_shift(act_one)
    skip, skip_sides = halo(skip_cells)
    part_two, first, second, skip, skip_sides, marks = lax.optimization_barrier(
        (part_two, first, second, skip, skip_sides, marks)
    )
    if zhs == 2:
        kernel_merge, kernel_up = in_place(me, first + second, merge_pieces, up_pieces)
    else:
        low_chip = jnp.where(core == 0, low_chip, low_chip[::-1])
        low_chip = lax.all_gather(low_chip, CHIPS, axis=0, tiled=True)
        kernel_merge = low_chip[:, :r3].reshape(-1, HALF)
        kernel_up = low_chip[:, r3:].reshape(-1, HALF)
    pre_two = group_scatter(part_two) + bias_two
    act_two = jax.nn.gelu(pre_two).astype(bf16)
    act_two, kernel_merge, kernel_up = lax.optimization_barrier((act_two, kernel_merge, kernel_up))

    act_own = act_two[:, 0]
    ups, act_chip = up_on_chip(me, act_own, swapped(act_own, "core"), kernel_up, bias_up[None])
    ups, sides = halo(ups)
    head_wide = jnp.pad(head_low, ((0, 0), (0, 128 - CLASSES)))
    pre_three, logits, planes = merge_on_chip(
        me,
        ups,
        swapped(ups, "core"),
        sides,
        swapped(sides, "core"),
        skip,
        skip_sides,
        kernel_merge,
        bias_three[None],
        head_wide,
    )
    logits = (logits + swapped(logits, "core"))[:, :CLASSES] + bias_head
    logits = logits.reshape(2, 2, 2, 64, CLASSES)
    pre_three = pre_three.reshape(2, 2, 2, 64, HALF)
    act_three = jax.nn.gelu(pre_three).astype(bf16)

    scaled = marks[1].astype(f32)
    onehot = (marks[0][..., None] == jnp.arange(CLASSES, dtype=jnp.int32)).astype(f32)
    log_probs = jax.nn.log_softmax(logits, axis=-1)
    loss_part = -0.5 * jnp.sum(scaled * jnp.sum(onehot * log_probs, axis=-1))
    grad_logits = ((jnp.exp(log_probs) - onehot) * (scaled / count_all)[..., None]).astype(bf16)

    head_part = jnp.einsum("iabwc,iabwk->ck", act_three, grad_logits, preferred_element_type=f32)
    grad_act_three = jnp.einsum(
        "iabwk,ck->iabwc", grad_logits, head_low, preferred_element_type=f32
    )
    grad_pre_three = gelu_back(pre_three, grad_act_three).astype(bf16)
    border, border_sides = halo(grad_pre_three)
    own_grad, away_grad = ups_grad_on_chip(me, border, border_sides, kernel_merge)
    grad_upper = (own_grad + swapped(away_grad, "core").astype(f32)).astype(bf16)
    grad_upper = grad_upper.reshape(2, 2, 2, 64, HALF)
    grad_act_two = jnp.einsum(
        "iabwo,abco->iwc",
        grad_upper,
        kernel_up.reshape(2, 2, C1, HALF),
        preferred_element_type=f32,
    )[:, None]
    grad_act_two = pair_scatter(grad_act_two, "core", 2, f32)
    grad_pre_two = gelu_back(pre_two, grad_act_two).astype(bf16)

    grad_two = group_gather(grad_pre_two)
    if zhs == 2:
        planes = lax.optimization_barrier((planes, grad_pre_two))[0]
        chip_parts = merge_grads(me, planes, grad_pre_three.reshape(512, HALF), r3, ru)
        grad_two, chip_parts = lax.optimization_barrier((grad_two, chip_parts))
        grad_two, inner, sides = second_back_on_chip(grad_two, kernel_two.reshape(-1, C1))
        grad_two, inner, sides, act_chip = lax.optimization_barrier(
            (grad_two, inner, sides, act_chip)
        )
        chip_parts = up_grads(me, act_chip, grad_upper, chip_parts, r3, ru)
        chip_parts, act_shifts = lax.optimization_barrier((chip_parts, act_shifts))
        second_grad = second_grad_on_chip(me, act_shifts, grad_two, r2, 16 * zhs)
        row = jnp.where(zh == 0, inner[:, 5:], inner[:, :1])
        column = jnp.where(x == 0, sides[1], sides[0])
        corner = jnp.where(zh == 0, column[:, 5:], column[:, :1])[:, :, None]
        column = swapped(column[:, 1:5, None], "x")
        corner = lax.ppermute(corner, ("zh", "x"), [(i, 3 - i) for i in range(4)])
        row = swapped(row, "zh")
        row, column, corner, chip_parts = lax.optimization_barrier(
            (row, column, corner, chip_parts)
        )
        at_row = jnp.arange(4)[None, :, None, None] == jnp.where(zh == 0, 3, 0)
        at_column = jnp.arange(64)[None, None, :, None] == jnp.where(x == 0, 63, 0)
        core_part = (
            inner[:, 1:5]
            + jnp.where(at_row, row, 0.0)
            + jnp.where(at_column, column, 0.0)
            + jnp.where(at_row & at_column, corner, 0.0)
        )
    else:
        cells = planes.reshape(2, 4, 4, 64, 2 * C0)
        chip_parts = (
            jnp.concatenate(
                [
                    jnp.einsum(
                        "iabwc,iabwo->co",
                        cells[:, high : high + 2, wide : wide + 2],
                        grad_pre_three,
                        preferred_element_type=f32,
                    )
                    for high in range(3)
                    for wide in range(3)
                ]
            ).astype(bf16),
            jnp.einsum(
                "iwc,iabwo->abco", act_chip, grad_upper, preferred_element_type=f32
            ).astype(bf16),
        )
        images, width = grad_two.shape[1], grad_two.shape[3]
        grad_two = grad_two.reshape(4, 2, images, width, C1).transpose(2, 0, 1, 3, 4)
        grad_two = grad_two.reshape(images, 4, 2 * width, C1)
        second_grad = kernel_grad(act_one, grad_two)
        spill = convolve(grad_two, turned(kernel_two), 2)
        inner = spill[:, 1:-1]
        inner = inner.at[:, :1].add(shifted(spill[:, -1:], "zh", 1))
        inner = inner.at[:, -1:].add(shifted(spill[:, :1], "zh", -1))
        core_part = inner[:, :, 1:-1]
        core_part = core_part.at[:, :, :1].add(shifted(inner[:, :, -1:], "x", 1))
        core_part = core_part.at[:, :, -1:].add(shifted(inner[:, :, :1], "x", -1))
    grad_pre_one = gelu_back(pre_one[:, 1:-1, 1:-1], core_part).astype(bf16)
    tiled = zhs == 2
    if tiled:
        grad_pre_one, second_grad = lax.optimization_barrier((grad_pre_one, second_grad))
        first_grad = first_grad_on_chip(me, feat_shifts, grad_pre_one, r1, 16 * zhs)
        def shard_sum(own, got):
            return (own.astype(f32) + got.astype(f32)).reshape(2, 8, -1, 128)

        def leave(part):
            away = lax.dynamic_index_in_dim(part, 1 - zh, axis=0, keepdims=False).astype(bf16)
            own = lax.dynamic_index_in_dim(part, zh, axis=0, keepdims=False)
            return own, away, swapped(away, "zh")

        chip_parts = sent(chip_parts, "zl", "y")
        chip_parts = sent(added(chip_parts), "y", "zl")
        second_stays = after(chip_parts[0], second_grad[0])[1]
        two_own, two_away, two_got = leave(shard_sum(second_stays, swapped(second_grad[1], "x")))
        two_away, first_stays = after(two_away, first_grad[0])
        one_own, one_away, one_got = leave(shard_sum(first_stays, swapped(first_grad[1], "x")))
        one_away, chip_parts = after(one_away, chip_parts)
        a_stays, a_goes = halves_of(*chip_parts[:2])
        a_got = swapped(a_goes, "x")
        a_goes, b_own = after(a_goes, chip_parts[2])
        b_stays, b_goes = halves_of(b_own, chip_parts[3])
        b_got = swapped(b_goes, "x")
        b_goes, a_stays = after(b_goes, a_stays)
        a_part = a_stays.astype(f32) + a_got.astype(f32)
        a_goes = a_part[2:].astype(bf16)
        a_last = swapped(a_goes, "zh")
        a_goes, two_own = after(a_goes, two_own)
        part_two = two_own + two_got.astype(f32)
        two_low, b_stays = after(part_two.astype(bf16), b_stays)
        b_part = b_stays.astype(f32) + b_got.astype(f32)
        b_goes = b_part[2:].astype(bf16)
        b_last = swapped(b_goes, "zh")
        a_last, b_goes, one_own = lax.optimization_barrier((a_last, b_goes, one_own))
        part_one = one_own + one_got.astype(f32)
        one_low = part_one.astype(bf16)
        part_chip = jnp.concatenate(
            [a_part[:2] + a_last.astype(f32), b_part[:2] + b_last.astype(f32)], axis=1
        )
        sq_kernels = jnp.sum(part_one * part_one) + jnp.sum(part_two * part_two)
        part = jnp.concatenate([one_low, two_low], axis=1)
        part = lax.all_to_all(part, MEMBERS, 0, 0, tiled=True)
        part_one, part_two = part[:, :r1], part[:, r1:]
        half = r3 // 2
        part_chip = jnp.concatenate(
            [
                part_chip[:, :half],
                part_chip[:, half + ru // 2 : r3 + ru // 2],
                part_chip[:, half : half + ru // 2],
                part_chip[:, r3 + ru // 2 :],
            ],
            axis=1,
        )
        part_two = part_two.reshape(8, r2 // 8, C1 // 128, 128).transpose(1, 0, 2, 3)
        share_two = part_two.reshape(-1).astype(f32)
    else:
        first_grad = kernel_grad(feat[:, 1:-1, 1:-1], grad_pre_one)
        mine = jnp.arange(8)[None, :, None] == member
        part_two = jnp.where(mine, second_grad.astype(bf16)[:, None], 0)
        share_two = lax.psum_scatter(
            part_two.reshape(-1, C1), AXES, scatter_dimension=0, tiled=True
        ).reshape(-1).astype(f32)
        part_one = far_scatter(first_grad)
        sq_kernels = jnp.sum(share_two * share_two) + jnp.sum(part_one * part_one)
        part_one = lax.all_to_all(part_one.astype(bf16), MEMBERS, 0, 0, tiled=True)
        part_chip = jnp.concatenate(
            [last_sum(chip_parts[0]), last_sum(chip_parts[1])], axis=1
        )
    share_one = jnp.einsum("qrm,cqm->rc", part_one, sorting, preferred_element_type=f32).reshape(-1)
    sq_chip = jnp.sum(part_chip * part_chip)
    part_chip = part_chip.astype(bf16)
    part_chip = in_order(part_chip[0], swapped(part_chip[1], "core"), "core", 1).astype(f32)
    share_merge = part_chip[:r3].reshape(-1)
    share_up = part_chip[r3:].reshape(-1)
    share_sq = sq_kernels + sq_chip
    spread_one = (
        jnp.where(jnp.arange(8)[None, :] == member, column_sum(grad_pre_one)[:, None], 0.0)
    ).reshape(-1)

    def half_of(values):
        shape = (2 * values.shape[0],) + values.shape[1:]
        return lax.dynamic_update_slice_in_dim(
            jnp.zeros(shape, f32), values, core * values.shape[0], axis=0
        )

    packed = jnp.concatenate(
        [
            spread_one,
            column_sum(grad_pre_two),
            half_of(column_sum(grad_upper)),
            half_of(column_sum(grad_pre_three)),
            0.5 * column_sum(grad_logits),
            half_of(head_part).reshape(-1),
            share_sq[None],
            loss_part[None],
        ]
    )
    packed = total(packed, ("core", "x", "y"))
    packed, share_one, share_two = lax.optimization_barrier((packed, share_one, share_two))
    packed = total(packed, ("zl", "zh"))
    bias_total = packed[: biases.shape[0]]
    head_total = packed[biases.shape[0] : -2].reshape(head_weight.shape)
    sq_total, loss_total = packed[-2], packed[-1]
    grad_norm = jnp.sqrt(sq_total + jnp.sum(jnp.square(packed[:-2])))
    factor = clip_norm / jnp.maximum(grad_norm, clip_norm)
    outs = ()
    for weight, moment, second, grad, decay in (
        (conv_first, conv_first_mom, conv_first_sec, share_one, weight_decay),
        (conv_second, conv_second_mom, conv_second_sec, share_two, weight_decay),
        (up_conv, up_conv_mom, up_conv_sec, share_up, weight_decay),
        (conv_merge, conv_merge_mom, conv_merge_sec, share_merge, weight_decay),
        (head_weight, head_mom, head_sec, head_total, weight_decay),
        (biases, biases_mom, biases_sec, bias_total, 0.0),
    ):
        outs += adamw(weight, moment, second, grad * factor, decay)
    return outs + (loss_total, count_all, grad_norm)


def solution(mesh):
    rows, cols = mesh.shape["rows"], mesh.shape["cols"]
    split = Mesh(mesh.devices.reshape(rows // 4, 2, 2, cols // 2, 2), AXES)
    image = P(None, ROWS, ("x", "core"))
    flat = P(AXES)
    return jax.shard_map(
        shards,
        mesh=split,
        in_specs=(image,) * 5 + (flat,) * 12 + (P(),) * 6,
        out_specs=(flat,) * 12 + (P(),) * 9,
        check_vma=False,
    )
```
